32 devices in a mesh: wall: 8 (over y, x, core), surf: 4 (over z).
Axes of the slice: x: 2, y: 2, z: 4, core: 2. Of those that a mesh axis runs over, the one named last changes fastest.
Arguments:
- state: bfloat16 [512, 162], P(('wall', 'surf')), may hold values from -6 to 6
- source: bfloat16 [512, 162], P(('wall', 'surf')), may hold values from -6 to 6
- face_coef: float32 [512, 4], P(('wall', 'surf')), may hold values from 0.1 to 0.5
- neighbour: int32 [512, 4], P(('wall', 'surf')), may hold values from 0 to 47
- lift: bfloat16 [162, 162], replicated, may hold values from -0.5 to 0.5
- elem_slot: int32 [16, 32], P('wall', 'surf'), may hold values from 0 to 15, as said below
- line_len: int32 [32], P('surf'), may hold values from 8 to 16
- dinv: bfloat16 [16, 32, 162, 162], P('wall', 'surf'), may hold values from -0.3 to 1.2
- lower: bfloat16 [16, 32, 162, 162], P('wall', 'surf'), may hold values from -1.4 to 0.4
- upper: bfloat16 [16, 32, 162, 162], P('wall', 'surf'), may hold values from -0.4 to 1.4
Outputs:
- solution: float32 [16, 32, 162], P('wall', 'surf')
The draws below stay inside these ranges and needn't reach their ends.
Inputs may be any that keep to these rules, and one draw needn't show every extreme that they name: `elem_slot`: on each device the entries form a permutation of its 16 slots.
All inputs are finite; a program needn't handle non-finite values.
Results may differ from the reference program's by a relative error of at most 0.0023.
Values may be sent and summed in bfloat16 or wider, within the bound.
No kernel may reach another device: no remote copies, remote signals or barrier semaphores. Data moves between devices by JAX's collectives and lax.ppermute only.
A program may use at most 128 MiB of HBM per device.

```python
import math
import jax
import jax.numpy as jnp
from jax import lax

B = 162
F = 4
E_DEV = 2
LINES = 8
SLOTS = 16
CELLS_PER_STRAND = 16
STRAND_COUNT = 32
ROWS = 512
N_SURF = 4


def draw_neighbour(key, part):
    key_a = jax.random.fold_in(key, 11)
    key_b = jax.random.fold_in(key, 12)
    pick = jax.random.randint(key_a, (ROWS, F), 0, 4)
    side = pick - (pick >= 2).astype(jnp.int32)
    slot_there = jax.random.randint(key_b, (ROWS, F), 0, SLOTS)
    values = (side * SLOTS + slot_there).astype(jnp.int32)
    values = values.at[0, 0].set(3 * SLOTS - 1)
    values = values.at[1, 0].set(0)
    return values


def draw_elem_slot(key, part):
    count = CELLS_PER_STRAND // E_DEV * (STRAND_COUNT // LINES)
    keys = jax.random.split(jax.random.fold_in(key, 21), count)
    perms = jax.vmap(lambda single: jax.random.permutation(single, SLOTS))(keys)
    perms = perms.reshape(CELLS_PER_STRAND // E_DEV, STRAND_COUNT // LINES, E_DEV, LINES)
    perms = jnp.transpose(perms, (0, 2, 1, 3)).reshape(CELLS_PER_STRAND, STRAND_COUNT)
    return perms.astype(jnp.int32)


def draw_line_len(key, part):
    values = jax.random.randint(jax.random.fold_in(key, 31), (STRAND_COUNT,), CELLS_PER_STRAND // 2, CELLS_PER_STRAND + 1)
    return values.at[0].set(CELLS_PER_STRAND).astype(jnp.int32)


def draw_dinv(key, part):
    key_d = jax.random.fold_in(key, 41)
    key_n = jax.random.fold_in(key, 42)
    shape = (CELLS_PER_STRAND, STRAND_COUNT, B, B)
    central_submatrix = jax.random.uniform(key_d, (CELLS_PER_STRAND, STRAND_COUNT, B), jnp.float32, 0.88, 0.92)
    noise = jnp.clip(jax.random.normal(key_n, shape, jnp.float32), -4.0, 4.0)
    values = central_submatrix[..., None] * jnp.eye(B, dtype=jnp.float32) + noise * (0.2 / B ** 0.5)
    return values.astype(jnp.bfloat16)


def coupling(base, noise, slow_share, sign):
    key_s = jax.random.fold_in(base, 1)
    key_f = jax.random.fold_in(base, 2)
    key_p = jax.random.fold_in(base, 3)
    key_c = jax.random.fold_in(base, 4)
    slow = jax.random.uniform(key_s, (STRAND_COUNT, B), jnp.float32) < slow_share
    fast = jax.random.uniform(key_f, (CELLS_PER_STRAND, STRAND_COUNT, B), jnp.float32, 0.3, 0.75)
    relaxation_factor = jnp.where(slow[None, :, :], 0.97, fast)
    cell_locations = jax.random.randint(key_p, (3, STRAND_COUNT), 0, CELLS_PER_STRAND)
    split_positions = jax.random.uniform(key_c, (3, STRAND_COUNT), jnp.float32, 0.5, 0.8)
    location_array = jnp.arange(CELLS_PER_STRAND, dtype=jnp.int32)[:, None]
    segment_span = jnp.ones((CELLS_PER_STRAND, STRAND_COUNT), jnp.float32)
    for chosen_entry in range(3):
        segment_span = segment_span * jnp.where(location_array == cell_locations[chosen_entry][None, :], split_positions[chosen_entry][None, :], 1.0)
    central_submatrix = relaxation_factor * segment_span[:, :, None] / 0.9
    values = central_submatrix[..., None] * jnp.eye(B, dtype=jnp.float32) + noise * (0.25 / B ** 0.5)
    return (sign * values).astype(jnp.bfloat16)


def draw_lower(key, part):
    base = jax.random.fold_in(key, 51)
    key_n = jax.random.fold_in(base, 9)
    shape = (CELLS_PER_STRAND, STRAND_COUNT, B, B)
    noise = jnp.clip(jax.random.normal(key_n, shape, jnp.float32), -4.0, 4.0)
    share = 0.5
    return coupling(base, noise, share, -1.0)


def draw_upper(key, part):
    base = jax.random.fold_in(key, 61)
    key_n = jax.random.fold_in(base, 9)
    shape = (CELLS_PER_STRAND, STRAND_COUNT, B, B)
    noise = jnp.clip(jax.random.normal(key_n, shape, jnp.float32), -4.0, 4.0)
    share = 0.5
    return coupling(base, noise, share, 1.0)


def steps_of(rng, extent, cuts, low, largest):
    factor_of, own = 1.0, jax.random.fold_in(rng, 6)
    for dim, shards_of in cuts:
        heights = jnp.exp(jax.random.uniform(jax.random.fold_in(own, dim), (shards_of,), jnp.float32, low / len(cuts), largest / len(cuts)))
        factor_of = factor_of * jnp.repeat(heights, extent[dim] // shards_of).reshape([-1 if axis == dim else 1 for axis in range(len(extent))])
    return factor_of


def normal_values(key, dims, spread, most, pieces=(), kind=jnp.bfloat16):
    values = spread * jax.random.normal(key, dims, jnp.float32)
    if pieces:
        values = values * steps_of(key, dims, pieces, -0.22, 0.18)
    return jnp.clip(values, -most, most).astype(kind)


def setup_inputs(seed: int = 0) -> dict:
    streams_of = jax.random.split(jax.random.key(seed), 11)
    return {
        "state": normal_values(streams_of[0], (ROWS, B), 1.0, 6.0, ((0, 32),)),
        "source": normal_values(streams_of[1], (ROWS, B), 1.0, 6.0, ((0, 32),)),
        "face_coef": jnp.clip(jnp.exp(math.log(0.5) - 1.609438 * jax.random.uniform(streams_of[2], (ROWS, F), jnp.float32) ** steps_of(streams_of[2], (ROWS, F), ((0, 32),), -0.2, 0.2)), 0.1, 0.5),
        "neighbour": draw_neighbour(jax.random.fold_in(streams_of[10], 71), 0),
        "lift": normal_values(streams_of[4], (B, B), B ** -0.5, 0.5),
        "elem_slot": draw_elem_slot(jax.random.fold_in(streams_of[10], 71), 0),
        "line_len": draw_line_len(jax.random.fold_in(streams_of[10], 71), 0),
        "dinv": draw_dinv(jax.random.fold_in(streams_of[10], 71), 0),
        "lower": draw_lower(jax.random.fold_in(streams_of[10], 71), 0),
        "upper": draw_upper(jax.random.fold_in(streams_of[10], 71), 0),
    }


def apply_block(matrix, vector):
    return jnp.einsum("lij,lj->li", matrix.astype(jnp.float32), vector, precision=lax.Precision.HIGHEST)


def reference(state, source, face_coef, neighbour, lift, elem_slot, line_len, dinv, lower, upper):
    rows = jnp.arange(ROWS, dtype=jnp.int32)
    device = rows // SLOTS
    wall_pos = device // N_SURF
    surf_pos = device % N_SURF
    offset = neighbour // SLOTS - 1
    slot_there = neighbour % SLOTS
    nbrow = ((wall_pos[:, None] * N_SURF + (surf_pos[:, None] + offset) % N_SURF) * SLOTS + slot_there).astype(jnp.int32)
    nb_vals = state[nbrow].astype(jnp.float32)
    face_sum = jnp.sum(face_coef[:, :, None] * (state.astype(jnp.float32)[:, None, :] - nb_vals), axis=1).astype(jnp.bfloat16)
    residual = source.astype(jnp.float32) - jnp.dot(face_sum, lift, preferred_element_type=jnp.float32)
    gpos = jnp.arange(CELLS_PER_STRAND, dtype=jnp.int32)[:, None]
    lpos = jnp.arange(STRAND_COUNT, dtype=jnp.int32)[None, :]
    row_of = (((gpos // E_DEV) * N_SURF + lpos // LINES) * SLOTS + elem_slot).astype(jnp.int32)
    line_rhs = residual[row_of]
    active = (gpos < line_len[None, :]).astype(jnp.float32)

    def forward(carried, items):
        dblock, lblock, rhs_now, act_now = items
        value = act_now[:, None] * apply_block(dblock, rhs_now - apply_block(lblock, carried))
        return value, value

    start = jnp.zeros((STRAND_COUNT, B), jnp.float32)
    _, y_vals = lax.scan(forward, start, (dinv, lower, line_rhs, active))

    def backward(carried, items):
        dblock, ublock, y_now, act_now = items
        value = act_now[:, None] * (y_now - apply_block(dblock, apply_block(ublock, carried)))
        return value, value

    _, solution = lax.scan(backward, start, (dinv, upper, y_vals, active), reverse=True)
    return solution
```

```python
import functools

import jax
import jax.numpy as jnp
from jax import lax
from jax.experimental import pallas as pl
from jax.experimental.pallas import tpu as pltpu
from jax.sharding import PartitionSpec as P

F32 = jnp.float32
BF16 = jnp.bfloat16
ROWS = 8
VMEM = pl.BlockSpec(memory_space=pltpu.VMEM)
SMEM = pl.BlockSpec(memory_space=pltpu.SMEM)
ANY = pl.BlockSpec(memory_space=pl.ANY)


def split2(x):
    high = x.astype(BF16)
    return high, (x - high.astype(F32)).astype(BF16)


def stacked(v):
    return jnp.concatenate(split2(v), axis=0)


def product(x, y):
    dot = functools.partial(jnp.dot, preferred_element_type=F32)
    return dot(x[0], y[0]) + (dot(x[0], y[1]) + dot(x[1], y[0]))


def row_index(width):
    return lax.broadcasted_iota(jnp.int32, (ROWS, width), 0)


def apply_pairs(vector, pair_of, lines):
    rows = row_index(vector.shape[1])
    both = stacked(vector)
    total = jnp.zeros(vector.shape, F32)
    for l in range(lines):
        high, low = pair_of(l)
        first = jnp.dot(both, high, preferred_element_type=F32)
        second = jnp.dot(both, low, preferred_element_type=F32)
        part = first[:ROWS] + first[ROWS:] + second[:ROWS]
        total = jnp.where(rows == l, part, total)
    return total


def apply_rows(vector, matrix_of, lines):
    rows = row_index(vector.shape[1])
    both = stacked(vector)
    total = jnp.zeros(vector.shape, F32)
    for l in range(lines):
        first = lax.dot_general(
            both, matrix_of(l), (((1,), (1,)), ((), ())), preferred_element_type=F32
        )
        total = jnp.where(rows == l, first[:ROWS] + first[ROWS:], total)
    return total


def core_of():
    return lax.rem(lax.axis_index("wall"), 2)


def chip_of():
    return lax.div(lax.axis_index("wall"), 2)


def relayout_kernel(dinv_ref, lower_ref, upper_ref, own_ref, send_ref, scratch):
    half = own_ref.shape[2]
    core = core_of()
    for a, ref in enumerate((dinv_ref, lower_ref, upper_ref)):
        for e in range(own_ref.shape[1]):
            slot = (a * own_ref.shape[1] + e) % 2
            scratch[slot] = ref[e].astype(F32)
            for l in range(half):
                own_ref[a, e, l] = scratch[slot, :, core * half + l, :].astype(BF16)
                send_ref[a, e, l] = scratch[slot, :, (1 - core) * half + l, :].astype(BF16)


def pair_kernel(*refs, first):
    if first:
        raw_ref, q_ref, s_ref, a_ref, c_ref = refs
    else:
        raw_ref, _, _, a_own, c_own, q_ref, s_ref, a_ref, c_ref = refs
    core = core_of()
    place = core if first else 1 - core
    count, lines = raw_ref.shape[1], raw_ref.shape[2]
    for l in range(lines):
        qs, ss = [], []
        for e in range(count):
            for held, ref, source in ((qs, q_ref, 1), (ss, s_ref, 2)):
                block = lax.dot_general(
                    raw_ref[source, e, l],
                    raw_ref[0, e, l],
                    (((0,), (1,)), ((), ())),
                    preferred_element_type=F32,
                )
                pair = split2(block)
                held.append(pair)
                ref[place, e, l, 0] = pair[0]
                ref[place, e, l, 1] = pair[1]
        forward = qs[0]
        for e in range(1, count):
            forward = split2(product(forward, qs[e]))
        backward = ss[count - 1]
        for e in range(count - 2, -1, -1):
            backward = split2(product(backward, ss[e]))
        if not first:
            own = (a_own[l, 0], a_own[l, 1])
            early = [jnp.where(core == 0, x, y) for x, y in zip(own, forward)]
            late = [jnp.where(core == 0, y, x) for x, y in zip(own, forward)]
            forward = split2(product(early, late))
            own = (c_own[l, 0], c_own[l, 1])
            early = [jnp.where(core == 0, x, y) for x, y in zip(own, backward)]
            late = [jnp.where(core == 0, y, x) for x, y in zip(own, backward)]
            backward = split2(product(late, early))
        a_ref[l, 0], a_ref[l, 1] = forward
        c_ref[l, 0], c_ref[l, 1] = backward


def prepare_kernel(
    slot_ref, len_ref, coef_ref, nb_ref, source_ref, weight_ref, rhs_ref, act_ref, *, block
):
    faces, slots = coef_ref.shape
    depth, line_count = slot_ref.shape
    half = line_count // 2
    blocks = half // block
    core, chip = core_of(), chip_of()
    cells = 3 * slots
    k = lax.broadcasted_iota(jnp.int32, (cells, slots), 0)
    e = lax.broadcasted_iota(jnp.int32, (cells, slots), 1)
    weight = jnp.zeros((cells, slots), F32)
    own = jnp.zeros((1, slots), F32)
    for f in range(faces):
        coef = coef_ref[f : f + 1, :]
        own = own + coef
        weight = weight - jnp.where(k == nb_ref[f : f + 1, :], coef, 0.0)
    weight = weight + jnp.where(k == e + slots, own, 0.0)
    count = 2 * depth * blocks * ROWS
    rows = lax.broadcasted_iota(jnp.int32, (count, slots), 0)
    slot = jnp.full((count, slots), -1, jnp.int32)
    for h in range(2):
        first_line = lax.rem(core + h, 2) * half
        for g in range(depth):
            for b in range(blocks):
                for r in range(block):
                    row = ((h * depth + g) * blocks + b) * ROWS + r
                    here = slot_ref[g, first_line + b * block + r]
                    slot = jnp.where(rows == row, here, slot)
    chosen = (slot == lax.broadcasted_iota(jnp.int32, (count, slots), 1)).astype(F32).astype(BF16)
    high, rest = split2(weight)
    rest = weight - high.astype(F32)
    mid, low = split2(rest)
    for i, part in enumerate((high, mid, low)):
        weight_ref[i * count : (i + 1) * count, :] = lax.dot_general(
            chosen, part, (((1,), (1,)), ((), ())), preferred_element_type=F32
        ).astype(BF16)
    rhs_ref[...] = jnp.dot(chosen, source_ref[...], preferred_element_type=F32)
    width = act_ref.shape[2]
    rows = lax.broadcasted_iota(jnp.int32, (blocks * ROWS, width), 0)
    length = jnp.zeros((blocks * ROWS, width), jnp.int32)
    for b in range(blocks):
        for r in range(block):
            here = len_ref[core * half + b * block + r]
            length = jnp.where(rows == b * ROWS + r, here, length)
    for g in range(2 * depth):
        act_ref[g] = (chip * (2 * depth) + g < length).astype(F32)


def residual_kernel(before, state, after, weight, source, lift, own_ref, send_ref):
    cells = jnp.concatenate([before[...], state[...], after[...]], axis=0)
    parts = jnp.dot(weight[...], cells, preferred_element_type=F32)
    count = source.shape[0]
    face_sum = parts[:count] + (parts[count : 2 * count] + parts[2 * count :])
    flux = jnp.dot(face_sum.astype(BF16), lift[...], preferred_element_type=F32)
    rhs = source[...] - flux
    depth, rows, _ = own_ref.shape
    for g in range(depth):
        own_ref[g] = rhs[g * rows : (g + 1) * rows]
        send_ref[g] = rhs[(depth + g) * rows : (depth + g + 1) * rows]


def scaled_kernel(rhs_ref, raw_ref, out_ref):
    for e in range(rhs_ref.shape[0]):
        out_ref[e] = apply_rows(rhs_ref[e], lambda l: raw_ref[0, e, l], raw_ref.shape[2])


def forward_local(scaled, q_ref, act_ref, carried):
    depth, lines = q_ref.shape[1], q_ref.shape[2]
    values = []
    for g in range(2 * depth):
        value = scaled[g]
        if carried is not None:
            value = value - apply_pairs(
                carried, lambda l: (q_ref[g // depth, g % depth, l, 0], q_ref[g // depth, g % depth, l, 1]), lines
            )
        carried = act_ref[g] * value
        values.append(carried)
    return values


def backward_local(values, s_ref, act_ref, carried):
    depth, lines = s_ref.shape[1], s_ref.shape[2]
    solved = [None] * len(values)
    for g in range(2 * depth - 1, -1, -1):
        value = values[g]
        if carried is not None:
            value = value - apply_pairs(
                carried, lambda l: (s_ref[g // depth, g % depth, l, 0], s_ref[g // depth, g % depth, l, 1]), lines
            )
        carried = act_ref[g] * value
        solved[g] = carried
    return solved


def first_kernel(own_ref, rhs_ref, raw_ref, q_ref, act_ref, scaled_ref, b_ref):
    depth = own_ref.shape[0]
    core = core_of()
    own = [own_ref[e] for e in range(depth)]
    other = [
        apply_rows(rhs_ref[e], lambda l: raw_ref[0, e, l], raw_ref.shape[2]) for e in range(depth)
    ]
    scaled = [jnp.where(core == 0, x, y) for x, y in zip(own, other)]
    scaled += [jnp.where(core == 0, y, x) for x, y in zip(own, other)]
    for g in range(2 * depth):
        scaled_ref[g] = scaled[g]
    b_ref[...] = forward_local(scaled, q_ref, act_ref, None)[-1]


def hop_kernel(came_ref, pair_ref, act_ref, local_ref, out_ref, *, chip):
    out_ref[...] = local_ref[...]

    @pl.when(chip_of() == chip)
    def _():
        gone = apply_pairs(
            came_ref[...], lambda l: (pair_ref[l, 0], pair_ref[l, 1]), pair_ref.shape[0]
        )
        out_ref[...] = act_ref[act_ref.shape[0] - 1] * gone + local_ref[...]


def chosen_arrival(refs, chips):
    here = chip_of()
    value = jnp.zeros(refs[0].shape, F32)
    for ref, chip in zip(refs, chips):
        value = jnp.where(here == chip, ref[...], value)
    return value


def turn_kernel(scaled_ref, q_ref, s_ref, act_ref, *refs, chips):
    came, y_ref, d_ref = refs[:-2], refs[-2], refs[-1]
    count = scaled_ref.shape[0]
    carried = chosen_arrival(came, chips)
    values = forward_local([scaled_ref[g] for g in range(count)], q_ref, act_ref, carried)
    for g in range(count):
        y_ref[g] = values[g]
    d_ref[...] = backward_local(values, s_ref, act_ref, None)[0]


def last_kernel(y_ref, s_ref, act_ref, *refs, chips):
    came, own_ref, send_ref = refs[:-2], refs[-2], refs[-1]
    count = y_ref.shape[0]
    depth = count // 2
    core = core_of()
    carried = chosen_arrival(came, chips)
    solved = backward_local([y_ref[g] for g in range(count)], s_ref, act_ref, carried)
    for e in range(depth):
        own_ref[e] = jnp.where(core == 0, solved[e], solved[depth + e])
        send_ref[e] = jnp.where(core == 0, solved[depth + e], solved[e])


def merge_kernel(own_ref, other_ref, out_ref, *, block):
    core = core_of()
    blocks = own_ref.shape[1] // ROWS
    for e in range(out_ref.shape[0]):
        own = [own_ref[e, b * ROWS : b * ROWS + block] for b in range(blocks)]
        other = [other_ref[e, b * ROWS : b * ROWS + block] for b in range(blocks)]
        out_ref[e] = jnp.where(
            core == 0,
            jnp.concatenate(own + other, axis=0),
            jnp.concatenate(other + own, axis=0),
        )


def padded_bytes(shape, dtype):
    size = jnp.dtype(dtype).itemsize
    shape = (1,) * (2 - len(shape)) + tuple(shape)
    rows = -(-shape[-2] // 16) * 16
    columns = -(-shape[-1] // 128) * 128
    total = rows * columns * size
    for extent in shape[:-2]:
        total *= extent
    return total


def run(kernel, operands, outs, blocks=1, scratch=(), aliases=None):
    everything = [(x.shape, x.dtype) for x, _ in operands] + [(s, t) for s, t, _ in outs]
    everything += [(s.shape, s.dtype) for s in scratch]
    limit = sum(padded_bytes(s, t) for s, t in everything)
    if blocks == 1:
        in_specs = [at if isinstance(at, pl.BlockSpec) else VMEM for _, at in operands]
        out_specs = [VMEM for _ in outs]
        grid = ()
    else:

        def spec(shape, at):
            if isinstance(at, pl.BlockSpec):
                return at
            if at is None:
                return pl.BlockSpec(shape, lambda i: (0,) * len(shape))
            size = tuple(n // blocks if axis == at else n for axis, n in enumerate(shape))
            return pl.BlockSpec(size, lambda i: tuple(i if axis == at else 0 for axis in range(len(shape))))

        in_specs = [spec(x.shape, at) for x, at in operands]
        out_specs = [spec(s, at) for s, _, at in outs]
        grid = (blocks,)
        limit = 2 * limit // blocks
    limit = min(limit + limit // 4 + (4 << 20), 60 << 20)
    return pl.pallas_call(
        kernel,
        grid=grid,
        in_specs=in_specs,
        out_specs=out_specs,
        out_shape=[jax.ShapeDtypeStruct(s, t) for s, t, _ in outs],
        scratch_shapes=list(scratch),
        input_output_aliases=aliases or {},
        compiler_params=pltpu.CompilerParams(vmem_limit_bytes=limit),
    )(*[x for x, _ in operands])


def flips(count):
    return [(i, i ^ 1) for i in range(count)]


def hop_pairs(count, start, end, spare):
    target = {i: i ^ 1 for i in range(count)}
    cycle = [start, end] + ([] if spare is None else [spare])
    for here, there in zip(cycle, cycle[1:] + cycle[:1]):
        for core in range(2):
            target[2 * here + core] = 2 * there + core
    return sorted(target.items())


def spare_chip(chips, start, end):
    behind = 2 * start - end
    if 0 <= behind < chips:
        return behind
    ahead = chips - 1 if end > start else 0
    return ahead if ahead not in (start, end) else None


def per_device(state, source, face_coef, neighbour, lift, elem_slot, line_len, dinv, lower, upper):
    wall_count = lax.axis_size("wall")
    surf_count = lax.axis_size("surf")
    chips = wall_count // 2
    depth, line_count, width, _ = dinv.shape
    half = line_count // 2
    block = max(n for n in range(1, ROWS + 1) if half % n == 0)
    blocks = half // block
    rows = blocks * ROWS
    core = lax.rem(lax.axis_index("wall"), 2)

    before = lax.ppermute(state, "surf", [(i, (i + 1) % surf_count) for i in range(surf_count)])
    after = lax.ppermute(state, "surf", [((i + 1) % surf_count, i) for i in range(surf_count)])

    raw_shape = (3, depth, half, width, width)
    if line_count == ROWS:
        turned = [jnp.transpose(x, (0, 2, 1, 3)) for x in (dinv, lower, upper)]
        own, send = run(
            relayout_kernel,
            [(x, None) for x in turned],
            [(raw_shape, BF16, None)] * 2,
            scratch=[pltpu.VMEM((2, width, line_count, width), F32)],
        )
    else:
        every = jnp.stack([dinv, lower, upper])
        own = lax.dynamic_slice_in_dim(every, core * half, half, axis=2)
        send = lax.dynamic_slice_in_dim(every, (1 - core) * half, half, axis=2)
    came = lax.ppermute(send, "wall", flips(wall_count))

    count = 2 * depth * rows
    weight, line_source, act = run(
        functools.partial(prepare_kernel, block=block),
        [
            (elem_slot, SMEM),
            (line_len, SMEM),
            (face_coef.T, None),
            (neighbour.T, None),
            (source, None),
        ],
        [
            ((3 * count, 3 * state.shape[0]), BF16, None),
            ((count, width), F32, None),
            ((2 * depth, rows, width), F32, None),
        ],
    )

    pairs_shape = (2, depth, half, 2, width, width)
    chip_shape = (half, 2, width, width)
    pair_outs = [(pairs_shape, BF16, 2), (pairs_shape, BF16, 2), (chip_shape, BF16, 0), (chip_shape, BF16, 0)]
    q_half, s_half, a_own, c_own = run(
        functools.partial(pair_kernel, first=True), [(own, 2)], pair_outs, blocks
    )
    own_rhs, send_rhs = run(
        residual_kernel,
        [(before, None), (state, None), (after, None), (weight, None), (line_source, None), (lift, None)],
        [((depth, rows, width), F32, None)] * 2,
    )
    came_rhs = lax.ppermute(send_rhs, "wall", flips(wall_count))
    (own_scaled,) = run(
        scaled_kernel, [(own_rhs, 1), (own, 2)], [((depth, rows, width), F32, 1)], blocks
    )
    q, s, a, c = run(
        functools.partial(pair_kernel, first=False),
        [(came, 2), (q_half, ANY), (s_half, ANY), (a_own, 0), (c_own, 0)],
        pair_outs,
        blocks,
        aliases={1: 0, 2: 1},
    )
    scaled, local = run(
        first_kernel,
        [(own_scaled, 1), (came_rhs, 1), (came, 2), (q, 2), (act, 1)],
        [((2 * depth, rows, width), F32, 1), ((rows, width), F32, 0)],
        blocks,
    )

    def hop(came, pair, local, chip):
        (out,) = run(
            functools.partial(hop_kernel, chip=chip),
            [(came, 0), (pair, 0), (act, 1), (local, 0)],
            [((rows, width), F32, 0)],
            blocks,
        )
        return out

    arrivals = []
    for chip in range(chips - 1):
        out = local if chip == 0 else hop(arrivals[-1], a, local, chip)
        pairs = hop_pairs(wall_count, chip, chip + 1, spare_chip(chips, chip, chip + 1))
        arrivals.append(lax.ppermute(out, "wall", pairs))
    y, back = run(
        functools.partial(turn_kernel, chips=list(range(1, chips))),
        [(scaled, 1), (q, 2), (s, 2), (act, 1)] + [(x, 0) for x in arrivals],
        [((2 * depth, rows, width), F32, 1), ((rows, width), F32, 0)],
        blocks,
    )
    arrivals = []
    for chip in range(chips - 1, 0, -1):
        out = back if chip == chips - 1 else hop(arrivals[-1], c, back, chip)
        pairs = hop_pairs(wall_count, chip, chip - 1, spare_chip(chips, chip, chip - 1))
        arrivals.append(lax.ppermute(out, "wall", pairs))
    own_part, send_part = run(
        functools.partial(last_kernel, chips=list(range(chips - 2, -1, -1))),
        [(y, 1), (s, 2), (act, 1)] + [(x, 0) for x in arrivals],
        [((depth, rows, width), F32, 1)] * 2,
        blocks,
    )
    other_part = lax.ppermute(send_part, "wall", flips(wall_count))
    (solution,) = run(
        functools.partial(merge_kernel, block=block),
        [(own_part, None), (other_part, None)],
        [((depth, line_count, width), F32, None)],
    )
    return solution


def solution(mesh):
    in_specs = (
        P(("wall", "surf"), None),
        P(("wall", "surf"), None),
        P(("wall", "surf"), None),
        P(("wall", "surf"), None),
        P(),
        P("wall", "surf"),
        P("surf"),
        P("wall", "surf", None, None),
        P("wall", "surf", None, None),
        P("wall", "surf", None, None),
    )
    out_specs = P("wall", "surf", None)
    return jax.shard_map(
        per_device, mesh=mesh, in_specs=in_specs, out_specs=out_specs, check_vma=False
    )
```

```python
import functools

import jax
import jax.numpy as jnp
from jax import lax
from jax.experimental import pallas as pl
from jax.experimental.pallas import tpu as pltpu
from jax.sharding import PartitionSpec as P

F32 = jnp.float32
BF16 = jnp.bfloat16
ROWS = 8
VMEM = pl.BlockSpec(memory_space=pltpu.VMEM)
SMEM = pl.BlockSpec(memory_space=pltpu.SMEM)
ANY = pl.BlockSpec(memory_space=pl.ANY)


def split2(x):
    high = x.astype(BF16)
    return high, (x - high.astype(F32)).astype(BF16)


def stacked(v):
    return jnp.concatenate(split2(v), axis=0)


def product(x, y):
    dot = functools.partial(jnp.dot, preferred_element_type=F32)
    return dot(x[0], y[0]) + (dot(x[0], y[1]) + dot(x[1], y[0]))


def row_index(width):
    return lax.broadcasted_iota(jnp.int32, (ROWS, width), 0)


def apply_pairs(vector, pair_of, lines):
    rows = row_index(vector.shape[1])
    both = stacked(vector)
    total = jnp.zeros(vector.shape, F32)
    for l in range(lines):
        high, low = pair_of(l)
        first = jnp.dot(both, high, preferred_element_type=F32)
        second = jnp.dot(both, low, preferred_element_type=F32)
        part = first[:ROWS] + first[ROWS:] + second[:ROWS]
        total = jnp.where(rows == l, part, total)
    return total


def apply_rows(vector, matrix_of, lines):
    rows = row_index(vector.shape[1])
    both = stacked(vector)
    total = jnp.zeros(vector.shape, F32)
    for l in range(lines):
        first = lax.dot_general(
            both, matrix_of(l), (((1,), (1,)), ((), ())), preferred_element_type=F32
        )
        total = jnp.where(rows == l, first[:ROWS] + first[ROWS:], total)
    return total


def core_of():
    return lax.rem(lax.axis_index("wall"), 2)


def chip_of():
    return lax.div(lax.axis_index("wall"), 2)


def relayout_kernel(dinv_ref, lower_ref, upper_ref, own_ref, send_ref, landed, arrived):
    kinds, depth, half = own_ref.shape[:3]
    core = core_of()
    copies = [
        [pltpu.make_async_copy(ref.at[e], landed.at[a, e], arrived.at[a, e]) for e in range(depth)]
        for a, ref in enumerate((dinv_ref, lower_ref, upper_ref))
    ]
    for copy in sum(copies, []):
        copy.start()
    for a in range(kinds):
        for e in range(depth):
            copies[a][e].wait()
            turned = jnp.swapaxes(landed[a, e], 0, 1)
            for l in range(half):
                own_ref[a, e, l] = jnp.where(core == 0, turned[l], turned[half + l])
                send_ref[a, e, l] = jnp.where(core == 0, turned[half + l], turned[l])


def pair_kernel(*refs, first):
    if first:
        raw_ref, q_ref, s_ref, a_ref, c_ref = refs
    else:
        raw_ref, _, _, a_own, c_own, q_ref, s_ref, a_ref, c_ref = refs
    core = core_of()
    place = core if first else 1 - core
    count, lines = raw_ref.shape[1], raw_ref.shape[2]
    for l in range(lines):
        qs, ss = [], []
        for e in range(count):
            for held, ref, source in ((qs, q_ref, 1), (ss, s_ref, 2)):
                block = lax.dot_general(
                    raw_ref[source, e, l],
                    raw_ref[0, e, l],
                    (((0,), (1,)), ((), ())),
                    preferred_element_type=F32,
                )
                pair = split2(block)
                held.append(pair)
                ref[place, e, l, 0] = pair[0]
                ref[place, e, l, 1] = pair[1]
        forward = qs[0]
        for e in range(1, count):
            forward = split2(product(forward, qs[e]))
        backward = ss[count - 1]
        for e in range(count - 2, -1, -1):
            backward = split2(product(backward, ss[e]))
        if not first:
            own = (a_own[l, 0], a_own[l, 1])
            early = [jnp.where(core == 0, x, y) for x, y in zip(own, forward)]
            late = [jnp.where(core == 0, y, x) for x, y in zip(own, forward)]
            forward = split2(product(early, late))
            own = (c_own[l, 0], c_own[l, 1])
            early = [jnp.where(core == 0, x, y) for x, y in zip(own, backward)]
            late = [jnp.where(core == 0, y, x) for x, y in zip(own, backward)]
            backward = split2(product(late, early))
        a_ref[l, 0], a_ref[l, 1] = forward
        c_ref[l, 0], c_ref[l, 1] = backward


def prepare_kernel(
    slot_ref, len_ref, coef_ref, nb_ref, source_ref, weight_ref, rhs_ref, act_ref, *, block
):
    faces, slots = coef_ref.shape
    depth, line_count = slot_ref.shape
    half = line_count // 2
    blocks = half // block
    core, chip = core_of(), chip_of()
    cells = 3 * slots
    k = lax.broadcasted_iota(jnp.int32, (cells, slots), 0)
    e = lax.broadcasted_iota(jnp.int32, (cells, slots), 1)
    weight = jnp.zeros((cells, slots), F32)
    own = jnp.zeros((1, slots), F32)
    for f in range(faces):
        coef = coef_ref[f : f + 1, :]
        own = own + coef
        weight = weight - jnp.where(k == nb_ref[f : f + 1, :], coef, 0.0)
    weight = weight + jnp.where(k == e + slots, own, 0.0)
    count = 2 * depth * blocks * ROWS
    rows = lax.broadcasted_iota(jnp.int32, (count, slots), 0)
    slot = jnp.full((count, slots), -1, jnp.int32)
    for h in range(2):
        first_line = lax.rem(core + h, 2) * half
        for g in range(depth):
            for b in range(blocks):
                for r in range(block):
                    row = ((h * depth + g) * blocks + b) * ROWS + r
                    here = slot_ref[g, first_line + b * block + r]
                    slot = jnp.where(rows == row, here, slot)
    chosen = (slot == lax.broadcasted_iota(jnp.int32, (count, slots), 1)).astype(F32).astype(BF16)
    high, rest = split2(weight)
    rest = weight - high.astype(F32)
    mid, low = split2(rest)
    for i, part in enumerate((high, mid, low)):
        weight_ref[i * count : (i + 1) * count, :] = lax.dot_general(
            chosen, part, (((1,), (1,)), ((), ())), preferred_element_type=F32
        ).astype(BF16)
    rhs_ref[...] = jnp.dot(chosen, source_ref[...], preferred_element_type=F32)
    width = act_ref.shape[2]
    rows = lax.broadcasted_iota(jnp.int32, (blocks * ROWS, width), 0)
    length = jnp.zeros((blocks * ROWS, width), jnp.int32)
    for b in range(blocks):
        for r in range(block):
            here = len_ref[core * half + b * block + r]
            length = jnp.where(rows == b * ROWS + r, here, length)
    for g in range(2 * depth):
        act_ref[g] = (chip * (2 * depth) + g < length).astype(F32)


def residual_kernel(before, state, after, weight, source, lift, own_ref, send_ref):
    cells = jnp.concatenate([before[...], state[...], after[...]], axis=0)
    parts = jnp.dot(weight[...], cells, preferred_element_type=F32)
    count = source.shape[0]
    face_sum = parts[:count] + (parts[count : 2 * count] + parts[2 * count :])
    flux = jnp.dot(face_sum.astype(BF16), lift[...], preferred_element_type=F32)
    rhs = source[...] - flux
    depth, rows, _ = own_ref.shape
    for g in range(depth):
        own_ref[g] = rhs[g * rows : (g + 1) * rows]
        send_ref[g] = rhs[(depth + g) * rows : (depth + g + 1) * rows]


def scaled_kernel(rhs_ref, raw_ref, out_ref):
    for e in range(rhs_ref.shape[0]):
        out_ref[e] = apply_rows(rhs_ref[e], lambda l: raw_ref[0, e, l], raw_ref.shape[2])


def forward_local(scaled, q_ref, act_ref, carried):
    depth, lines = q_ref.shape[1], q_ref.shape[2]
    values = []
    for g in range(2 * depth):
        value = scaled[g]
        if carried is not None:
            value = value - apply_pairs(
                carried, lambda l: (q_ref[g // depth, g % depth, l, 0], q_ref[g // depth, g % depth, l, 1]), lines
            )
        carried = act_ref[g] * value
        values.append(carried)
    return values


def backward_local(values, s_ref, act_ref, carried):
    depth, lines = s_ref.shape[1], s_ref.shape[2]
    solved = [None] * len(values)
    for g in range(2 * depth - 1, -1, -1):
        value = values[g]
        if carried is not None:
            value = value - apply_pairs(
                carried, lambda l: (s_ref[g // depth, g % depth, l, 0], s_ref[g // depth, g % depth, l, 1]), lines
            )
        carried = act_ref[g] * value
        solved[g] = carried
    return solved


def first_kernel(own_ref, rhs_ref, raw_ref, q_ref, act_ref, scaled_ref, b_ref):
    depth = own_ref.shape[0]
    core = core_of()
    own = [own_ref[e] for e in range(depth)]
    other = [
        apply_rows(rhs_ref[e], lambda l: raw_ref[0, e, l], raw_ref.shape[2]) for e in range(depth)
    ]
    scaled = [jnp.where(core == 0, x, y) for x, y in zip(own, other)]
    scaled += [jnp.where(core == 0, y, x) for x, y in zip(own, other)]
    for g in range(2 * depth):
        scaled_ref[g] = scaled[g]
    b_ref[...] = forward_local(scaled, q_ref, act_ref, None)[-1]


def hop_kernel(came_ref, pair_ref, act_ref, local_ref, out_ref, *, chip):
    out_ref[...] = local_ref[...]

    @pl.when(chip_of() == chip)
    def _():
        gone = apply_pairs(
            came_ref[...], lambda l: (pair_ref[l, 0], pair_ref[l, 1]), pair_ref.shape[0]
        )
        out_ref[...] = act_ref[act_ref.shape[0] - 1] * gone + local_ref[...]


def chosen_arrival(refs, chips):
    here = chip_of()
    value = jnp.zeros(refs[0].shape, F32)
    for ref, chip in zip(refs, chips):
        value = jnp.where(here == chip, ref[...], value)
    return value


def turn_kernel(scaled_ref, q_ref, s_ref, act_ref, *refs, chips):
    came, y_ref, d_ref = refs[:-2], refs[-2], refs[-1]
    count = scaled_ref.shape[0]
    carried = chosen_arrival(came, chips)
    values = forward_local([scaled_ref[g] for g in range(count)], q_ref, act_ref, carried)
    for g in range(count):
        y_ref[g] = values[g]
    d_ref[...] = backward_local(values, s_ref, act_ref, None)[0]


def last_kernel(y_ref, s_ref, act_ref, *refs, chips):
    came, own_ref, send_ref = refs[:-2], refs[-2], refs[-1]
    count = y_ref.shape[0]
    depth = count // 2
    core = core_of()
    carried = chosen_arrival(came, chips)
    solved = backward_local([y_ref[g] for g in range(count)], s_ref, act_ref, carried)
    for e in range(depth):
        own_ref[e] = jnp.where(core == 0, solved[e], solved[depth + e])
        send_ref[e] = jnp.where(core == 0, solved[depth + e], solved[e])


def merge_kernel(own_ref, other_ref, out_ref, *, block):
    core = core_of()
    blocks = own_ref.shape[1] // ROWS
    for e in range(out_ref.shape[0]):
        own = [own_ref[e, b * ROWS : b * ROWS + block] for b in range(blocks)]
        other = [other_ref[e, b * ROWS : b * ROWS + block] for b in range(blocks)]
        out_ref[e] = jnp.where(
            core == 0,
            jnp.concatenate(own + other, axis=0),
            jnp.concatenate(other + own, axis=0),
        )


def padded_bytes(shape, dtype):
    size = jnp.dtype(dtype).itemsize
    shape = (1,) * (2 - len(shape)) + tuple(shape)
    rows = -(-shape[-2] // 16) * 16
    columns = -(-shape[-1] // 128) * 128
    total = rows * columns * size
    for extent in shape[:-2]:
        total *= extent
    return total


def run(kernel, operands, outs, blocks=1, scratch=(), aliases=None):
    everything = [(x.shape, x.dtype) for x, _ in operands] + [(s, t) for s, t, _ in outs]
    everything += [(s.shape, s.dtype) for s in scratch if s.memory_space == pltpu.VMEM]
    limit = sum(padded_bytes(s, t) for s, t in everything)
    if blocks == 1:
        in_specs = [at if isinstance(at, pl.BlockSpec) else VMEM for _, at in operands]
        out_specs = [VMEM for _ in outs]
        grid = ()
    else:

        def spec(shape, at):
            if isinstance(at, pl.BlockSpec):
                return at
            if at is None:
                return pl.BlockSpec(shape, lambda i: (0,) * len(shape))
            size = tuple(n // blocks if axis == at else n for axis, n in enumerate(shape))
            return pl.BlockSpec(size, lambda i: tuple(i if axis == at else 0 for axis in range(len(shape))))

        in_specs = [spec(x.shape, at) for x, at in operands]
        out_specs = [spec(s, at) for s, _, at in outs]
        grid = (blocks,)
        limit = 2 * limit // blocks
    limit = min(limit + limit // 4 + (4 << 20), 60 << 20)
    return pl.pallas_call(
        kernel,
        grid=grid,
        in_specs=in_specs,
        out_specs=out_specs,
        out_shape=[jax.ShapeDtypeStruct(s, t) for s, t, _ in outs],
        scratch_shapes=list(scratch),
        input_output_aliases=aliases or {},
        compiler_params=pltpu.CompilerParams(vmem_limit_bytes=limit),
    )(*[x for x, _ in operands])


def flips(count):
    return [(i, i ^ 1) for i in range(count)]


def hop_pairs(count, start, end, spare):
    target = {i: i ^ 1 for i in range(count)}
    cycle = [start, end] + ([] if spare is None else [spare])
    for here, there in zip(cycle, cycle[1:] + cycle[:1]):
        for core in range(2):
            target[2 * here + core] = 2 * there + core
    return sorted(target.items())


def spare_chip(chips, start, end):
    behind = 2 * start - end
    if 0 <= behind < chips:
        return behind
    ahead = chips - 1 if end > start else 0
    return ahead if ahead not in (start, end) else None


def per_device(state, source, face_coef, neighbour, lift, elem_slot, line_len, dinv, lower, upper):
    wall_count = lax.axis_size("wall")
    surf_count = lax.axis_size("surf")
    chips = wall_count // 2
    depth, line_count, width, _ = dinv.shape
    half = line_count // 2
    block = max(n for n in range(1, ROWS + 1) if half % n == 0)
    blocks = half // block
    rows = blocks * ROWS
    core = lax.rem(lax.axis_index("wall"), 2)

    before = lax.ppermute(state, "surf", [(i, (i + 1) % surf_count) for i in range(surf_count)])
    after = lax.ppermute(state, "surf", [((i + 1) % surf_count, i) for i in range(surf_count)])

    raw_shape = (3, depth, half, width, width)
    if line_count == ROWS:
        turned = [jnp.transpose(x, (0, 2, 1, 3)) for x in (dinv, lower, upper)]
        own, send = run(
            relayout_kernel,
            [(x, ANY) for x in turned],
            [(raw_shape, BF16, None)] * 2,
            scratch=[
                pltpu.VMEM((3, depth, width, line_count, width), BF16),
                pltpu.SemaphoreType.DMA((3, depth)),
            ],
        )
    else:
        every = jnp.stack([dinv, lower, upper])
        own = lax.dynamic_slice_in_dim(every, core * half, half, axis=2)
        send = lax.dynamic_slice_in_dim(every, (1 - core) * half, half, axis=2)
    came = lax.ppermute(send, "wall", flips(wall_count))

    count = 2 * depth * rows
    weight, line_source, act = run(
        functools.partial(prepare_kernel, block=block),
        [
            (elem_slot, SMEM),
            (line_len, SMEM),
            (face_coef.T, None),
            (neighbour.T, None),
            (source, None),
        ],
        [
            ((3 * count, 3 * state.shape[0]), BF16, None),
            ((count, width), F32, None),
            ((2 * depth, rows, width), F32, None),
        ],
    )

    pairs_shape = (2, depth, half, 2, width, width)
    chip_shape = (half, 2, width, width)
    pair_outs = [(pairs_shape, BF16, 2), (pairs_shape, BF16, 2), (chip_shape, BF16, 0), (chip_shape, BF16, 0)]
    q_half, s_half, a_own, c_own = run(
        functools.partial(pair_kernel, first=True), [(own, 2)], pair_outs, blocks
    )
    own_rhs, send_rhs = run(
        residual_kernel,
        [(before, None), (state, None), (after, None), (weight, None), (line_source, None), (lift, None)],
        [((depth, rows, width), F32, None)] * 2,
    )
    came_rhs = lax.ppermute(send_rhs, "wall", flips(wall_count))
    (own_scaled,) = run(
        scaled_kernel, [(own_rhs, 1), (own, 2)], [((depth, rows, width), F32, 1)], blocks
    )
    q, s, a, c = run(
        functools.partial(pair_kernel, first=False),
        [(came, 2), (q_half, ANY), (s_half, ANY), (a_own, 0), (c_own, 0)],
        pair_outs,
        blocks,
        aliases={1: 0, 2: 1},
    )
    scaled, local = run(
        first_kernel,
        [(own_scaled, 1), (came_rhs, 1), (came, 2), (q, 2), (act, 1)],
        [((2 * depth, rows, width), F32, 1), ((rows, width), F32, 0)],
        blocks,
    )

    def hop(came, pair, local, chip):
        (out,) = run(
            functools.partial(hop_kernel, chip=chip),
            [(came, 0), (pair, 0), (act, 1), (local, 0)],
            [((rows, width), F32, 0)],
            blocks,
        )
        return out

    arrivals = []
    for chip in range(chips - 1):
        out = local if chip == 0 else hop(arrivals[-1], a, local, chip)
        pairs = hop_pairs(wall_count, chip, chip + 1, spare_chip(chips, chip, chip + 1))
        arrivals.append(lax.ppermute(out, "wall", pairs))
    y, back = run(
        functools.partial(turn_kernel, chips=list(range(1, chips))),
        [(scaled, 1), (q, 2), (s, 2), (act, 1)] + [(x, 0) for x in arrivals],
        [((2 * depth, rows, width), F32, 1), ((rows, width), F32, 0)],
        blocks,
    )
    arrivals = []
    for chip in range(chips - 1, 0, -1):
        out = back if chip == chips - 1 else hop(arrivals[-1], c, back, chip)
        pairs = hop_pairs(wall_count, chip, chip - 1, spare_chip(chips, chip, chip - 1))
        arrivals.append(lax.ppermute(out, "wall", pairs))
    own_part, send_part = run(
        functools.partial(last_kernel, chips=list(range(chips - 2, -1, -1))),
        [(y, 1), (s, 2), (act, 1)] + [(x, 0) for x in arrivals],
        [((depth, rows, width), F32, 1)] * 2,
        blocks,
    )
    other_part = lax.ppermute(send_part, "wall", flips(wall_count))
    (solution,) = run(
        functools.partial(merge_kernel, block=block),
        [(own_part, None), (other_part, None)],
        [((depth, line_count, width), F32, None)],
    )
    return solution


def solution(mesh):
    in_specs = (
        P(("wall", "surf"), None),
        P(("wall", "surf"), None),
        P(("wall", "surf"), None),
        P(("wall", "surf"), None),
        P(),
        P("wall", "surf"),
        P("surf"),
        P("wall", "surf", None, None),
        P("wall", "surf", None, None),
        P("wall", "surf", None, None),
    )
    out_specs = P("wall", "surf", None)
    return jax.shard_map(
        per_device, mesh=mesh, in_specs=in_specs, out_specs=out_specs, check_vma=False
    )
```

```python
import functools

import jax
import jax.numpy as jnp
from jax import lax
from jax.experimental import pallas as pl
from jax.experimental.pallas import tpu as pltpu
from jax.sharding import PartitionSpec as P

F32 = jnp.float32
BF16 = jnp.bfloat16
TILE = 8
VMEM = pl.BlockSpec(memory_space=pltpu.VMEM)
SMEM = pl.BlockSpec(memory_space=pltpu.SMEM)
HBM = pl.BlockSpec(memory_space=pltpu.HBM)


def split2(x):
    high = x.astype(BF16)
    return high, (x - high.astype(F32)).astype(BF16)


def product(x, y):
    dot = functools.partial(jnp.dot, preferred_element_type=F32)
    return dot(x[0], y[0]) + (dot(x[0], y[1]) + dot(x[1], y[0]))


def apply_pairs(vector, ref, *at):
    count = vector.shape[0]
    rows = lax.broadcasted_iota(jnp.int32, vector.shape, 0)
    both = jnp.concatenate(split2(vector), axis=0)
    total = jnp.zeros(vector.shape, F32)
    for l in range(count):
        first = jnp.dot(both, ref[(*at, l, 0)], preferred_element_type=F32)
        second = jnp.dot(both, ref[(*at, l, 1)], preferred_element_type=F32)
        total = jnp.where(rows == l, first[:count] + first[count:] + second[:count], total)
    return total


def apply_rows(vector, ref, *at):
    count = vector.shape[0]
    rows = lax.broadcasted_iota(jnp.int32, vector.shape, 0)
    both = jnp.concatenate(split2(vector), axis=0)
    total = jnp.zeros(vector.shape, F32)
    for l in range(count):
        first = lax.dot_general(
            both, ref[(*at, l)], (((1,), (1,)), ((), ())), preferred_element_type=F32
        )
        total = jnp.where(rows == l, first[:count] + first[count:], total)
    return total


def core_of():
    return lax.rem(lax.axis_index("wall"), 2)


def chip_of():
    return lax.div(lax.axis_index("wall"), 2)


def relayout_kernel(dinv_ref, lower_ref, upper_ref, raw_ref, landed, arrived):
    kinds, depth, lines = raw_ref.shape[:3]
    copies = [
        [pltpu.make_async_copy(ref.at[e], landed.at[a, e], arrived.at[a, e]) for e in range(depth)]
        for a, ref in enumerate((dinv_ref, lower_ref, upper_ref))
    ]
    for copy in sum(copies, []):
        copy.start()
    for a in range(kinds):
        for e in range(depth):
            copies[a][e].wait()
            turned = jnp.swapaxes(landed[a, e], 0, 1)
            for l in range(lines):
                raw_ref[a, e, l] = turned[l]


def pair_kernel(raw_ref, q_ref, s_ref, own_ref, send_ref):
    core = core_of()
    count, lines = raw_ref.shape[1], raw_ref.shape[2]
    for l in range(lines):
        qs, ss = [], []
        for e in range(count):
            for held, ref, source in ((qs, q_ref, 1), (ss, s_ref, 2)):
                block = lax.dot_general(
                    raw_ref[source, e, l],
                    raw_ref[0, e, l],
                    (((0,), (1,)), ((), ())),
                    preferred_element_type=F32,
                )
                pair = split2(block)
                held.append(pair)
                ref[e, l, 0], ref[e, l, 1] = pair
        forward = qs[0]
        for e in range(1, count):
            forward = split2(product(forward, qs[e]))
        backward = ss[count - 1]
        for e in range(count - 2, -1, -1):
            backward = split2(product(backward, ss[e]))
        if count % 2:
            forward, backward = [[-x for x in pair] for pair in (forward, backward)]
        for i in range(2):
            own_ref[l, i] = jnp.where(core == 0, backward[i], forward[i])
            send_ref[l, i] = jnp.where(core == 0, forward[i], backward[i])


def chip_kernel(got_ref, own_ref, chip_ref):
    for l in range(own_ref.shape[0]):
        pair = split2(product((got_ref[l, 0], got_ref[l, 1]), (own_ref[l, 0], own_ref[l, 1])))
        chip_ref[l, 0], chip_ref[l, 1] = pair


def through_kernel(len_ref, q_ref, s_ref, own_ref, send_ref, out_ref, *, last):
    depth, lines = q_ref.shape[:2]
    first_line = pl.program_id(0) * lines if pl_grid(len_ref, lines) else 0

    @pl.when(chip_of() == last)
    def _():
        core = core_of()
        place = lax.axis_index("wall") * depth
        for l in range(lines):
            length = len_ref[first_line + l]
            active = [(place + g < length).astype(F32) for g in range(depth)]
            whole = [jnp.where(core == 0, send_ref[l, i], own_ref[l, i]) for i in range(2)]
            steps = [(-q_ref[0, l, 0], -q_ref[0, l, 1])]
            for g in range(1, depth - 1):
                steps.append(split2(-product(steps[-1], (q_ref[g, l, 0], q_ref[g, l, 1]))))
            value = active[depth - 1] * (whole[0].astype(F32) + whole[1].astype(F32))
            for g in range(depth - 2, -1, -1):
                reach = steps[g][0].astype(F32) + steps[g][1].astype(F32)
                value = active[g] * (reach - product(split2(value), (s_ref[g, l, 0], s_ref[g, l, 1])))
            out_ref[l, 0], out_ref[l, 1] = split2(value)


def pl_grid(len_ref, lines):
    return len_ref.shape[0] != lines


def prepare_kernel(slot_ref, len_ref, coef_ref, nb_ref, source_ref, weight_ref, rhs_ref, act_ref):
    faces, slots = coef_ref.shape
    depth, lines = slot_ref.shape
    cells = 3 * slots
    k = lax.broadcasted_iota(jnp.int32, (cells, slots), 0)
    e = lax.broadcasted_iota(jnp.int32, (cells, slots), 1)
    weight = jnp.zeros((cells, slots), F32)
    own = jnp.zeros((1, slots), F32)
    for f in range(faces):
        coef = coef_ref[f : f + 1, :]
        own = own + coef
        weight = weight - jnp.where(k == nb_ref[f : f + 1, :], coef, 0.0)
    weight = weight + jnp.where(k == e + slots, own, 0.0)
    count = depth * lines
    rows = lax.broadcasted_iota(jnp.int32, (count, slots), 0)
    slot = jnp.zeros((count, slots), jnp.int32)
    for g in range(depth):
        for l in range(lines):
            slot = jnp.where(rows == g * lines + l, slot_ref[g, l], slot)
    chosen = (slot == lax.broadcasted_iota(jnp.int32, (count, slots), 1)).astype(F32).astype(BF16)
    high = weight.astype(BF16)
    mid, low = split2(weight - high.astype(F32))
    for i, part in enumerate((high, mid, low)):
        weight_ref[i * count : (i + 1) * count, :] = lax.dot_general(
            chosen, part, (((1,), (1,)), ((), ())), preferred_element_type=F32
        ).astype(BF16)
    rhs_ref[...] = jnp.dot(chosen, source_ref[...], preferred_element_type=F32)
    rows = lax.broadcasted_iota(jnp.int32, act_ref.shape[1:], 0)
    length = jnp.zeros(act_ref.shape[1:], jnp.int32)
    for l in range(lines):
        length = jnp.where(rows == l, len_ref[l], length)
    place = lax.axis_index("wall") * depth
    for g in range(depth):
        act_ref[g] = (place + g < length).astype(F32)


def residual_kernel(before, state, after, weight, source, lift, rhs_ref):
    cells = jnp.concatenate([before[...], state[...], after[...]], axis=0)
    parts = jnp.dot(weight[...], cells, preferred_element_type=F32)
    count = source.shape[0]
    face_sum = parts[:count] + (parts[count : 2 * count] + parts[2 * count :])
    flux = jnp.dot(face_sum.astype(BF16), lift[...], preferred_element_type=F32)
    rhs = source[...] - flux
    depth, lines, _ = rhs_ref.shape
    for g in range(depth):
        rhs_ref[g] = rhs[g * lines : (g + 1) * lines]


def forward_local(scaled, q_ref, act_ref, carried):
    values = []
    for g, value in enumerate(scaled):
        if carried is not None:
            value = value - apply_pairs(carried, q_ref, g)
        carried = act_ref[g] * value
        values.append(carried)
    return values


def backward_local(values, s_ref, act_ref, carried):
    solved = [None] * len(values)
    for g in range(len(values) - 1, -1, -1):
        value = values[g]
        if carried is not None:
            value = value - apply_pairs(carried, s_ref, g)
        carried = act_ref[g] * value
        solved[g] = carried
    return solved


def local_kernel(rhs_ref, raw_ref, q_ref, act_ref, scaled_ref, y_ref):
    depth = rhs_ref.shape[0]
    scaled = [apply_rows(rhs_ref[g], raw_ref, 0, g) for g in range(depth)]
    values = forward_local(scaled, q_ref, act_ref, None)
    for g in range(depth):
        scaled_ref[g] = scaled[g]
        y_ref[g] = values[g]


def chip_local_kernel(came_ref, own_ref, act_ref, y_ref, out_ref):
    depth = y_ref.shape[0]
    out_ref[...] = y_ref[depth - 1]

    @pl.when(core_of() == 1)
    def _():
        out_ref[...] = act_ref[depth - 1] * apply_pairs(came_ref[...], own_ref) + y_ref[depth - 1]


def echo_kernel(y_ref, s_ref, act_ref, out_ref):
    depth = y_ref.shape[0]
    out_ref[...] = backward_local([y_ref[g] for g in range(depth)], s_ref, act_ref, None)[0]


def hop_kernel(came_ref, pair_ref, act_ref, local_ref, out_ref, *, chip, core):
    out_ref[...] = local_ref[...]

    @pl.when(jnp.logical_and(chip_of() == chip, core_of() == core))
    def _():
        gone = apply_pairs(came_ref[...], pair_ref)
        out_ref[...] = act_ref[act_ref.shape[0] - 1] * gone + local_ref[...]


def chosen_arrival(refs, chips, like):
    here = chip_of()
    value = jnp.zeros(like, F32)
    for ref, chip in zip(refs, chips):
        value = jnp.where(here == chip, ref[...], value)
    return value


def enter_kernel(echo_ref, *refs, chips):
    out_ref = refs[-1]
    out_ref[0] = chosen_arrival(refs[:-1], chips, echo_ref.shape)
    out_ref[1] = echo_ref[...]


def turn_kernel(
    enter_ref, met_ref, echo_ref, y_ref, act_ref, send_ref, own_ref, own_d, came_d, out_ref, mid_ref, *, last
):
    depth = y_ref.shape[0]
    out_ref[...] = echo_ref[...]
    mid_ref[...] = echo_ref[...]

    @pl.when(jnp.logical_and(chip_of() == last, core_of() == 0))
    def _():
        enter = enter_ref[...]
        leave = act_ref[depth - 1] * apply_pairs(enter, send_ref) + y_ref[depth - 1]
        first = apply_pairs(enter, own_d) + echo_ref[...]
        middle = apply_pairs(leave, came_d) + met_ref[1]
        mid_ref[...] = middle
        out_ref[...] = apply_pairs(middle, own_ref) + first


def inner_kernel(entered_ref, met_ref, got_ref, came_ref, scaled_ref, q_ref, s_ref, act_ref, y_ref, first_ref, flow, *, last):
    depth = scaled_ref.shape[0]

    @pl.when(chip_of() != last)
    def _():
        flow[...] = met_ref[0]

        @pl.when(core_of() == 1)
        def _():
            flow[...] = apply_pairs(entered_ref[0], got_ref) + came_ref[...]

        scaled = [scaled_ref[g] for g in range(depth)]
        values = forward_local(scaled, q_ref, act_ref, flow[...])
        for g in range(depth):
            y_ref[g] = values[g]
        first_ref[...] = backward_local(values, s_ref, act_ref, None)[0]


def inner_chip_kernel(met_ref, first_ref, own_ref, out_ref):
    @pl.when(core_of() == 0)
    def _():
        out_ref[...] = apply_pairs(met_ref[...], own_ref) + first_ref[...]


def leave_kernel(enter_ref, *refs, chips):
    out_ref = refs[-1]
    out_ref[0] = chosen_arrival(refs[:-1], chips, enter_ref.shape)
    out_ref[1] = enter_ref[...]


def middle_kernel(leave_ref, got_ref, met_ref, mid_ref, out_ref, *, last):
    out_ref[...] = mid_ref[...]

    @pl.when(jnp.logical_and(chip_of() != last, core_of() == 0))
    def _():
        out_ref[...] = apply_pairs(leave_ref[0], got_ref) + met_ref[...]


def last_kernel(
    met_ref, middle_ref, enter_ref, came_ref, got_ref, scaled_ref, q_ref, s_ref, act_ref, y_ref, out_ref, flow, held, *, last
):
    depth = y_ref.shape[0]
    core = core_of()
    for g in range(depth):
        held[g] = y_ref[g]

    @pl.when(chip_of() == last)
    def _():
        flow[...] = enter_ref[...]

        @pl.when(core == 1)
        def _():
            flow[...] = apply_pairs(met_ref[1], got_ref) + came_ref[...]

        scaled = [scaled_ref[g] for g in range(depth)]
        for g, value in enumerate(forward_local(scaled, q_ref, act_ref, flow[...])):
            held[g] = value

    carried = jnp.where(core == 0, middle_ref[...], met_ref[0])
    solved = backward_local([held[g] for g in range(depth)], s_ref, act_ref, carried)
    for g in range(depth):
        out_ref[g] = solved[g]


def padded_bytes(shape, dtype):
    size = jnp.dtype(dtype).itemsize
    shape = (1,) * (2 - len(shape)) + tuple(shape)
    total = -(-shape[-2] // 16) * 16 * -(-shape[-1] // 128) * 128 * size
    for extent in shape[:-2]:
        total *= extent
    return total


def run(kernel, operands, outs, blocks=1, scratch=()):
    held = [(x.shape, x.dtype) for x, _ in operands] + [(s, t) for s, t, _ in outs]
    limit = sum(padded_bytes(s, t) for s, t in held)
    if blocks == 1:
        in_specs = [at if isinstance(at, pl.BlockSpec) else VMEM for _, at in operands]
        out_specs = [VMEM for _ in outs]
        grid = ()
    else:

        def spec(shape, at):
            if isinstance(at, pl.BlockSpec):
                return at
            if at is None:
                return pl.BlockSpec(shape, lambda i: (0,) * len(shape))
            size = tuple(n // blocks if axis == at else n for axis, n in enumerate(shape))
            return pl.BlockSpec(size, lambda i: tuple(i if axis == at else 0 for axis in range(len(shape))))

        in_specs = [spec(x.shape, at) for x, at in operands]
        out_specs = [spec(s, at) for s, _, at in outs]
        grid = (blocks,)
        limit = 2 * limit // blocks
    limit += sum(padded_bytes(s.shape, s.dtype) for s in scratch if s.memory_space == pltpu.VMEM)
    limit = min(limit + limit // 4 + (4 << 20), 60 << 20)
    return pl.pallas_call(
        kernel,
        grid=grid,
        in_specs=in_specs,
        out_specs=out_specs,
        out_shape=[jax.ShapeDtypeStruct(s, t) for s, t, _ in outs],
        scratch_shapes=list(scratch),
        compiler_params=pltpu.CompilerParams(vmem_limit_bytes=limit),
    )(*[x for x, _ in operands])


def hop_pairs(count, start, end):
    target = {i: i ^ 1 for i in range(count)}
    target.update({start: end, end: end ^ 1, end ^ 1: start ^ 1, start ^ 1: start})
    return sorted(target.items())


def per_device(state, source, face_coef, neighbour, lift, elem_slot, line_len, dinv, lower, upper):
    wall_count = lax.axis_size("wall")
    surf_count = lax.axis_size("surf")
    chips = wall_count // 2
    last = chips - 1
    depth, lines, width, _ = dinv.shape
    slots = state.shape[0]
    block = TILE if lines % TILE == 0 else lines
    blocks = lines // block
    flips = [(i, i ^ 1) for i in range(wall_count)]
    line_vector = ((lines, width), F32, 0)
    two_vectors = ((2, lines, width), F32, 1)
    element_vectors = ((depth, lines, width), F32, 1)
    line_pairs = ((lines, 2, width, width), BF16, 0)
    element_pairs = ((depth, lines, 2, width, width), BF16, 1)
    flow = pltpu.VMEM((block, width), F32)

    before = lax.ppermute(state, "surf", [(i, (i + 1) % surf_count) for i in range(surf_count)])
    after = lax.ppermute(state, "surf", [((i + 1) % surf_count, i) for i in range(surf_count)])

    raw_shape = (3, depth, lines, width, width)
    if lines == TILE:
        (raw,) = run(
            relayout_kernel,
            [(jnp.transpose(x, (0, 2, 1, 3)), HBM) for x in (dinv, lower, upper)],
            [(raw_shape, BF16, None)],
            scratch=[
                pltpu.VMEM((3, depth, width, lines, width), BF16),
                pltpu.SemaphoreType.DMA((3, depth)),
            ],
        )
    else:
        raw = jnp.stack([dinv, lower, upper])
    q, s, own, send = run(
        pair_kernel, [(raw, 2)], [element_pairs, element_pairs, line_pairs, line_pairs], blocks
    )
    got = lax.ppermute(send, "wall", flips)

    count = depth * lines
    weight, line_source, act = run(
        prepare_kernel,
        [(elem_slot, SMEM), (line_len, SMEM), (face_coef.T, None), (neighbour.T, None), (source, None)],
        [((3 * count, 3 * slots), BF16, None), ((count, width), F32, None), element_vectors],
    )
    (rhs,) = run(
        residual_kernel,
        [(before, None), (state, None), (after, None), (weight, None), (line_source, None), (lift, None)],
        [element_vectors],
    )
    scaled, y_local = run(
        local_kernel,
        [(rhs, 1), (raw, 2), (q, 1), (act, 1)],
        [element_vectors, element_vectors],
        blocks,
    )
    came_y = lax.ppermute(y_local[depth - 1], "wall", flips)
    (chip,) = run(chip_kernel, [(got, 0), (own, 0)], [line_pairs], blocks)
    (y_chip,) = run(
        chip_local_kernel, [(came_y, 0), (own, 0), (act, 1), (y_local, 1)], [line_vector], blocks
    )
    (through,) = run(
        functools.partial(through_kernel, last=last),
        [(line_len, SMEM), (q, 1), (s, 1), (own, 0), (send, 0)],
        [line_pairs],
        blocks,
    )
    came_through = lax.ppermute(through, "wall", flips)
    (echo,) = run(echo_kernel, [(y_local, 1), (s, 1), (act, 1)], [line_vector], blocks)

    def hop(came, local, at, core):
        (out,) = run(
            functools.partial(hop_kernel, chip=at, core=core),
            [(came, 0), (chip, 0), (act, 1), (local, 0)],
            [line_vector],
            blocks,
        )
        return out

    arrivals = []
    for at in range(last):
        if at == last - 1:
            (entered,) = run(
                functools.partial(enter_kernel, chips=list(range(1, last))),
                [(echo, 0)] + [(x, 0) for x in arrivals],
                [two_vectors],
                blocks,
            )
        out = y_chip if at == 0 else hop(arrivals[-1], y_chip, at, 1)
        end = 2 * at + 3 if at + 1 < last else 2 * last
        arrivals.append(lax.ppermute(out, "wall", hop_pairs(wall_count, 2 * at + 1, end)))
    met = lax.ppermute(entered, "wall", flips)
    enter_last = arrivals[-1]
    x_last, x_middle = run(
        functools.partial(turn_kernel, last=last),
        [(enter_last, 0), (met, 1), (echo, 0), (y_local, 1), (act, 1)]
        + [(x, 0) for x in (send, own, through, came_through)],
        [line_vector, line_vector],
        blocks,
    )
    y, first = run(
        functools.partial(inner_kernel, last=last),
        [(entered, 1), (met, 1), (got, 0), (came_y, 0), (scaled, 1), (q, 1), (s, 1), (act, 1)],
        [element_vectors, line_vector],
        blocks,
        [flow],
    )
    arrivals = [lax.ppermute(x_last, "wall", hop_pairs(wall_count, 2 * last, 2 * last - 2))]
    came_first = lax.ppermute(first, "wall", flips)
    (x_chip,) = run(inner_chip_kernel, [(came_first, 0), (first, 0), (own, 0)], [line_vector], blocks)
    for at in range(last - 1, 0, -1):
        out = hop(arrivals[-1], x_chip, at, 0)
        arrivals.append(lax.ppermute(out, "wall", hop_pairs(wall_count, 2 * at, 2 * at - 2)))
    (left,) = run(
        functools.partial(leave_kernel, chips=list(range(last - 1, -1, -1))),
        [(enter_last, 0)] + [(x, 0) for x in arrivals],
        [two_vectors],
        blocks,
    )
    met_left = lax.ppermute(left, "wall", flips)
    (middle,) = run(
        functools.partial(middle_kernel, last=last),
        [(left, 1), (got, 0), (came_first, 0), (x_middle, 0)],
        [line_vector],
        blocks,
    )
    (solution,) = run(
        functools.partial(last_kernel, last=last),
        [(met_left, 1), (middle, 0), (enter_last, 0), (came_y, 0), (got, 0)]
        + [(x, 1) for x in (scaled, q, s, act, y)],
        [element_vectors],
        blocks,
        [flow, pltpu.VMEM((depth, block, width), F32)],
    )
    return solution


def solution(mesh):
    in_specs = (
        P(("wall", "surf"), None),
        P(("wall", "surf"), None),
        P(("wall", "surf"), None),
        P(("wall", "surf"), None),
        P(),
        P("wall", "surf"),
        P("surf"),
        P("wall", "surf", None, None),
        P("wall", "surf", None, None),
        P("wall", "surf", None, None),
    )
    out_specs = P("wall", "surf", None)
    return jax.shard_map(
        per_device, mesh=mesh, in_specs=in_specs, out_specs=out_specs, check_vma=False
    )
```

```python
import functools

import jax
import jax.numpy as jnp
from jax import lax
from jax.experimental import pallas as pl
from jax.experimental.pallas import tpu as pltpu
from jax.sharding import PartitionSpec as P

F32 = jnp.float32
BF16 = jnp.bfloat16
TILE = 8
LANES = 128
VMEM = pl.BlockSpec(memory_space=pltpu.VMEM)
ANY = pl.BlockSpec(memory_space=pl.ANY)
SMEM = pl.BlockSpec(memory_space=pltpu.SMEM)


def split2(x):
    high = x.astype(BF16)
    return high, (x - high.astype(F32)).astype(BF16)


def product(x, y):
    dot = functools.partial(jnp.dot, preferred_element_type=F32)
    return dot(x[0], y[0]) + (dot(x[0], y[1]) + dot(x[1], y[0]))


def room_of(width):
    rows = -(-width // (2 * TILE)) * 2 * TILE
    main = width // LANES * LANES
    return rows, 2 * main + (LANES if width - main <= LANES // 2 else 2 * LANES), main


def pair_at(ref, width, *at):
    if len(ref.shape) > 2:
        return [ref[(*at, i)] for i in range(2)]
    rows, columns, main = room_of(width)
    here = pl.ds(at[0] * rows, width)
    step = (columns - 2 * main) // 2
    if width == main:
        return [ref[here, i * main : (i + 1) * main] for i in range(2)]
    return [
        jnp.concatenate(
            [
                ref[here, i * main : (i + 1) * main],
                ref[here, 2 * main + i * step : 2 * main + i * step + width - main],
            ],
            axis=1,
        )
        for i in range(2)
    ]


def store_pair(ref, pair, *at):
    if len(ref.shape) > 2:
        for i in range(2):
            ref[(*at, i)] = pair[i]
        return
    width = pair[0].shape[0]
    rows, columns, main = room_of(width)
    here = pl.ds(at[0] * rows, width)
    step = (columns - 2 * main) // 2
    for i in range(2):
        ref[here, i * main : (i + 1) * main] = pair[i][:, :main]
        if width > main:
            ref[here, 2 * main + i * step : 2 * main + i * step + width - main] = pair[i][:, main:]


def apply_pairs(vector, ref, *at):
    count = vector.shape[0]
    rows = lax.broadcasted_iota(jnp.int32, vector.shape, 0)
    both = jnp.concatenate(split2(vector), axis=0)
    total = jnp.zeros(vector.shape, F32)
    for l in range(count):
        part, here = ref, l
        if isinstance(ref, (list, tuple)):
            each = count // len(ref)
            part, here = ref[l // each], l % each
        high, low = pair_at(part, vector.shape[1], *at, here)
        first = jnp.dot(both, high, preferred_element_type=F32)
        second = jnp.dot(both, low, preferred_element_type=F32)
        total = jnp.where(rows == l, first[:count] + first[count:] + second[:count], total)
    return total


def apply_rows(vector, ref, *at):
    count = vector.shape[0]
    rows = lax.broadcasted_iota(jnp.int32, vector.shape, 0)
    both = jnp.concatenate(split2(vector), axis=0)
    total = jnp.zeros(vector.shape, F32)
    for l in range(count):
        first = lax.dot_general(
            both, ref[(*at, l)], (((1,), (1,)), ((), ())), preferred_element_type=F32
        )
        total = jnp.where(rows == l, first[:count] + first[count:], total)
    return total


def core_of():
    return lax.rem(lax.axis_index("wall"), 2)


def chip_of():
    return lax.div(lax.axis_index("wall"), 2)


def pair_kernel(raw_ref, *refs, first_chip, **options):
    @pl.when(chip_of() >= first_chip)
    def _():
        make_pairs(raw_ref, *refs[-3:], **options)


def make_pairs(raw_ref, step_ref, whole_ref, sent_ref, *, kind, lines, ascending):
    count = raw_ref.shape[1]
    for l in range(*lines):
        steps = []
        for e in range(count):
            block = lax.dot_general(
                raw_ref[kind, e, l], raw_ref[0, e, l], (((0,), (1,)), ((), ())), preferred_element_type=F32
            )
            steps.append(split2(block))
            store_pair(step_ref, steps[-1], e, l)
        if not ascending:
            steps = steps[::-1]
        whole = steps[0]
        for step in steps[1:]:
            whole = split2(product(whole, step))
        if count % 2:
            whole = [-x for x in whole]
        store_pair(whole_ref, whole, l - lines[0])
        store_pair(sent_ref, whole, l - lines[0])


def chip_kernel(*refs, parts, width, own_first):
    got_refs, own_refs, chip_ref = refs[:parts], refs[parts:-1], refs[-1]

    @pl.when(core_of() == 1)
    def _():
        each = chip_ref.shape[0] // parts
        for l in range(chip_ref.shape[0]):
            pairs = [pair_at(x[l // each], width, l % each) for x in (got_refs, own_refs)]
            store_pair(chip_ref, split2(product(*(pairs[::-1] if own_first else pairs))), l)


def relayout_kernel(*refs, kinds):
    raw_ref, landed, arrived = refs[-3:]
    _, depth, lines = raw_ref.shape[:3]
    copies = [
        pltpu.make_async_copy(ref.at[e], landed.at[a, e], arrived.at[a, e])
        for a, ref in enumerate(refs[:kinds])
        for e in range(depth)
    ]
    for copy in copies:
        copy.start()
    for i, copy in enumerate(copies):
        copy.wait()
        a, e = divmod(i, depth)
        turned = jnp.swapaxes(landed[a, e], 0, 1)
        for l in range(lines):
            raw_ref[a, e, l] = turned[l]


def prepare_kernel(*refs):
    places, (weight_ref, rhs_ref, act_ref, state_ref, lift_ref) = refs[:7], refs[7:12]
    slot_ref, len_ref, coef_ref, nb_ref, source_ref, arrived = refs[12:]
    targets = (slot_ref, len_ref, coef_ref, nb_ref, source_ref, state_ref, lift_ref)
    copies = [
        pltpu.make_async_copy(there, here, arrived.at[i]) for i, (there, here) in enumerate(zip(places, targets))
    ]
    for copy in copies:
        copy.start()
    for copy in copies:
        copy.wait()
    faces, slots = coef_ref.shape
    depth, lines = slot_ref.shape
    cells = 3 * slots
    k = lax.broadcasted_iota(jnp.int32, (cells, slots), 0)
    e = lax.broadcasted_iota(jnp.int32, (cells, slots), 1)
    weight = jnp.zeros((cells, slots), F32)
    own = jnp.zeros((1, slots), F32)
    for f in range(faces):
        coef = coef_ref[f : f + 1, :]
        own = own + coef
        weight = weight - jnp.where(k == nb_ref[f : f + 1, :], coef, 0.0)
    weight = weight + jnp.where(k == e + slots, own, 0.0)
    count = depth * lines
    rows = lax.broadcasted_iota(jnp.int32, (count, slots), 0)
    slot = jnp.zeros((count, slots), jnp.int32)
    for g in range(depth):
        for l in range(lines):
            slot = jnp.where(rows == g * lines + l, slot_ref[g, l], slot)
    chosen = (slot == lax.broadcasted_iota(jnp.int32, (count, slots), 1)).astype(F32).astype(BF16)
    high = weight.astype(BF16)
    mid, low = split2(weight - high.astype(F32))
    for i, part in enumerate((high, mid, low)):
        weight_ref[i * count : (i + 1) * count, :] = lax.dot_general(
            chosen, part, (((1,), (1,)), ((), ())), preferred_element_type=F32
        ).astype(BF16)
    rhs_ref[...] = jnp.dot(chosen, source_ref[...], preferred_element_type=F32)
    rows = lax.broadcasted_iota(jnp.int32, act_ref.shape[1:], 0)
    length = jnp.zeros(act_ref.shape[1:], jnp.int32)
    for l in range(lines):
        length = jnp.where(rows == l, len_ref[l], length)
    place = lax.axis_index("wall") * depth
    for g in range(depth):
        act_ref[g] = (place + g < length).astype(F32)


def residual_kernel(before, state, after, weight, source, lift, rhs_ref):
    cells = jnp.concatenate([before[...], state[...], after[...]], axis=0)
    parts = jnp.dot(weight[...], cells, preferred_element_type=F32)
    count = source.shape[0]
    face_sum = parts[:count] + (parts[count : 2 * count] + parts[2 * count :])
    flux = jnp.dot(face_sum.astype(BF16), lift[...], preferred_element_type=F32)
    rhs = source[...] - flux
    depth, lines, _ = rhs_ref.shape
    for g in range(depth):
        rhs_ref[g] = rhs[g * lines : (g + 1) * lines]


def forward_local(scaled, q_ref, act_ref, carried):
    values = []
    for g, value in enumerate(scaled):
        if carried is not None:
            value = value - apply_pairs(carried, q_ref, g)
        carried = act_ref[g] * value
        values.append(carried)
    return values


def backward_local(values, s_ref, act_ref, carried):
    solved = [None] * len(values)
    for g in range(len(values) - 1, -1, -1):
        value = values[g]
        if carried is not None:
            value = value - apply_pairs(carried, s_ref, g)
        carried = act_ref[g] * value
        solved[g] = carried
    return solved


def local_kernel(rhs_ref, raw_ref, act_ref, scaled_ref, y_ref, leave_ref):
    depth = rhs_ref.shape[0]
    scaled = [apply_rows(rhs_ref[g], raw_ref, 0, g) for g in range(depth)]
    values = raw_steps(scaled, raw_ref, act_ref, None)
    for g in range(depth):
        scaled_ref[g] = scaled[g]
        y_ref[g] = values[g]
    leave_ref[...] = values[-1]


def raw_steps(scaled, raw_ref, act_ref, carried):
    values = []
    for g, value in enumerate(scaled):
        if carried is not None:
            value = value - apply_rows(apply_rows(carried, raw_ref, 1, g), raw_ref, 0, g)
        carried = act_ref[g] * value
        values.append(carried)
    return values


def wall_kernel(came_ref, scaled_ref, raw_ref, act_ref, y_ref, out_ref, leave_ref):
    depth = y_ref.shape[0]
    out_ref[...] = y_ref[...]
    leave_ref[...] = y_ref[depth - 1]

    @pl.when(lax.axis_index("wall") == 1)
    def _():
        values = raw_steps([scaled_ref[g] for g in range(depth)], raw_ref, act_ref, came_ref[...])
        for g in range(depth):
            out_ref[g] = values[g]
        leave_ref[...] = values[-1]


def chip_local_kernel(came_ref, act_ref, y_ref, *refs):
    own_refs, out_ref = refs[:-1], refs[-1]
    depth = y_ref.shape[0]
    out_ref[...] = y_ref[depth - 1]

    @pl.when(jnp.logical_and(core_of() == 1, chip_of() > 0))
    def _():
        out_ref[...] = act_ref[depth - 1] * apply_pairs(came_ref[...], own_refs) + y_ref[depth - 1]


def hop_kernel(came_ref, act_ref, local_ref, *refs, chip):
    pair_refs, out_ref = refs[:-1], refs[-1]
    out_ref[...] = local_ref[...]

    @pl.when(jnp.logical_and(chip_of() == chip, core_of() == 1))
    def _():
        gone = apply_pairs(came_ref[...], pair_refs)
        out_ref[...] = act_ref[act_ref.shape[0] - 1] * gone + local_ref[...]


def early_hop_kernel(came_ref, act_ref, mate_ref, y_ref, *refs, chip, parts):
    got_refs, own_refs, out_ref = refs[:parts], refs[parts : 2 * parts], refs[-1]
    depth = y_ref.shape[0]
    out_ref[...] = came_ref[...]

    @pl.when(jnp.logical_and(chip_of() == chip, core_of() == 1))
    def _():
        middle = apply_pairs(came_ref[...], got_refs) + mate_ref[...]
        out_ref[...] = act_ref[depth - 1] * apply_pairs(middle, own_refs) + y_ref[depth - 1]


def chosen_arrival(refs, chips, like):
    here = chip_of()
    value = jnp.zeros(like, F32)
    for ref, chip in zip(refs, chips):
        value = jnp.where(here == chip, ref[...], value)
    return value


def choose_kernel(*refs, chips):
    refs[-1][...] = chosen_arrival(refs[:-1], chips, refs[-1].shape)


def inner_kernel(
    direct_ref, met_ref, came_ref, scaled_ref, q_ref, s_ref, act_ref, wall_ref, *refs, on_last, last, parts
):
    got_refs = refs[:parts]
    y_ref, first_ref, flow = refs[-3:]
    depth = scaled_ref.shape[0]
    here = chip_of()

    @pl.when(here == last if on_last else jnp.logical_and(here > 0, here != last))
    def _():
        flow[...] = met_ref[...]

        @pl.when(core_of() == 1)
        def _():
            flow[...] = apply_pairs(direct_ref[...], got_refs) + came_ref[...]

        values = forward_local([scaled_ref[g] for g in range(depth)], q_ref, act_ref, flow[...])
        for g in range(depth):
            y_ref[g] = values[g]

    if not on_last:

        @pl.when(here == 0)
        def _():
            y_ref[...] = wall_ref[...]

    @pl.when(here == last if on_last else here != last)
    def _():
        first_ref[...] = backward_local([y_ref[g] for g in range(depth)], s_ref, act_ref, None)[0]


def reach_kernel(first_ref, got_ref, out_ref):
    @pl.when(core_of() == 1)
    def _():
        out_ref[...] = apply_pairs(first_ref[...], got_ref)


def add_kernel(x_ref, y_ref, out_ref):
    out_ref[...] = x_ref[...] + y_ref[...]


def leave_kernel(own_ref, first_ref, *refs, chips):
    came_ref, out_ref = refs[-2:]
    came_ref[...] = chosen_arrival(refs[:-2], chips, came_ref.shape)
    out_ref[...] = first_ref[...]

    @pl.when(core_of() == 1)
    def _():
        out_ref[...] = apply_pairs(came_ref[...], own_ref) + first_ref[...]


def last_kernel(beyond_ref, met_ref, s_ref, act_ref, y_ref, out_ref):
    depth = y_ref.shape[0]
    carried = jnp.where(core_of() == 0, met_ref[...], beyond_ref[...])
    solved = backward_local([y_ref[g] for g in range(depth)], s_ref, act_ref, carried)
    for g in range(depth):
        out_ref[g] = solved[g]


def padded_bytes(shape, dtype):
    size = jnp.dtype(dtype).itemsize
    shape = (1,) * (2 - len(shape)) + tuple(shape)
    total = -(-shape[-2] // 16) * 16 * -(-shape[-1] // 128) * 128 * size
    for extent in shape[:-2]:
        total *= extent
    return total


def run(kernel, operands, outs, blocks=1, scratch=(), aliases=None):
    held = [(x.shape, x.dtype) for x, _ in operands] + [(s, t) for s, t, _ in outs]
    limit = sum(padded_bytes(s, t) for s, t in held)
    if blocks == 1:
        in_specs = [at if isinstance(at, pl.BlockSpec) else VMEM for _, at in operands]
        out_specs = [VMEM for _ in outs]
        grid = ()
    else:

        def spec(shape, at):
            if isinstance(at, pl.BlockSpec):
                return at
            if at is None:
                return pl.BlockSpec(shape, lambda i: (0,) * len(shape))
            size = tuple(n // blocks if axis == at else n for axis, n in enumerate(shape))
            return pl.BlockSpec(size, lambda i: tuple(i if axis == at else 0 for axis in range(len(shape))))

        in_specs = [spec(x.shape, at) for x, at in operands]
        out_specs = [spec(s, at) for s, _, at in outs]
        grid = (blocks,)
        limit = 2 * limit // blocks
    limit += sum(padded_bytes(s.shape, s.dtype) for s in scratch if s.memory_space == pltpu.VMEM)
    limit = min(limit + (2 << 20), 60 << 20)
    return pl.pallas_call(
        kernel,
        grid=grid,
        in_specs=in_specs,
        out_specs=out_specs,
        out_shape=[jax.ShapeDtypeStruct(s, t) for s, t, _ in outs],
        scratch_shapes=list(scratch),
        input_output_aliases=aliases or {},
        compiler_params=pltpu.CompilerParams(vmem_limit_bytes=limit),
        cost_estimate=pl.CostEstimate(flops=1, bytes_accessed=1, transcendentals=0),
    )(*[x for x, _ in operands])


def hop_pairs(count, start, end, core=1):
    start, end = 2 * start + 1, 2 * end + core
    target = {i: i ^ 1 for i in range(count)}
    target.update({start: end, end: end ^ 1, end ^ 1: start ^ 1, start ^ 1: start})
    return sorted(target.items())


def in_hbm(value):
    return pltpu.with_memory_space_constraint(value, pltpu.HBM)


def after(value, *others):
    return lax.optimization_barrier((value, *others))[0]


def per_device(state, source, face_coef, neighbour, lift, elem_slot, line_len, dinv, lower, upper):
    wall_count = lax.axis_size("wall")
    surf_count = lax.axis_size("surf")
    last = wall_count // 2 - 1
    depth, lines, width, _ = dinv.shape
    slots = state.shape[0]
    block = TILE if lines % TILE == 0 else lines
    blocks = lines // block
    parts = 2 if blocks == 1 and lines % 2 == 0 else 1
    room, columns, _ = room_of(width)
    line_vector = ((lines, width), F32, 0)
    element_vectors = ((depth, lines, width), F32, 1)
    line_sent = ((lines * room, columns), BF16, 0)
    line_pairs = ((lines, 2, width, width), BF16, 0)
    part_sent = ((lines // parts * room, columns), BF16, 0)
    part_pairs = ((lines // parts, 2, width, width), BF16, 0)
    element_pairs = ((depth, lines, 2, width, width), BF16, 1)

    def mates(value):
        return lax.ppermute(value, "wall", [(i, i ^ 1) for i in range(wall_count)])

    count = depth * lines
    rows = lax.broadcasted_iota(jnp.int32, (count, slots), 0)
    slot = jnp.zeros((count, slots), jnp.int32)
    for g in range(depth):
        for l in range(lines):
            slot = jnp.where(rows == g * lines + l, slot_ref[g, l], slot)
    chosen = (slot == lax.broadcasted_iota(jnp.int32, (count, slots), 1)).astype(F32).astype(BF16)
    high = weight.astype(BF16)
    mid, low = split2(weight - high.astype(F32))
    for i, part in enumerate((high, mid, low)):
        weight_ref[i * count : (i + 1) * count, :] = lax.dot_general(
            chosen, part, (((1,), (1,)), ((), ())), preferred_element_type=F32
        ).astype(BF16)
    rhs_ref[...] = jnp.dot(chosen, source_ref[...], preferred_element_type=F32)
    rows = lax.broadcasted_iota(jnp.int32, act_ref.shape[1:], 0)
    length = jnp.zeros(act_ref.shape[1:], jnp.int32)
    for l in range(lines):
        length = jnp.where(rows == l, len_ref[l], length)
    place = lax.axis_index("wall") * depth
    for g in range(depth):
        act_ref[g] = (place + g < length).astype(F32)


def residual_kernel(before, state, after, weight, source, lift, rhs_ref):
    cells = jnp.concatenate([before[...], state[...], after[...]], axis=0)
    parts = jnp.dot(weight[...], cells, preferred_element_type=F32)
    count = source.shape[0]
    face_sum = parts[:count] + (parts[count : 2 * count] + parts[2 * count :])
    flux = jnp.dot(face_sum.astype(BF16), lift[...], preferred_element_type=F32)
    rhs = source[...] - flux
    depth, lines, _ = rhs_ref.shape
    for g in range(depth):
        rhs_ref[g] = rhs[g * lines : (g + 1) * lines]


def forward_local(scaled, q_ref, act_ref, carried):
    values = []
    for g, value in enumerate(scaled):
        if carried is not None:
            value = value - apply_pairs(carried, q_ref, g)
        carried = act_ref[g] * value
        values.append(carried)
    return values


def backward_local(values, s_ref, act_ref, carried):
    solved = [None] * len(values)
    for g in range(len(values) - 1, -1, -1):
        value = values[g]
        if carried is not None:
            value = value - apply_pairs(carried, s_ref, g)
        carried = act_ref[g] * value
        solved[g] = carried
    return solved


def local_kernel(rhs_ref, raw_ref, act_ref, scaled_ref, y_ref, leave_ref):
    depth = rhs_ref.shape[0]
    scaled = [apply_rows(rhs_ref[g], raw_ref, 0, g) for g in range(depth)]
    values = raw_steps(scaled, raw_ref, act_ref, None)
    for g in range(depth):
        scaled_ref[g] = scaled[g]
        y_ref[g] = values[g]
    leave_ref[...] = values[-1]


def raw_steps(scaled, raw_ref, act_ref, carried):
    values = []
    for g, value in enumerate(scaled):
        if carried is not None:
            value = value - apply_rows(apply_rows(carried, raw_ref, 1, g), raw_ref, 0, g)
        carried = act_ref[g] * value
        values.append(carried)
    return values


def wall_kernel(came_ref, scaled_ref, raw_ref, act_ref, y_ref, out_ref, leave_ref):
    depth = y_ref.shape[0]
    out_ref[...] = y_ref[...]
    leave_ref[...] = y_ref[depth - 1]

    @pl.when(lax.axis_index("wall") == 1)
    def _():
        values = raw_steps([scaled_ref[g] for g in range(depth)], raw_ref, act_ref, came_ref[...])
        for g in range(depth):
            out_ref[g] = values[g]
        leave_ref[...] = values[-1]


def chip_local_kernel(came_ref, act_ref, y_ref, *refs):
    own_refs, out_ref = refs[:-1], refs[-1]
    depth = y_ref.shape[0]
    out_ref[...] = y_ref[depth - 1]

    @pl.when(jnp.logical_and(core_of() == 1, chip_of() > 0))
    def _():
        out_ref[...] = act_ref[depth - 1] * apply_pairs(came_ref[...], own_refs) + y_ref[depth - 1]


def hop_kernel(came_ref, act_ref, local_ref, *refs, chip):
    pair_refs, out_ref = refs[:-1], refs[-1]
    out_ref[...] = local_ref[...]

    @pl.when(jnp.logical_and(chip_of() == chip, core_of() == 1))
    def _():
        gone = apply_pairs(came_ref[...], pair_refs)
        out_ref[...] = act_ref[act_ref.shape[0] - 1] * gone + local_ref[...]


def chosen_arrival(refs, chips, like):
    here = chip_of()
    value = jnp.zeros(like, F32)
    for ref, chip in zip(refs, chips):
        value = jnp.where(here == chip, ref[...], value)
    return value


def choose_kernel(*refs, chips):
    refs[-1][...] = chosen_arrival(refs[:-1], chips, refs[-1].shape)


def inner_kernel(
    direct_ref, met_ref, came_ref, scaled_ref, q_ref, s_ref, act_ref, wall_ref, *refs, on_last, last, parts
):
    got_refs = refs[:parts]
    y_ref, first_ref, flow = refs[-3:]
    depth = scaled_ref.shape[0]
    here = chip_of()

    @pl.when(here == last if on_last else jnp.logical_and(here > 0, here != last))
    def _():
        flow[...] = met_ref[...]

        @pl.when(core_of() == 1)
        def _():
            flow[...] = apply_pairs(direct_ref[...], got_refs) + came_ref[...]

        values = forward_local([scaled_ref[g] for g in range(depth)], q_ref, act_ref, flow[...])
        for g in range(depth):
            y_ref[g] = values[g]

    if not on_last:

        @pl.when(here == 0)
        def _():
            y_ref[...] = wall_ref[...]

    @pl.when(here == last if on_last else here != last)
    def _():
        first_ref[...] = backward_local([y_ref[g] for g in range(depth)], s_ref, act_ref, None)[0]


def reach_kernel(first_ref, got_ref, out_ref):
    @pl.when(core_of() == 1)
    def _():
        out_ref[...] = apply_pairs(first_ref[...], got_ref)


def add_kernel(x_ref, y_ref, out_ref):
    out_ref[...] = x_ref[...] + y_ref[...]


def leave_kernel(own_ref, first_ref, *refs, chips):
    came_ref, out_ref = refs[-2:]
    came_ref[...] = chosen_arrival(refs[:-2], chips, came_ref.shape)
    out_ref[...] = first_ref[...]

    @pl.when(core_of() == 1)
    def _():
        out_ref[...] = apply_pairs(came_ref[...], own_ref) + first_ref[...]


def last_kernel(beyond_ref, met_ref, s_ref, act_ref, y_ref, out_ref):
    depth = y_ref.shape[0]
    carried = jnp.where(core_of() == 0, met_ref[...], beyond_ref[...])
    solved = backward_local([y_ref[g] for g in range(depth)], s_ref, act_ref, carried)
    for g in range(depth):
        out_ref[g] = solved[g]


def padded_bytes(shape, dtype):
    size = jnp.dtype(dtype).itemsize
    shape = (1,) * (2 - len(shape)) + tuple(shape)
    total = -(-shape[-2] // 16) * 16 * -(-shape[-1] // 128) * 128 * size
    for extent in shape[:-2]:
        total *= extent
    return total


def run(kernel, operands, outs, blocks=1, scratch=(), aliases=None):
    held = [(x.shape, x.dtype) for x, _ in operands] + [(s, t) for s, t, _ in outs]
    limit = sum(padded_bytes(s, t) for s, t in held)
    if blocks == 1:
        in_specs = [at if isinstance(at, pl.BlockSpec) else VMEM for _, at in operands]
        out_specs = [VMEM for _ in outs]
        grid = ()
    else:

        def spec(shape, at):
            if isinstance(at, pl.BlockSpec):
                return at
            if at is None:
                return pl.BlockSpec(shape, lambda i: (0,) * len(shape))
            size = tuple(n // blocks if axis == at else n for axis, n in enumerate(shape))
            return pl.BlockSpec(size, lambda i: tuple(i if axis == at else 0 for axis in range(len(shape))))

        in_specs = [spec(x.shape, at) for x, at in operands]
        out_specs = [spec(s, at) for s, _, at in outs]
        grid = (blocks,)
        limit = 2 * limit // blocks
    limit += sum(padded_bytes(s.shape, s.dtype) for s in scratch if s.memory_space == pltpu.VMEM)
    limit = min(limit + (2 << 20), 60 << 20)
    return pl.pallas_call(
        kernel,
        grid=grid,
        in_specs=in_specs,
        out_specs=out_specs,
        out_shape=[jax.ShapeDtypeStruct(s, t) for s, t, _ in outs],
        scratch_shapes=list(scratch),
        input_output_aliases=aliases or {},
        compiler_params=pltpu.CompilerParams(vmem_limit_bytes=limit),
        cost_estimate=pl.CostEstimate(flops=1, bytes_accessed=1, transcendentals=0),
    )(*[x for x, _ in operands])


def hop_pairs(count, start, end, core=1):
    start, end = 2 * start + 1, 2 * end + core
    target = {i: i ^ 1 for i in range(count)}
    target.update({start: end, end: end ^ 1, end ^ 1: start ^ 1, start ^ 1: start})
    return sorted(target.items())


def in_hbm(value):
    return pltpu.with_memory_space_constraint(value, pltpu.HBM)


def after(value, *others):
    return lax.optimization_barrier((value, *others))[0]


def per_device(state, source, face_coef, neighbour, lift, elem_slot, line_len, dinv, lower, upper):
    wall_count = lax.axis_size("wall")
    surf_count = lax.axis_size("surf")
    last = wall_count // 2 - 1
    depth, lines, width, _ = dinv.shape
    slots = state.shape[0]
    block = TILE if lines % TILE == 0 else lines
    blocks = lines // block
    parts = 2 if blocks == 1 and lines % 2 == 0 else 1
    room, columns, _ = room_of(width)
    line_vector = ((lines, width), F32, 0)
    element_vectors = ((depth, lines, width), F32, 1)
    line_sent = ((lines * room, columns), BF16, 0)
    line_pairs = ((lines, 2, width, width), BF16, 0)
    part_sent = ((lines // parts * room, columns), BF16, 0)
    part_pairs = ((lines // parts, 2, width, width), BF16, 0)
    element_pairs = ((depth, lines, 2, width, width), BF16, 1)

    def mates(value):
        return lax.ppermute(value, "wall", [(i, i ^ 1) for i in range(wall_count)])

    def relaid(arrays, *others):
        if lines != TILE:
            return jnp.stack(arrays)
        shape = (len(arrays), depth, lines, width, width)
        return run(
            functools.partial(relayout_kernel, kinds=len(arrays)),
            [(in_hbm(jnp.transpose(x, (0, 2, 1, 3))), ANY) for x in arrays] + [(x, None) for x in others],
            [(shape, BF16, None)],
            scratch=[
                pltpu.VMEM((len(arrays), depth, width, lines, width), BF16),
                pltpu.SemaphoreType.DMA((len(arrays), depth)),
            ],
        )[0]

    count = depth * lines
    small = (elem_slot, line_len, face_coef.T, neighbour.T, source)
    weight, line_source, act, near_state, near_lift = run(
        prepare_kernel,
        [(in_hbm(x), ANY) for x in (*small, state, lift)],
        [
            ((3 * count, 3 * slots), BF16, None),
            ((count, width), F32, None),
            element_vectors,
            (state.shape, BF16, None),
            (lift.shape, BF16, None),
        ],
        scratch=[(pltpu.SMEM if i < 2 else pltpu.VMEM)(x.shape, x.dtype) for i, x in enumerate(small)]
        + [pltpu.SemaphoreType.DMA((len(small) + 2,))],
    )
    before = lax.ppermute(state, "surf", [(i, (i + 1) % surf_count) for i in range(surf_count)])
    beyond = lax.ppermute(state, "surf", [((i + 1) % surf_count, i) for i in range(surf_count)])
    (rhs,) = run(
        residual_kernel,
        [(x, None) for x in (before, near_state, beyond, weight, line_source, near_lift)],
        [element_vectors],
    )
    blocks_in = (dinv, lower, upper)
    if lines == TILE:
        (raw,) = run(
            functools.partial(relayout_kernel, kinds=3),
            [(in_hbm(jnp.transpose(x, (0, 2, 1, 3))), ANY) for x in blocks_in]
            + [(x, None) for x in (before, beyond, weight)],
            [((3, depth, lines, width, width), BF16, None)],
            scratch=[
                pltpu.VMEM((3, depth, width, lines, width), BF16),
                pltpu.SemaphoreType.DMA((3, depth)),
            ],
        )
    else:
        raw = jnp.stack(blocks_in)
    scaled, y_local, y_leave = run(
        local_kernel,
        [(rhs, 1), (raw, 2), (act, 1)],
        [element_vectors, element_vectors, line_vector],
        blocks,
    )
    came_y = mates(y_leave)
    wall_y, wall_leave = run(
        wall_kernel,
        [(came_y, 0), (scaled, 1), (raw, 2), (act, 1), (y_local, 1)],
        [element_vectors, line_vector],
        blocks,
    )
    arrivals = [lax.ppermute(wall_leave, "wall", hop_pairs(wall_count, 0, 1))]
    a, got_a, q = [], [], None
    for part in range(parts):
        each = block // parts
        q, whole, sent = run(
            functools.partial(
                pair_kernel, first_chip=1, kind=1, lines=(part * each, part * each + each), ascending=True
            ),
            [(after(raw, wall_leave if part else y_leave), 2)] + ([] if q is None else [(q, ANY)]),
            [element_pairs, part_pairs, part_sent],
            blocks,
            aliases={} if q is None else {1: 0},
        )
        a.append(whole)
        got_a.append(mates(after(sent, got_a[-1] if part else came_y)))
    s, c, sent_c = run(
        functools.partial(pair_kernel, first_chip=0, kind=2, lines=(0, block), ascending=False),
        [(after(raw, a[-1], wall_leave), 2)],
        [element_pairs, line_pairs, line_sent],
        blocks,
    )
    got_c = mates(after(sent_c, arrivals[0],got_a[-1]))

    def hop(came, pairs, local, at):
        (out,) = run(
            functools.partial(hop_kernel, chip=at),
            [(came, 0), (act, 1), (local, 0)] + [(x, 0) for x in pairs],
            [line_vector],
            blocks,
        )
        return out

    out = wall_leave
    for at in range(1, last):
        if at == 1:
            (out,) = run(
                functools.partial(early_hop_kernel, chip=at, parts=parts),
                [(arrivals[-1], 0), (act, 1), (came_y, 0), (y_local, 1)] + [(x, 0) for x in got_a + a],
                [line_vector],
                blocks,
            )
            (chip_a,) = run(
                functools.partial(chip_kernel, parts=parts, width=width, own_first=False),
                [(after(x, out) if i == 0 else x, 0) for i, x in enumerate(got_a + a)],
                [line_pairs],
                blocks,
            )
            (y_chip,) = run(
                chip_local_kernel,
                [(after(came_y, out), 0), (act, 1), (y_local, 1)] + [(x, 0) for x in a],
                [line_vector],
                blocks,
            )
        else:
            out = hop(arrivals[-1], [chip_a], y_chip, at)
        arrivals.append(lax.ppermute(out, "wall", hop_pairs(wall_count, at, at + 1)))
    direct = lax.ppermute(out, "wall", hop_pairs(wall_count, last - 1, last, 0))

    def inner(on_last, entered, met, held=()):
        return run(
            functools.partial(inner_kernel, on_last=on_last, last=last, parts=parts),
            [(entered, 0), (met, 0), (came_y, 0)]
            + [(x, 1) for x in (scaled, q, s, act, wall_y)]
            + [(x, 0) for x in got_a]
            + [(x, ANY) for x in held],
            [element_vectors, line_vector],
            blocks,
            [pltpu.VMEM((block, width), F32)],
            {8 + parts: 0, 9 + parts: 1} if held else {},
        )

    def chosen(arrived, chips):
        return run(
            functools.partial(choose_kernel, chips=chips), [(x, 0) for x in arrived], [line_vector], blocks
        )[0]

    chips = list(range(1, last))
    entered = chosen(arrivals[:-1], chips)
    held = inner(False, after(entered, out), mates(entered))
    y, first = inner(True, arrivals[-1], direct, held)
    came_first = mates(first)
    (reach,) = run(reach_kernel, [(first, 0), (got_c, 0)], [line_vector], blocks)
    (x_chip,) = run(add_kernel, [(reach, 0), (came_first, 0)], [line_vector], blocks)
    arrived = [lax.ppermute(x_chip, "wall", hop_pairs(wall_count, last, last - 1))]
    (chip_c,) = run(
        functools.partial(chip_kernel, parts=1, width=width, own_first=True),
        [(after(got_c, x_chip), 0), (c, 0)],
        [line_pairs],
        blocks,
    )
    for at in range(last - 1, 0, -1):
        out = hop(arrived[-1], [chip_c], x_chip, at)
        arrived.append(lax.ppermute(out, "wall", hop_pairs(wall_count, at, at - 1)))
    beyond, left = run(
        functools.partial(leave_kernel, chips=list(range(last - 1, -1, -1))),
        [(x, 0) for x in (c, first, *arrived)],
        [line_vector, line_vector],
        blocks,
    )
    met_left = mates(left)
    (solution,) = run(
        last_kernel, [(beyond, 0), (met_left, 0)] + [(x, 1) for x in (s, act, y)], [element_vectors], blocks
    )
    return solution


def solution(mesh):
    in_specs = (
        P(("wall", "surf"), None),
        P(("wall", "surf"), None),
        P(("wall", "surf"), None),
        P(("wall", "surf"), None),
        P(),
        P("wall", "surf"),
        P("surf"),
        P("wall", "surf", None, None),
        P("wall", "surf", None, None),
        P("wall", "surf", None, None),
    )
    out_specs = P("wall", "surf", None)
    return jax.shard_map(
        per_device, mesh=mesh, in_specs=in_specs, out_specs=out_specs, check_vma=False
    )
```

```python
import functools

import jax
import jax.numpy as jnp
from jax import lax
from jax.experimental import pallas as pl
from jax.experimental.pallas import tpu as pltpu
from jax.sharding import PartitionSpec as P

F32 = jnp.float32
BF16 = jnp.bfloat16
TILE = 8
LANES = 128
VMEM = pl.BlockSpec(memory_space=pltpu.VMEM)
ANY = pl.BlockSpec(memory_space=pl.ANY)
SMEM = pl.BlockSpec(memory_space=pltpu.SMEM)


def split2(x):
    high = x.astype(BF16)
    return high, (x - high.astype(F32)).astype(BF16)


def product(x, y):
    dot = functools.partial(jnp.dot, preferred_element_type=F32)
    return dot(x[0], y[0]) + (dot(x[0], y[1]) + dot(x[1], y[0]))


def room_of(width):
    rows = -(-width // (2 * TILE)) * 2 * TILE
    main = width // LANES * LANES
    return rows, 2 * main + (LANES if width - main <= LANES // 2 else 2 * LANES), main


def pair_at(ref, width, *at):
    if len(ref.shape) > 2:
        return [ref[(*at, i)] for i in range(2)]
    rows, columns, main = room_of(width)
    here = pl.ds(at[0] * rows, width)
    step = (columns - 2 * main) // 2
    if width == main:
        return [ref[here, i * main : (i + 1) * main] for i in range(2)]
    return [
        jnp.concatenate(
            [
                ref[here, i * main : (i + 1) * main],
                ref[here, 2 * main + i * step : 2 * main + i * step + width - main],
            ],
            axis=1,
        )
        for i in range(2)
    ]


def store_pair(ref, pair, *at):
    if len(ref.shape) > 2:
        for i in range(2):
            ref[(*at, i)] = pair[i]
        return
    width = pair[0].shape[0]
    rows, columns, main = room_of(width)
    here = pl.ds(at[0] * rows, width)
    step = (columns - 2 * main) // 2
    for i in range(2):
        ref[here, i * main : (i + 1) * main] = pair[i][:, :main]
        if width > main:
            ref[here, 2 * main + i * step : 2 * main + i * step + width - main] = pair[i][:, main:]


def apply_pairs(vector, ref, *at):
    count = vector.shape[0]
    rows = lax.broadcasted_iota(jnp.int32, vector.shape, 0)
    both = jnp.concatenate(split2(vector), axis=0)
    total = jnp.zeros(vector.shape, F32)
    for l in range(count):
        part, here = ref, l
        if isinstance(ref, (list, tuple)):
            each = count // len(ref)
            part, here = ref[l // each], l % each
        high, low = pair_at(part, vector.shape[1], *at, here)
        first = jnp.dot(both, high, preferred_element_type=F32)
        second = jnp.dot(both, low, preferred_element_type=F32)
        total = jnp.where(rows == l, first[:count] + first[count:] + second[:count], total)
    return total


def apply_rows(vector, ref, *at):
    count = vector.shape[0]
    rows = lax.broadcasted_iota(jnp.int32, vector.shape, 0)
    both = jnp.concatenate(split2(vector), axis=0)
    total = jnp.zeros(vector.shape, F32)
    for l in range(count):
        first = lax.dot_general(
            both, ref[(*at, l)], (((1,), (1,)), ((), ())), preferred_element_type=F32
        )
        total = jnp.where(rows == l, first[:count] + first[count:], total)
    return total


def core_of():
    return lax.rem(lax.axis_index("wall"), 2)


def chip_of():
    return lax.div(lax.axis_index("wall"), 2)


def pair_kernel(raw_ref, *refs, first_chip, fetch, turn, **options):
    if fetch:
        next_ref, landed, arrived = refs[0], refs[4], refs[-1]
        copies = [
            pltpu.make_async_copy(next_ref.at[e], landed.at[0, e], arrived.at[e]) for e in range(next_ref.shape[0])
        ]
        for copy in copies:
            copy.start()
        refs = refs[1:4]
    other_ref = raw_ref
    if turn:
        other_ref = refs[-1]
        for e in range(raw_ref.shape[1]):
            turn_blocks(refs[0], 0, e, other_ref)
        refs = refs[1:4]

    @pl.when(chip_of() >= first_chip)
    def _():
        make_pairs(raw_ref, other_ref, *refs[-3:], **options)

    if fetch:
        for copy in copies:
            copy.wait()


def make_pairs(raw_ref, other_ref, step_ref, whole_ref, sent_ref, *, kind, lines, ascending):
    count = raw_ref.shape[1]
    for l in range(*lines):
        steps = []
        for e in range(count):
            block = lax.dot_general(
                other_ref[kind, e, l], raw_ref[0, e, l], (((0,), (1,)), ((), ())), preferred_element_type=F32
            )
            steps.append(split2(block))
            store_pair(step_ref, steps[-1], e, l)
        if not ascending:
            steps = steps[::-1]
        whole = steps[0]
        for step in steps[1:]:
            whole = split2(product(whole, step))
        if count % 2:
            whole = [-x for x in whole]
        store_pair(whole_ref, whole, l - lines[0])
        store_pair(sent_ref, whole, l - lines[0])


def chip_kernel(*refs, parts, width, own_first):
    got_refs, own_refs, chip_ref = refs[:parts], refs[parts:-1], refs[-1]

    @pl.when(core_of() == 1)
    def _():
        each = chip_ref.shape[0] // parts
        for l in range(chip_ref.shape[0]):
            pairs = [pair_at(x[l // each], width, l % each) for x in (got_refs, own_refs)]
            store_pair(chip_ref, split2(product(*(pairs[::-1] if own_first else pairs))), l)


def turn_blocks(landed_ref, a, e, raw_ref):
    turned = jnp.swapaxes(landed_ref[a, e], 0, 1)
    for l in range(raw_ref.shape[2]):
        raw_ref[a, e, l] = turned[l]


def relayout_kernel(*refs, kinds):
    raw_ref, landed, arrived = refs[-3:]
    depth = raw_ref.shape[1]
    copies = [
        pltpu.make_async_copy(ref.at[e], landed.at[a, e], arrived.at[a, e])
        for a, ref in enumerate(refs[:kinds])
        for e in range(depth)
    ]
    for copy in copies:
        copy.start()
    for i, copy in enumerate(copies):
        copy.wait()
        turn_blocks(landed, *divmod(i, depth), raw_ref)


def prepare_kernel(*refs):
    places, (weight_ref, rhs_ref, act_ref, state_ref, lift_ref) = refs[:7], refs[7:12]
    slot_ref, len_ref, coef_ref, nb_ref, source_ref, arrived = refs[12:]
    targets = (slot_ref, len_ref, coef_ref, nb_ref, source_ref, state_ref, lift_ref)
    copies = [
        pltpu.make_async_copy(there, here, arrived.at[i]) for i, (there, here) in enumerate(zip(places, targets))
    ]
    for copy in copies:
        copy.start()
    for copy in copies:
        copy.wait()
    faces, slots = coef_ref.shape
    depth, lines = slot_ref.shape
    cells = 3 * slots
    k = lax.broadcasted_iota(jnp.int32, (cells, slots), 0)
    e = lax.broadcasted_iota(jnp.int32, (cells, slots), 1)
    weight = jnp.zeros((cells, slots), F32)
    own = jnp.zeros((1, slots), F32)
    for f in range(faces):
        coef = coef_ref[f : f + 1, :]
        own = own + coef
        weight = weight - jnp.where(k == nb_ref[f : f + 1, :], coef, 0.0)
    weight = weight + jnp.where(k == e + slots, own, 0.0)
    count = depth * lines
    rows = lax.broadcasted_iota(jnp.int32, (count, slots), 0)
    slot = jnp.zeros((count, slots), jnp.int32)
    for g in range(depth):
        for l in range(lines):
            slot = jnp.where(rows == g * lines + l, slot_ref[g, l], slot)
    chosen = (slot == lax.broadcasted_iota(jnp.int32, (count, slots), 1)).astype(F32).astype(BF16)
    high = weight.astype(BF16)
    mid, low = split2(weight - high.astype(F32))
    for i, part in enumerate((high, mid, low)):
        weight_ref[i * count : (i + 1) * count, :] = lax.dot_general(
            chosen, part, (((1,), (1,)), ((), ())), preferred_element_type=F32
        ).astype(BF16)
    rhs_ref[...] = jnp.dot(chosen, source_ref[...], preferred_element_type=F32)
    rows = lax.broadcasted_iota(jnp.int32, act_ref.shape[1:], 0)
    length = jnp.zeros(act_ref.shape[1:], jnp.int32)
    for l in range(lines):
        length = jnp.where(rows == l, len_ref[l], length)
    place = lax.axis_index("wall") * depth
    for g in range(depth):
        act_ref[g] = (place + g < length).astype(F32)


def residual_kernel(before, state, after, weight, source, lift, rhs_ref):
    cells = jnp.concatenate([before[...], state[...], after[...]], axis=0)
    parts = jnp.dot(weight[...], cells, preferred_element_type=F32)
    count = source.shape[0]
    face_sum = parts[:count] + (parts[count : 2 * count] + parts[2 * count :])
    flux = jnp.dot(face_sum.astype(BF16), lift[...], preferred_element_type=F32)
    rhs = source[...] - flux
    depth, lines, _ = rhs_ref.shape
    for g in range(depth):
        rhs_ref[g] = rhs[g * lines : (g + 1) * lines]


def forward_local(scaled, q_ref, act_ref, carried):
    values = []
    for g, value in enumerate(scaled):
        if carried is not None:
            value = value - apply_pairs(carried, q_ref, g)
        carried = act_ref[g] * value
        values.append(carried)
    return values


def backward_local(values, s_ref, act_ref, carried):
    solved = [None] * len(values)
    for g in range(len(values) - 1, -1, -1):
        value = values[g]
        if carried is not None:
            value = value - apply_pairs(carried, s_ref, g)
        carried = act_ref[g] * value
        solved[g] = carried
    return solved


def local_kernel(rhs_ref, raw_ref, act_ref, scaled_ref, y_ref, leave_ref):
    depth = rhs_ref.shape[0]
    scaled = [apply_rows(rhs_ref[g], raw_ref, 0, g) for g in range(depth)]
    values = raw_steps(scaled, raw_ref, act_ref, None)
    for g in range(depth):
        scaled_ref[g] = scaled[g]
        y_ref[g] = values[g]
    leave_ref[...] = values[-1]


def raw_steps(scaled, raw_ref, act_ref, carried):
    values = []
    for g, value in enumerate(scaled):
        if carried is not None:
            value = value - apply_rows(apply_rows(carried, raw_ref, 1, g), raw_ref, 0, g)
        carried = act_ref[g] * value
        values.append(carried)
    return values


def wall_kernel(came_ref, scaled_ref, raw_ref, act_ref, y_ref, out_ref, leave_ref):
    depth = y_ref.shape[0]
    out_ref[...] = y_ref[...]
    leave_ref[...] = y_ref[depth - 1]

    @pl.when(lax.axis_index("wall") == 1)
    def _():
        values = raw_steps([scaled_ref[g] for g in range(depth)], raw_ref, act_ref, came_ref[...])
        for g in range(depth):
            out_ref[g] = values[g]
        leave_ref[...] = values[-1]


def chip_local_kernel(came_ref, act_ref, y_ref, *refs):
    own_refs, out_ref = refs[:-1], refs[-1]
    depth = y_ref.shape[0]
    out_ref[...] = y_ref[depth - 1]

    @pl.when(jnp.logical_and(core_of() == 1, chip_of() > 0))
    def _():
        out_ref[...] = act_ref[depth - 1] * apply_pairs(came_ref[...], own_refs) + y_ref[depth - 1]


def three_terms(x):
    high = x.astype(BF16)
    return high, *split2(x - high.astype(F32))


def through_kernel(act_ref, q_ref, s_ref, y_ref, *refs, parts):
    whole_refs, (out_ref, sent_ref, echo_ref) = refs[:parts], refs[parts:]
    depth, lines, _, _, width = q_ref.shape
    main, below = width // LANES * LANES, lines * room_of(width)[0]
    echo = backward_local([y_ref[g] for g in range(depth)], s_ref, act_ref, None)[0]
    echo_ref[...] = echo
    for i, term in enumerate(three_terms(echo)):
        sent_ref[below + 2 * TILE * i : below + 2 * TILE * i + lines, :main] = term[:, :main]
        if width > main:
            sent_ref[below + 2 * TILE * i : below + 2 * TILE * i + lines, main:width] = term[:, main:]

    @pl.when(chip_of() > 0)
    def _():
        for l in range(lines):
            active = [act_ref[g, l : l + 1, :] for g in range(depth)]
            steps = [[-x for x in pair_at(q_ref, width, 0, l)]]
            for g in range(1, depth - 1):
                steps.append(split2(-product(steps[-1], pair_at(q_ref, width, g, l))))
            each = lines // parts
            high, low = pair_at(whole_refs[l // each], width, l % each)
            value = active[depth - 1] * (high.astype(F32) + low.astype(F32))
            for g in range(depth - 2, -1, -1):
                reach = steps[g][0].astype(F32) + steps[g][1].astype(F32)
                value = active[g] * (reach - product(split2(value), pair_at(s_ref, width, g, l)))
            pair = split2(value)
            store_pair(out_ref, pair, l)
            store_pair(sent_ref, pair, l)


def hop_kernel(came_ref, act_ref, local_ref, idle_ref, *refs, chip):
    pair_refs, out_ref = refs[:-1], refs[-1]
    out_ref[...] = idle_ref[...]

    @pl.when(jnp.logical_and(chip_of() == chip, core_of() == 1))
    def _():
        gone = apply_pairs(came_ref[...], pair_refs)
        out_ref[...] = act_ref[act_ref.shape[0] - 1] * gone + local_ref[...]


def early_hop_kernel(came_ref, act_ref, mate_ref, y_ref, *refs, chip, parts):
    got_refs, own_refs, out_ref = refs[:parts], refs[parts : 2 * parts], refs[-1]
    depth = y_ref.shape[0]
    out_ref[...] = came_ref[...]

    @pl.when(jnp.logical_and(chip_of() == chip, core_of() == 1))
    def _():
        middle = apply_pairs(came_ref[...], got_refs) + mate_ref[...]
        out_ref[...] = act_ref[depth - 1] * apply_pairs(middle, own_refs) + y_ref[depth - 1]


def chosen_arrival(refs, chips, like):
    here = chip_of()
    value = jnp.zeros(like, F32)
    for ref, chip in zip(refs, chips):
        value = jnp.where(here == chip, ref[...], value)
    return value


def choose_kernel(*refs, chips):
    refs[-1][...] = chosen_arrival(refs[:-1], chips, refs[-1].shape)


def turn_kernel(enter_ref, came_ref, echo_ref, got_c, got_d, own_d, *refs, parts, chips, fill):
    got_refs, (enter_y, mid_ref, out_ref) = refs[:parts], refs[-3:]
    inside = jnp.logical_and(chip_of() >= chips[0], chip_of() < chips[1])
    if fill:

        @pl.when(jnp.logical_not(inside))
        def _():
            enter_y[...] = enter_ref[...]
            mid_ref[...] = echo_ref[...]
            out_ref[...] = echo_ref[...]

    @pl.when(jnp.logical_and(inside, core_of() == 1))
    def _():
        enter = enter_ref[...]
        leave = apply_pairs(enter, got_refs) + came_ref[...]
        middle = apply_pairs(leave, own_d) + echo_ref[...]
        lines, width = enter.shape
        below = lines * room_of(width)[0]
        first = apply_pairs(enter, got_d)
        for i in range(3):
            first = first + got_d[below + 2 * TILE * i : below + 2 * TILE * i + lines, :width].astype(F32)
        enter_y[...] = leave
        mid_ref[...] = middle
        out_ref[...] = apply_pairs(middle, got_c) + first


def send_kernel(x_ref, enter_ref, out_ref, *, last):
    out_ref[...] = jnp.where(chip_of() == last, x_ref[...], enter_ref[...])


def steps_kernel(flow_ref, scaled_ref, q_ref, act_ref, wall_ref, *refs, late):
    y_ref = refs[-1]
    depth = scaled_ref.shape[0]
    here, core = chip_of(), core_of()
    if late:
        inside = jnp.logical_and(core == 0, here > 1)
    else:
        inside = jnp.logical_and(here > 0, jnp.logical_or(core == 1, here == 1))

        @pl.when(here == 0)
        def _():
            y_ref[...] = wall_ref[...]

    @pl.when(inside)
    def _():
        values = forward_local([scaled_ref[g] for g in range(depth)], q_ref, act_ref, flow_ref[...])
        for g in range(depth):
            y_ref[g] = values[g]


def entry_kernel(own_ref, came_ref, out_ref):
    out_ref[...] = jnp.where(core_of() == 1, own_ref[...], came_ref[...])


def leave_kernel(own_ref, first_ref, *refs, chips):
    came_ref, out_ref = refs[-2:]
    came_ref[...] = chosen_arrival(refs[:-2], chips, came_ref.shape)
    out_ref[...] = first_ref[...]

    @pl.when(core_of() == 1)
    def _():
        out_ref[...] = apply_pairs(came_ref[...], own_ref) + first_ref[...]


def last_kernel(beyond_ref, met_ref, s_ref, act_ref, y_ref, out_ref):
    depth = y_ref.shape[0]
    carried = jnp.where(core_of() == 0, met_ref[...], beyond_ref[...])
    solved = backward_local([y_ref[g] for g in range(depth)], s_ref, act_ref, carried)
    for g in range(depth):
        out_ref[g] = solved[g]


def padded_bytes(shape, dtype):
    size = jnp.dtype(dtype).itemsize
    shape = (1,) * (2 - len(shape)) + tuple(shape)
    total = -(-shape[-2] // 16) * 16 * -(-shape[-1] // 128) * 128 * size
    for extent in shape[:-2]:
        total *= extent
    return total


def run(kernel, operands, outs, blocks=1, scratch=(), aliases=None):
    held = [(x.shape, x.dtype) for x, _ in operands] + [(s, t) for s, t, _ in outs]
    limit = sum(padded_bytes(s, t) for s, t in held)
    if blocks == 1:
        in_specs = [at if isinstance(at, pl.BlockSpec) else VMEM for _, at in operands]
        out_specs = [VMEM for _ in outs]
        grid = ()
    else:

        def spec(shape, at):
            if isinstance(at, pl.BlockSpec):
                return at
            if at is None:
                return pl.BlockSpec(shape, lambda i: (0,) * len(shape))
            size = tuple(n // blocks if axis == at else n for axis, n in enumerate(shape))
            return pl.BlockSpec(size, lambda i: tuple(i if axis == at else 0 for axis in range(len(shape))))

        in_specs = [spec(x.shape, at) for x, at in operands]
        out_specs = [spec(s, at) for s, _, at in outs]
        grid = (blocks,)
        limit = 2 * limit // blocks
    limit += sum(padded_bytes(s.shape, s.dtype) for s in scratch if s.memory_space == pltpu.VMEM)
    limit = min(limit + (2 << 20), 60 << 20)
    return pl.pallas_call(
        kernel,
        grid=grid,
        in_specs=in_specs,
        out_specs=out_specs,
        out_shape=[jax.ShapeDtypeStruct(s, t) for s, t, _ in outs],
        scratch_shapes=list(scratch),
        input_output_aliases=aliases or {},
        compiler_params=pltpu.CompilerParams(vmem_limit_bytes=limit),
        cost_estimate=pl.CostEstimate(flops=1, bytes_accessed=1, transcendentals=0),
    )(*[x for x, _ in operands])


def hop_pairs(count, start, end):
    start, end = 2 * start + 1, 2 * end + 1
    target = {i: i ^ 1 for i in range(count)}
    target.update({start: end, end: end ^ 1, end ^ 1: start ^ 1, start ^ 1: start})
    return sorted(target.items())


def in_hbm(value):
    return pltpu.with_memory_space_constraint(value, pltpu.HBM)


def after(value, *others):
    return lax.optimization_barrier((value, *others))[0]


def per_device(state, source, face_coef, neighbour, lift, elem_slot, line_len, dinv, lower, upper):
    wall_count = lax.axis_size("wall")
    surf_count = lax.axis_size("surf")
    last = wall_count // 2 - 1
    depth, lines, width, _ = dinv.shape
    slots = state.shape[0]
    block = TILE if lines % TILE == 0 else lines
    blocks = lines // block
    parts = 1
    room, columns, _ = room_of(width)
    line_vector = ((lines, width), F32, 0)
    element_vectors = ((depth, lines, width), F32, 1)
    line_sent = ((lines * room, columns), BF16, 0)
    vector_sent = ((lines * room + 6 * TILE * blocks, columns), BF16, 0)
    line_pairs = ((lines, 2, width, width), BF16, 0)
    part_sent = ((lines // parts * room, columns), BF16, 0)
    part_pairs = ((lines // parts, 2, width, width), BF16, 0)
    element_pairs = ((depth, lines, 2, width, width), BF16, 1)

    def mates(value):
        return lax.ppermute(value, "wall", [(i, i ^ 1) for i in range(wall_count)])

    def relaid(arrays, *others):
        if lines != TILE:
            return jnp.stack(arrays)
        shape = (len(arrays), depth, lines, width, width)
        return run(
            functools.partial(relayout_kernel, kinds=len(arrays)),
            [(in_hbm(jnp.transpose(x, (0, 2, 1, 3))), ANY) for x in arrays] + [(x, None) for x in others],
            [(shape, BF16, None)],
            scratch=[
                pltpu.VMEM((len(arrays), depth, width, lines, width), BF16),
                pltpu.SemaphoreType.DMA((len(arrays), depth)),
            ],
        )[0]

    count = depth * lines
    small = (elem_slot, line_len, face_coef.T, neighbour.T, source)
    weight, line_source, act, near_state, near_lift = run(
        prepare_kernel,
        [(in_hbm(x), ANY) for x in (*small, state, lift)],
        [
            ((3 * count, 3 * slots), BF16, None),
            ((count, width), F32, None),
            element_vectors,
            (state.shape, BF16, None),
            (lift.shape, BF16, None),
        ],
        scratch=[(pltpu.SMEM if i < 2 else pltpu.VMEM)(x.shape, x.dtype) for i, x in enumerate(small)]
        + [pltpu.SemaphoreType.DMA((len(small) + 2,))],
    )
    before = lax.ppermute(state, "surf", [(i, (i + 1) % surf_count) for i in range(surf_count)])
    beyond = lax.ppermute(state, "surf", [((i + 1) % surf_count, i) for i in range(surf_count)])
    (rhs,) = run(
        residual_kernel,
        [(x, None) for x in (before, near_state, beyond, weight, line_source, near_lift)],
        [element_vectors],
    )
    in_place = lines == TILE
    if in_place:
        blocks_in = [in_hbm(jnp.transpose(x, (0, 2, 1, 3))) for x in (dinv, lower, upper)]
        (raw,) = run(
            functools.partial(relayout_kernel, kinds=2),
            [(x, ANY) for x in blocks_in[:2]] + [(x, None) for x in (before, weight)],
            [((2, depth, lines, width, width), BF16, None)],
            scratch=[
                pltpu.VMEM((2, depth, width, lines, width), BF16),
                pltpu.SemaphoreType.DMA((2, depth)),
            ],
        )
    else:
        raw = jnp.stack([dinv, lower, upper])
    scaled, y_local, y_leave = run(
        local_kernel,
        [(rhs, 1), (raw, 2), (act, 1)],
        [element_vectors, element_vectors, line_vector],
        blocks,
    )
    came_y = mates(y_leave)
    wall_y, wall_leave = run(
        wall_kernel,
        [(came_y, 0), (scaled, 1), (raw, 2), (act, 1), (y_local, 1)],
        [element_vectors, line_vector],
        blocks,
    )
    arrivals = [lax.ppermute(wall_leave, "wall", hop_pairs(wall_count, 0, 1))]
    q, *rest = run(
        functools.partial(
            pair_kernel, first_chip=1, fetch=in_place, turn=False, kind=1, lines=(0, block), ascending=True
        ),
        [(after(raw, y_leave), 2)] + ([(blocks_in[2], ANY)] if in_place else []),
        [element_pairs, line_pairs, line_sent] + ([((1, *blocks_in[2].shape), BF16, None)] if in_place else []),
        blocks,
        [pltpu.SemaphoreType.DMA((depth,))] if in_place else [],
    )
    a, got_a = [rest[0]], [mates(after(rest[1], came_y))]
    s, c, sent_c = run(
        functools.partial(
            pair_kernel,
            first_chip=0,
            fetch=False,
            turn=in_place,
            kind=0 if in_place else 2,
            lines=(0, block),
            ascending=False,
        ),
        [(after(raw, a[-1], wall_leave), 2)] + ([(rest[2], None)] if in_place else []),
        [element_pairs, line_pairs, line_sent],
        blocks,
        [pltpu.VMEM((1, depth, lines, width, width), BF16)] if in_place else [],
    )
    got_c = mates(after(sent_c, arrivals[0],got_a[-1]))

    def hop(came, pairs, local, idle, at):
        (out,) = run(
            functools.partial(hop_kernel, chip=at),
            [(came, 0), (act, 1), (local, 0), (idle, 0)] + [(x, 0) for x in pairs],
            [line_vector],
            blocks,
        )
        return out

    out = wall_leave
    for at in range(1, last):
        if at == 1:
            (out,) = run(
                functools.partial(early_hop_kernel, chip=at, parts=parts),
                [(arrivals[-1], 0), (act, 1), (came_y, 0), (y_local, 1)] + [(x, 0) for x in got_a + a],
                [line_vector],
                blocks,
            )
            (chip_a,) = run(
                functools.partial(chip_kernel, parts=parts, width=width, own_first=False),
                [(after(x, out) if i == 0 else x, 0) for i, x in enumerate(got_a + a)],
                [line_pairs],
                blocks,
            )
            (y_chip,) = run(
                chip_local_kernel,
                [(after(came_y, out), 0), (act, 1), (y_local, 1)] + [(x, 0) for x in a],
                [line_vector],
                blocks,
            )
            through, sent_d, echo = run(
                functools.partial(through_kernel, parts=parts),
                [(act, 1), (after(q, out, chip_a, y_chip), 1), (s, 1), (wall_y, 1)] + [(x, 0) for x in a],
                [line_pairs, vector_sent, line_vector],
                blocks,
            )
        else:
            out = hop(arrivals[-1], [chip_a], y_chip, y_chip, at)
        arrivals.append(lax.ppermute(out, "wall", hop_pairs(wall_count, at, at + 1)))
        if at == 1:
            got_d = mates(after(sent_d, got_c, arrivals[-1]))

    def chosen(arrived, chips):
        return run(
            functools.partial(choose_kernel, chips=chips), [(x, 0) for x in arrived], [line_vector], blocks
        )[0]

    def turn(first_chip, end_chip, entered, held=()):
        return run(
            functools.partial(turn_kernel, parts=parts, chips=(first_chip, end_chip), fill=not held),
            [(x, 0) for x in (entered, came_y, echo, got_c, got_d, through, *got_a)]
            + [(x, ANY) for x in held],
            [line_vector] * 3,
            blocks,
            aliases={6 + parts + i: i for i in range(3)} if held else {},
        )

    def steps(late, flow, held=()):
        return run(
            functools.partial(steps_kernel, late=late),
            [(flow, 0)] + [(x, 1) for x in (scaled, q, act, wall_y)] + [(x, ANY) for x in held],
            [element_vectors],
            blocks,
            aliases={5: 0} if held else {},
        )

    entered = chosen(arrivals[:-1], list(range(1, last)))
    held = turn(last - 1, last, after(entered, out))
    arrivals[-1] = after(arrivals[-1], held[0])
    held = turn(last, last + 1, arrivals[-1], held)
    x_chip = held[-1]
    entered = chosen(arrivals, list(range(1, last + 1)))
    (out,) = run(functools.partial(send_kernel, last=last), [(x_chip, 0), (entered, 0)], [line_vector], blocks)
    arrived = [lax.ppermute(out, "wall", hop_pairs(wall_count, last, last - 1))]
    (chip_c,) = run(
        functools.partial(chip_kernel, parts=1, width=width, own_first=True),
        [(after(got_c, x_chip), 0), (c, 0)],
        [line_pairs],
        blocks,
    )
    y = ()
    for at in range(last - 1, 0, -1):
        came = arrived[-1]
        if at == 1:
            enter_y, middle, x_chip = turn(1, last - 1, after(entered, out), held)
            (flow,) = run(entry_kernel, [(enter_y, 0), (after(arrived[0], out), 0)], [line_vector], blocks)
            y = steps(False, flow)
            came = after(came, *y)
        out = hop(came, [chip_c], x_chip, entered, at)
        arrived.append(lax.ppermute(out, "wall", hop_pairs(wall_count, at, at - 1)))
    (y,) = steps(True, arrived[-1], y)
    beyond, left = run(
        functools.partial(leave_kernel, chips=list(range(last - 1, -1, -1))),
        [(x, 0) for x in (c, middle, *arrived)],
        [line_vector, line_vector],
        blocks,
    )
    met_left = mates(left)
    (solution,) = run(
        last_kernel, [(beyond, 0), (met_left, 0)] + [(x, 1) for x in (s, act, y)], [element_vectors], blocks
    )
    return solution


def solution(mesh):
    in_specs = (
        P(("wall", "surf"), None),
        P(("wall", "surf"), None),
        P(("wall", "surf"), None),
        P(("wall", "surf"), None),
        P(),
        P("wall", "surf"),
        P("surf"),
        P("wall", "surf", None, None),
        P("wall", "surf", None, None),
        P("wall", "surf", None, None),
    )
    out_specs = P("wall", "surf", None)
    return jax.shard_map(
        per_device, mesh=mesh, in_specs=in_specs, out_specs=out_specs, check_vma=False
    )
```

```python
import functools

import jax
import jax.numpy as jnp
from jax import lax
from jax.experimental import pallas as pl
from jax.experimental.pallas import tpu as pltpu
from jax.sharding import PartitionSpec as P

F32 = jnp.float32
BF16 = jnp.bfloat16
TILE = 8
LANES = 128
VMEM = pl.BlockSpec(memory_space=pltpu.VMEM)
ANY = pl.BlockSpec(memory_space=pl.ANY)
SMEM = pl.BlockSpec(memory_space=pltpu.SMEM)


def split2(x):
    high = x.astype(BF16)
    return high, (x - high.astype(F32)).astype(BF16)


def product(x, y):
    dot = functools.partial(jnp.dot, preferred_element_type=F32)
    return dot(x[0], y[0]) + (dot(x[0], y[1]) + dot(x[1], y[0]))


def room_of(width):
    rows = -(-width // (2 * TILE)) * 2 * TILE
    main = width // LANES * LANES
    return rows, 2 * main + (LANES if width - main <= LANES // 2 else 2 * LANES), main


def pair_at(ref, width, *at):
    if len(ref.shape) > 2:
        return [ref[(*at, i)] for i in range(2)]
    rows, columns, main = room_of(width)
    here = pl.ds(at[0] * rows, width)
    step = (columns - 2 * main) // 2
    if width == main:
        return [ref[here, i * main : (i + 1) * main] for i in range(2)]
    return [
        jnp.concatenate(
            [
                ref[here, i * main : (i + 1) * main],
                ref[here, 2 * main + i * step : 2 * main + i * step + width - main],
            ],
            axis=1,
        )
        for i in range(2)
    ]


def store_pair(ref, pair, *at):
    if len(ref.shape) > 2:
        for i in range(2):
            ref[(*at, i)] = pair[i]
        return
    width = pair[0].shape[0]
    rows, columns, main = room_of(width)
    here = pl.ds(at[0] * rows, width)
    step = (columns - 2 * main) // 2
    for i in range(2):
        ref[here, i * main : (i + 1) * main] = pair[i][:, :main]
        if width > main:
            ref[here, 2 * main + i * step : 2 * main + i * step + width - main] = pair[i][:, main:]


def apply_pairs(vector, ref, *at):
    count = vector.shape[0]
    rows = lax.broadcasted_iota(jnp.int32, vector.shape, 0)
    both = jnp.concatenate(split2(vector), axis=0)
    total = jnp.zeros(vector.shape, F32)
    for l in range(count):
        part, here = ref, l
        if isinstance(ref, (list, tuple)):
            each = count // len(ref)
            part, here = ref[l // each], l % each
        high, low = pair_at(part, vector.shape[1], *at, here)
        first = jnp.dot(both, high, preferred_element_type=F32)
        second = jnp.dot(both, low, preferred_element_type=F32)
        total = jnp.where(rows == l, first[:count] + first[count:] + second[:count], total)
    return total


def apply_rows(vector, ref, *at):
    count = vector.shape[0]
    rows = lax.broadcasted_iota(jnp.int32, vector.shape, 0)
    both = jnp.concatenate(split2(vector), axis=0)
    total = jnp.zeros(vector.shape, F32)
    for l in range(count):
        first = lax.dot_general(
            both, ref[(*at, l)], (((1,), (1,)), ((), ())), preferred_element_type=F32
        )
        total = jnp.where(rows == l, first[:count] + first[count:], total)
    return total


def core_of():
    return lax.rem(lax.axis_index("wall"), 2)


def chip_of():
    return lax.div(lax.axis_index("wall"), 2)


def between(chips, core):
    inside = jnp.logical_and(chip_of() >= chips[0], chip_of() < chips[1])
    return jnp.logical_and(inside, core_of() == core)


def pair_kernel(raw_ref, *refs, first_chip, fetch, turn, **options):
    if fetch:
        next_ref, landed, arrived = refs[0], refs[4], refs[-1]
        copies = [
            pltpu.make_async_copy(next_ref.at[e], landed.at[0, e], arrived.at[e]) for e in range(next_ref.shape[0])
        ]
        for copy in copies:
            copy.start()
        refs = refs[1:4]
    other_ref = raw_ref
    if turn:
        other_ref = refs[-1]
        for e in range(raw_ref.shape[1]):
            turn_blocks(refs[0], 0, e, other_ref)
        refs = refs[1:4]

    @pl.when(chip_of() >= first_chip)
    def _():
        make_pairs(raw_ref, other_ref, *refs[-3:], **options)

    if fetch:
        for copy in copies:
            copy.wait()


def make_pairs(raw_ref, other_ref, step_ref, whole_ref, sent_ref, *, kind, lines, ascending):
    count, width = raw_ref.shape[1], raw_ref.shape[3]
    for l in range(*lines):
        for e in range(count):
            block = lax.dot_general(
                other_ref[kind, e, l], raw_ref[0, e, l], (((0,), (1,)), ((), ())), preferred_element_type=F32
            )
            store_pair(step_ref, split2(block), e, l)
    order = list(range(count)) if ascending else list(range(count))[::-1]
    for l in range(*lines):
        whole = pair_at(step_ref, width, order[0], l)
        for e in order[1:]:
            whole = split2(product(whole, pair_at(step_ref, width, e, l)))
        if count % 2:
            whole = [-x for x in whole]
        store_pair(whole_ref, whole, l - lines[0])
        store_pair(sent_ref, whole, l - lines[0])


def chip_kernel(*refs, parts, width, own_first, chips):
    got_refs, own_refs, chip_ref = refs[:parts], refs[parts:-1], refs[-1]

    @pl.when(between(chips, 1))
    def _():
        each = chip_ref.shape[0] // parts
        for l in range(chip_ref.shape[0]):
            pairs = [pair_at(x[l // each], width, l % each) for x in (got_refs, own_refs)]
            store_pair(chip_ref, split2(product(*(pairs[::-1] if own_first else pairs))), l)


def turn_blocks(landed_ref, a, e, raw_ref):
    turned = jnp.swapaxes(landed_ref[a, e], 0, 1)
    for l in range(raw_ref.shape[2]):
        raw_ref[a, e, l] = turned[l]


def prepare_kernel(*refs, taken):
    blocks = refs[7 : 7 + taken]
    places, (weight_ref, rhs_ref, act_ref, state_ref, lift_ref) = refs[:7], refs[7 + taken : 12 + taken]
    slot_ref, len_ref, coef_ref, nb_ref, source_ref, arrived = refs[12 + taken + (taken > 0) :][:6]
    targets = (slot_ref, len_ref, coef_ref, nb_ref, source_ref, state_ref, lift_ref)
    copies = [
        pltpu.make_async_copy(there, here, arrived.at[i]) for i, (there, here) in enumerate(zip(places, targets))
    ]
    block_copies = []
    if taken:
        raw_ref, landed, landed_at = refs[12 + taken], refs[-2], refs[-1]
        block_copies = [
            pltpu.make_async_copy(ref.at[e], landed.at[a, e], landed_at.at[a, e])
            for a, ref in enumerate(blocks)
            for e in range(landed.shape[1])
        ]
    for copy in copies + block_copies:
        copy.start()
    for copy in copies:
        copy.wait()
    faces, slots = coef_ref.shape
    depth, lines = slot_ref.shape
    cells = 3 * slots
    k = lax.broadcasted_iota(jnp.int32, (cells, slots), 0)
    e = lax.broadcasted_iota(jnp.int32, (cells, slots), 1)
    weight = jnp.zeros((cells, slots), F32)
    own = jnp.zeros((1, slots), F32)
    for f in range(faces):
        coef = coef_ref[f : f + 1, :]
        own = own + coef
        weight = weight - jnp.where(k == nb_ref[f : f + 1, :], coef, 0.0)
    weight = weight + jnp.where(k == e + slots, own, 0.0)
    count = depth * lines
    rows = lax.broadcasted_iota(jnp.int32, (count, slots), 0)
    slot = jnp.zeros((count, slots), jnp.int32)
    for g in range(depth):
        for l in range(lines):
            slot = jnp.where(rows == g * lines + l, slot_ref[g, l], slot)
    chosen = (slot == lax.broadcasted_iota(jnp.int32, (count, slots), 1)).astype(F32).astype(BF16)
    high = weight.astype(BF16)
    mid, low = split2(weight - high.astype(F32))
    for i, part in enumerate((high, mid, low)):
        weight_ref[i * count : (i + 1) * count, :] = lax.dot_general(
            chosen, part, (((1,), (1,)), ((), ())), preferred_element_type=F32
        ).astype(BF16)
    rhs_ref[...] = jnp.dot(chosen, source_ref[...], preferred_element_type=F32)
    rows = lax.broadcasted_iota(jnp.int32, act_ref.shape[1:], 0)
    length = jnp.zeros(act_ref.shape[1:], jnp.int32)
    for l in range(lines):
        length = jnp.where(rows == l, len_ref[l], length)
    place = lax.axis_index("wall") * depth
    for g in range(depth):
        act_ref[g] = (place + g < length).astype(F32)
    for i, copy in enumerate(block_copies):
        copy.wait()
        turn_blocks(landed, *divmod(i, landed.shape[1]), raw_ref)


def residual_kernel(before, state, after, weight, source, lift, rhs_ref):
    cells = jnp.concatenate([before[...], state[...], after[...]], axis=0)
    parts = jnp.dot(weight[...], cells, preferred_element_type=F32)
    count = source.shape[0]
    face_sum = parts[:count] + (parts[count : 2 * count] + parts[2 * count :])
    flux = jnp.dot(face_sum.astype(BF16), lift[...], preferred_element_type=F32)
    rhs = source[...] - flux
    depth, lines, _ = rhs_ref.shape
    for g in range(depth):
        rhs_ref[g] = rhs[g * lines : (g + 1) * lines]


def forward_local(scaled, q_ref, act_ref, carried):
    values = []
    for g, value in enumerate(scaled):
        if carried is not None:
            value = value - apply_pairs(carried, q_ref, g)
        carried = act_ref[g] * value
        values.append(carried)
    return values


def backward_local(values, s_ref, act_ref, carried):
    solved = [None] * len(values)
    for g in range(len(values) - 1, -1, -1):
        value = values[g]
        if carried is not None:
            value = value - apply_pairs(carried, s_ref, g)
        carried = act_ref[g] * value
        solved[g] = carried
    return solved


def local_kernel(rhs_ref, raw_ref, act_ref, scaled_ref, y_ref, leave_ref):
    depth = rhs_ref.shape[0]
    scaled = [apply_rows(rhs_ref[g], raw_ref, 0, g) for g in range(depth)]
    values = raw_steps(scaled, raw_ref, act_ref, None)
    for g in range(depth):
        scaled_ref[g] = scaled[g]
        y_ref[g] = values[g]
    leave_ref[...] = values[-1]


def raw_steps(scaled, raw_ref, act_ref, carried):
    values = []
    for g, value in enumerate(scaled):
        if carried is not None:
            value = value - apply_rows(apply_rows(carried, raw_ref, 1, g), raw_ref, 0, g)
        carried = act_ref[g] * value
        values.append(carried)
    return values


def wall_kernel(came_ref, scaled_ref, raw_ref, act_ref, y_ref, out_ref, leave_ref):
    depth = y_ref.shape[0]
    out_ref[...] = y_ref[...]
    leave_ref[...] = y_ref[depth - 1]

    @pl.when(lax.axis_index("wall") == 1)
    def _():
        values = raw_steps([scaled_ref[g] for g in range(depth)], raw_ref, act_ref, came_ref[...])
        for g in range(depth):
            out_ref[g] = values[g]
        leave_ref[...] = values[-1]


def chip_local_kernel(came_ref, act_ref, y_ref, *refs, chips):
    own_refs, out_ref = refs[:-1], refs[-1]
    depth = y_ref.shape[0]
    out_ref[...] = y_ref[depth - 1]

    @pl.when(between(chips, 1))
    def _():
        out_ref[...] = act_ref[depth - 1] * apply_pairs(came_ref[...], own_refs) + y_ref[depth - 1]


def three_terms(x):
    high = x.astype(BF16)
    return high, *split2(x - high.astype(F32))


def through_kernel(act_ref, q_ref, s_ref, y_ref, *refs, parts):
    whole_refs, (out_ref, sent_ref, echo_ref) = refs[:parts], refs[parts:]
    depth, lines, _, _, width = q_ref.shape
    main, below = width // LANES * LANES, lines * room_of(width)[0]
    echo = backward_local([y_ref[g] for g in range(depth)], s_ref, act_ref, None)[0]
    echo_ref[...] = echo
    for i, term in enumerate(three_terms(echo)):
        sent_ref[below + 2 * TILE * i : below + 2 * TILE * i + lines, :main] = term[:, :main]
        if width > main:
            sent_ref[below + 2 * TILE * i : below + 2 * TILE * i + lines, main:width] = term[:, main:]

    @pl.when(chip_of() > 0)
    def _():
        for l in range(lines):
            active = [act_ref[g, l : l + 1, :] for g in range(depth)]
            steps = [[-x for x in pair_at(q_ref, width, 0, l)]]
            for g in range(1, depth - 1):
                steps.append(split2(-product(steps[-1], pair_at(q_ref, width, g, l))))
            each = lines // parts
            value = [
                (active[depth - 1] * x.astype(F32)).astype(BF16)
                for x in pair_at(whole_refs[l // each], width, l % each)
            ]
            for g in range(depth - 2, -1, -1):
                reach = steps[g][0].astype(F32) + steps[g][1].astype(F32)
                total = active[g] * (reach - product(value, pair_at(s_ref, width, g, l)))
                value = split2(total)
            pair = value
            store_pair(out_ref, pair, l)
            store_pair(sent_ref, pair, l)


def hop_kernel(came_ref, act_ref, local_ref, idle_ref, *refs, chip):
    pair_refs, out_ref = refs[:-1], refs[-1]
    out_ref[...] = idle_ref[...]

    @pl.when(jnp.logical_and(chip_of() == chip, core_of() == 1))
    def _():
        gone = apply_pairs(came_ref[...], pair_refs)
        out_ref[...] = act_ref[act_ref.shape[0] - 1] * gone + local_ref[...]


def early_hop_kernel(came_ref, act_ref, mate_ref, y_ref, *refs, chip, parts):
    got_refs, own_refs, out_ref = refs[:parts], refs[parts : 2 * parts], refs[-1]
    depth = y_ref.shape[0]
    out_ref[...] = came_ref[...]

    @pl.when(jnp.logical_and(chip_of() == chip, core_of() == 1))
    def _():
        middle = apply_pairs(came_ref[...], got_refs) + mate_ref[...]
        out_ref[...] = act_ref[depth - 1] * apply_pairs(middle, own_refs) + y_ref[depth - 1]


def chosen_arrival(refs, chips, like):
    here = chip_of()
    value = jnp.zeros(like, F32)
    for ref, chip in zip(refs, chips):
        value = jnp.where(here == chip, ref[...], value)
    return value


def choose_kernel(*refs, chips):
    refs[-1][...] = chosen_arrival(refs[:-1], chips, refs[-1].shape)


def turn_kernel(enter_ref, came_ref, echo_ref, got_c, got_d, own_d, *refs, parts, chips, fill):
    got_refs, (enter_y, mid_ref, out_ref) = refs[:parts], refs[-3:]
    inside = jnp.logical_and(chip_of() >= chips[0], chip_of() < chips[1])
    if fill:

        @pl.when(jnp.logical_not(inside))
        def _():
            enter_y[...] = enter_ref[...]
            mid_ref[...] = echo_ref[...]
            out_ref[...] = echo_ref[...]

    @pl.when(jnp.logical_and(inside, core_of() == 1))
    def _():
        enter = enter_ref[...]
        leave = apply_pairs(enter, got_refs) + came_ref[...]
        middle = apply_pairs(leave, own_d) + echo_ref[...]
        lines, width = enter.shape
        below = lines * room_of(width)[0]
        first = apply_pairs(enter, got_d)
        for i in range(3):
            first = first + got_d[below + 2 * TILE * i : below + 2 * TILE * i + lines, :width].astype(F32)
        enter_y[...] = leave
        mid_ref[...] = middle
        out_ref[...] = apply_pairs(middle, got_c) + first


def send_kernel(x_ref, enter_ref, out_ref, *, last):
    out_ref[...] = jnp.where(chip_of() == last, x_ref[...], enter_ref[...])


def steps_kernel(flow_ref, scaled_ref, q_ref, act_ref, wall_ref, *refs, late):
    y_ref = refs[-1]
    depth = scaled_ref.shape[0]
    here, core = chip_of(), core_of()
    if late:
        inside = jnp.logical_and(core == 0, here > 1)
    else:
        inside = jnp.logical_and(here > 0, jnp.logical_or(core == 1, here == 1))

        @pl.when(here == 0)
        def _():
            y_ref[...] = wall_ref[...]

    @pl.when(inside)
    def _():
        values = forward_local([scaled_ref[g] for g in range(depth)], q_ref, act_ref, flow_ref[...])
        for g in range(depth):
            y_ref[g] = values[g]


def entry_kernel(own_ref, came_ref, out_ref):
    out_ref[...] = jnp.where(core_of() == 1, own_ref[...], came_ref[...])


def leave_kernel(own_ref, first_ref, *refs, chips):
    came_ref, out_ref = refs[-2:]
    came_ref[...] = chosen_arrival(refs[:-2], chips, came_ref.shape)
    out_ref[...] = first_ref[...]

    @pl.when(jnp.logical_and(core_of() == 1, chip_of() > 0))
    def _():
        out_ref[...] = apply_pairs(came_ref[...], own_ref) + first_ref[...]


def wall_middle_kernel(came_ref, got_c, got_d, out_ref):
    @pl.when(lax.axis_index("wall") == 0)
    def _():
        lines, width = came_ref.shape
        below = lines * room_of(width)[0]
        value = apply_pairs(came_ref[...], got_c)
        for i in range(3):
            value = value + got_d[below + 2 * TILE * i : below + 2 * TILE * i + lines, :width].astype(F32)
        out_ref[...] = value


def last_kernel(beyond_ref, met_ref, middle_ref, wall_ref, s_ref, act_ref, y_ref, out_ref):
    depth = y_ref.shape[0]
    core, chip = core_of(), chip_of()
    first = jnp.where(chip == 0, middle_ref[...], met_ref[...])
    second = jnp.where(chip == 0, wall_ref[...], beyond_ref[...])
    solved = backward_local(
        [y_ref[g] for g in range(depth)], s_ref, act_ref, jnp.where(core == 0, first, second)
    )
    for g in range(depth):
        out_ref[g] = solved[g]


def padded_bytes(shape, dtype):
    size = jnp.dtype(dtype).itemsize
    shape = (1,) * (2 - len(shape)) + tuple(shape)
    total = -(-shape[-2] // 16) * 16 * -(-shape[-1] // 128) * 128 * size
    for extent in shape[:-2]:
        total *= extent
    return total


def run(kernel, operands, outs, blocks=1, scratch=(), aliases=None):
    held = [(x.shape, x.dtype) for x, _ in operands] + [(s, t) for s, t, _ in outs]
    limit = sum(padded_bytes(s, t) for s, t in held)
    if blocks == 1:
        in_specs = [at if isinstance(at, pl.BlockSpec) else VMEM for _, at in operands]
        out_specs = [VMEM for _ in outs]
        grid = ()
    else:

        def spec(shape, at):
            if isinstance(at, pl.BlockSpec):
                return at
            if at is None:
                return pl.BlockSpec(shape, lambda i: (0,) * len(shape))
            size = tuple(n // blocks if axis == at else n for axis, n in enumerate(shape))
            return pl.BlockSpec(size, lambda i: tuple(i if axis == at else 0 for axis in range(len(shape))))

        in_specs = [spec(x.shape, at) for x, at in operands]
        out_specs = [spec(s, at) for s, _, at in outs]
        grid = (blocks,)
        limit = 2 * limit // blocks
    limit += sum(padded_bytes(s.shape, s.dtype) for s in scratch if s.memory_space == pltpu.VMEM)
    limit = min(limit + (2 << 20), 60 << 20)
    return pl.pallas_call(
        kernel,
        grid=grid,
        in_specs=in_specs,
        out_specs=out_specs,
        out_shape=[jax.ShapeDtypeStruct(s, t) for s, t, _ in outs],
        scratch_shapes=list(scratch),
        input_output_aliases=aliases or {},
        compiler_params=pltpu.CompilerParams(vmem_limit_bytes=limit),
        cost_estimate=pl.CostEstimate(flops=1, bytes_accessed=1, transcendentals=0),
    )(*[x for x, _ in operands])


def hop_pairs(count, start, end, core=1, relay=None):
    start, end = 2 * start + 1, 2 * end + core
    target = {i: i ^ 1 for i in range(count)}
    cycle = [start, end, end ^ 1, start ^ 1]
    if relay is not None:
        cycle[3:3] = [2 * relay, 2 * relay + 1]
    target.update(zip(cycle, cycle[1:] + cycle[:1]))
    return sorted(target.items())


def in_hbm(value):
    return pltpu.with_memory_space_constraint(value, pltpu.HBM)


def after(value, *others):
    return lax.optimization_barrier((value, *others))[0]


def per_device(state, source, face_coef, neighbour, lift, elem_slot, line_len, dinv, lower, upper):
    wall_count = lax.axis_size("wall")
    surf_count = lax.axis_size("surf")
    last = wall_count // 2 - 1
    depth, lines, width, _ = dinv.shape
    slots = state.shape[0]
    block = TILE if lines % TILE == 0 else lines
    blocks = lines // block
    parts = 1
    room, columns, _ = room_of(width)
    line_vector = ((lines, width), F32, 0)
    element_vectors = ((depth, lines, width), F32, 1)
    line_sent = ((lines * room, columns), BF16, 0)
    vector_sent = ((lines * room + 6 * TILE * blocks, columns), BF16, 0)
    line_pairs = ((lines, 2, width, width), BF16, 0)
    part_sent = ((lines // parts * room, columns), BF16, 0)
    part_pairs = ((lines // parts, 2, width, width), BF16, 0)
    element_pairs = ((depth, lines, 2, width, width), BF16, 1)

    def mates(value):
        return lax.ppermute(value, "wall", [(i, i ^ 1) for i in range(wall_count)])

    def relaid(arrays, *others):
        if lines != TILE:
            return jnp.stack(arrays)
        shape = (len(arrays), depth, lines, width, width)
        return run(
            functools.partial(relayout_kernel, kinds=len(arrays)),
            [(in_hbm(jnp.transpose(x, (0, 2, 1, 3))), ANY) for x in arrays] + [(x, None) for x in others],
            [(shape, BF16, None)],
            scratch=[
                pltpu.VMEM((len(arrays), depth, width, lines, width), BF16),
                pltpu.SemaphoreType.DMA((len(arrays), depth)),
            ],
        )[0]

    count = depth * lines
    small = (elem_slot, line_len, face_coef.T, neighbour.T, source)
    in_place = lines == TILE
    blocks_in = [in_hbm(jnp.transpose(x, (0, 2, 1, 3))) for x in (dinv, lower, upper)] if in_place else []
    weight, line_source, act, near_state, near_lift, *landed = run(
        functools.partial(prepare_kernel, taken=2 if in_place else 0),
        [(in_hbm(x), ANY) for x in (*small, state, lift)] + [(x, ANY) for x in blocks_in[:2]],
        [
            ((3 * count, 3 * slots), BF16, None),
            ((count, width), F32, None),
            element_vectors,
            (state.shape, BF16, None),
            (lift.shape, BF16, None),
        ]
        + ([((2, depth, lines, width, width), BF16, None)] if in_place else []),
        scratch=[(pltpu.SMEM if i < 2 else pltpu.VMEM)(x.shape, x.dtype) for i, x in enumerate(small)]
        + [pltpu.SemaphoreType.DMA((len(small) + 2,))]
        + (
            [pltpu.VMEM((2, depth, width, lines, width), BF16), pltpu.SemaphoreType.DMA((2, depth))]
            if in_place
            else []
        ),
    )
    before = lax.ppermute(state, "surf", [(i, (i + 1) % surf_count) for i in range(surf_count)])
    beyond = lax.ppermute(state, "surf", [((i + 1) % surf_count, i) for i in range(surf_count)])
    (rhs,) = run(
        residual_kernel,
        [(x, None) for x in (before, near_state, beyond, weight, line_source, near_lift)],
        [element_vectors],
    )
    raw = landed[0] if in_place else jnp.stack([dinv, lower, upper])
    scaled, y_local, y_leave = run(
        local_kernel,
        [(rhs, 1), (raw, 2), (act, 1)],
        [element_vectors, element_vectors, line_vector],
        blocks,
    )
    came_y = mates(y_leave)
    wall_y, wall_leave = run(
        wall_kernel,
        [(came_y, 0), (scaled, 1), (raw, 2), (act, 1), (y_local, 1)],
        [element_vectors, line_vector],
        blocks,
    )
    arrivals = [lax.ppermute(wall_leave, "wall", hop_pairs(wall_count, 0, 1))]
    q, *rest = run(
        functools.partial(
            pair_kernel, first_chip=1, fetch=in_place, turn=False, kind=1, lines=(0, block), ascending=True
        ),
        [(after(raw, y_leave), 2)] + ([(blocks_in[2], ANY)] if in_place else []),
        [element_pairs, line_pairs, line_sent] + ([((1, *blocks_in[2].shape), BF16, None)] if in_place else []),
        blocks,
        [pltpu.SemaphoreType.DMA((depth,))] if in_place else [],
    )
    a, got_a = [rest[0]], [mates(after(rest[1], came_y))]
    s, c, sent_c = run(
        functools.partial(
            pair_kernel,
            first_chip=0,
            fetch=False,
            turn=in_place,
            kind=0 if in_place else 2,
            lines=(0, block),
            ascending=False,
        ),
        [(after(raw, a[-1], wall_leave), 2)] + ([(rest[2], None)] if in_place else []),
        [element_pairs, line_pairs, line_sent],
        blocks,
        [pltpu.VMEM((1, depth, lines, width, width), BF16)] if in_place else [],
    )
    got_c = mates(after(sent_c, arrivals[0],got_a[-1]))

    def hop(came, pairs, local, idle, at):
        (out,) = run(
            functools.partial(hop_kernel, chip=at),
            [(came, 0), (act, 1), (local, 0), (idle, 0)] + [(x, 0) for x in pairs],
            [line_vector],
            blocks,
        )
        return out

    out = wall_leave
    for at in range(1, last):
        if at == 1:
            (out,) = run(
                functools.partial(early_hop_kernel, chip=at, parts=parts),
                [(arrivals[-1], 0), (act, 1), (came_y, 0), (y_local, 1)] + [(x, 0) for x in got_a + a],
                [line_vector],
                blocks,
            )
            (chip_a,) = run(
                functools.partial(chip_kernel, parts=parts, width=width, own_first=False, chips=(2, last)),
                [(after(x, out) if i == 0 else x, 0) for i, x in enumerate(got_a + a)],
                [line_pairs],
                blocks,
            )
            (y_chip,) = run(
                functools.partial(chip_local_kernel, chips=(2, last)),
                [(after(came_y, out), 0), (act, 1), (y_local, 1)] + [(x, 0) for x in a],
                [line_vector],
                blocks,
            )
            through, sent_d, echo = run(
                functools.partial(through_kernel, parts=parts),
                [(act, 1), (after(q, out, chip_a, y_chip), 1), (s, 1), (wall_y, 1)] + [(x, 0) for x in a],
                [line_pairs, vector_sent, line_vector],
                blocks,
            )
        else:
            out = hop(arrivals[-1], [chip_a], y_chip, y_chip, at)
        pairs = hop_pairs(wall_count, at, at + 1, relay={1: 0}.get(at))
        arrivals.append(lax.ppermute(out, "wall", pairs))
        if at == 1:
            got_d = mates(after(sent_d, got_c, arrivals[-1]))

    def chosen(arrived, chips):
        return run(
            functools.partial(choose_kernel, chips=chips), [(x, 0) for x in arrived], [line_vector], blocks
        )[0]

    def turn(first_chip, end_chip, entered, held=()):
        return run(
            functools.partial(turn_kernel, parts=parts, chips=(first_chip, end_chip), fill=not held),
            [(x, 0) for x in (entered, came_y, echo, got_c, got_d, through, *got_a)]
            + [(x, ANY) for x in held],
            [line_vector] * 3,
            blocks,
            aliases={6 + parts + i: i for i in range(3)} if held else {},
        )

    def steps(late, flow, held=()):
        return run(
            functools.partial(steps_kernel, late=late),
            [(flow, 0)] + [(x, 1) for x in (scaled, q, act, wall_y)] + [(x, ANY) for x in held],
            [element_vectors],
            blocks,
            aliases={5: 0} if held else {},
        )

    (chip_c,) = run(
        functools.partial(chip_kernel, parts=1, width=width, own_first=True, chips=(1, last)),
        [(after(got_c, out), 0), (c, 0)],
        [line_pairs],
        blocks,
    )
    arrivals[-1] = after(arrivals[-1], chip_c)
    held = turn(last, last + 1, arrivals[-1])
    entered = chosen(arrivals, list(range(1, last + 1)))
    x_chip = held[-1]
    (out,) = run(functools.partial(send_kernel, last=last), [(x_chip, 0), (entered, 0)], [line_vector], blocks)
    arrived = [lax.ppermute(out, "wall", hop_pairs(wall_count, last, last - 1))]
    held = turn(last - 1, last, after(entered, out), held)
    x_chip = held[-1]
    y = ()
    for at in range(last - 1, 0, -1):
        came = arrived[-1]
        if at == 1:
            enter_y, middle, x_chip = turn(1, last - 1, after(entered, out), held)
            (flow,) = run(entry_kernel, [(enter_y, 0), (after(arrived[0], out), 0)], [line_vector], blocks)
            y = steps(False, flow)
            came = after(came, *y)
        out = hop(came, [chip_c], x_chip, entered, at)
        arrived.append(lax.ppermute(out, "wall", hop_pairs(wall_count, at, at - 1, int(at > 1), {}.get(at))))
    wall = lax.ppermute(out, "wall", hop_pairs(wall_count, 1, 0))
    beyond, left = run(
        functools.partial(leave_kernel, chips=list(range(last - 1, 0, -1))),
        [(x, 0) for x in (c, middle, *arrived[:-1])],
        [line_vector, line_vector],
        blocks,
    )
    met_left = mates(after(left, out))
    (y,) = steps(True, arrived[-1], y)
    (wall_middle,) = run(
        wall_middle_kernel, [(after(arrived[-1], wall), 0), (got_c, 0), (got_d, 0)], [line_vector], blocks
    )
    (solution,) = run(
        last_kernel,
        [(beyond, 0), (met_left, 0), (wall_middle, 0), (wall, 0)] + [(x, 1) for x in (s, act, y)],
        [element_vectors],
        blocks,
    )
    return solution


def solution(mesh):
    in_specs = (
        P(("wall", "surf"), None),
        P(("wall", "surf"), None),
        P(("wall", "surf"), None),
        P(("wall", "surf"), None),
        P(),
        P("wall", "surf"),
        P("surf"),
        P("wall", "surf", None, None),
        P("wall", "surf", None, None),
        P("wall", "surf", None, None),
    )
    out_specs = P("wall", "surf", None)
    return jax.shard_map(
        per_device, mesh=mesh, in_specs=in_specs, out_specs=out_specs, check_vma=False
    )
```

```python
import functools

import jax
import jax.numpy as jnp
from jax import lax
from jax.experimental import pallas as pl
from jax.experimental.pallas import tpu as pltpu
from jax.sharding import PartitionSpec as P

F32 = jnp.float32
BF16 = jnp.bfloat16
TILE = 8
LANES = 128
VMEM = pl.BlockSpec(memory_space=pltpu.VMEM)
ANY = pl.BlockSpec(memory_space=pl.ANY)
SMEM = pl.BlockSpec(memory_space=pltpu.SMEM)


def split2(x):
    high = x.astype(BF16)
    return high, (x - high.astype(F32)).astype(BF16)


def product(x, y):
    dot = functools.partial(jnp.dot, preferred_element_type=F32)
    return dot(x[0], y[0]) + (dot(x[0], y[1]) + dot(x[1], y[0]))


def room_of(width):
    rows = -(-width // (2 * TILE)) * 2 * TILE
    main = width // LANES * LANES
    return rows, 2 * main + (LANES if width - main <= LANES // 2 else 2 * LANES), main


def pair_at(ref, width, *at):
    if len(ref.shape) > 2:
        return [ref[(*at, i)] for i in range(2)]
    rows, columns, main = room_of(width)
    here = pl.ds(at[0] * rows, width)
    step = (columns - 2 * main) // 2
    if width == main:
        return [ref[here, i * main : (i + 1) * main] for i in range(2)]
    return [
        jnp.concatenate(
            [
                ref[here, i * main : (i + 1) * main],
                ref[here, 2 * main + i * step : 2 * main + i * step + width - main],
            ],
            axis=1,
        )
        for i in range(2)
    ]


def store_pair(ref, pair, *at):
    if len(ref.shape) > 2:
        for i in range(2):
            ref[(*at, i)] = pair[i]
        return
    width = pair[0].shape[0]
    rows, columns, main = room_of(width)
    here = pl.ds(at[0] * rows, width)
    step = (columns - 2 * main) // 2
    for i in range(2):
        ref[here, i * main : (i + 1) * main] = pair[i][:, :main]
        if width > main:
            ref[here, 2 * main + i * step : 2 * main + i * step + width - main] = pair[i][:, main:]


def apply_pairs(vector, ref, *at):
    count = vector.shape[0]
    rows = lax.broadcasted_iota(jnp.int32, vector.shape, 0)
    both = jnp.concatenate(split2(vector), axis=0)
    total = jnp.zeros(vector.shape, F32)
    for l in range(count):
        part, here = ref, l
        if isinstance(ref, (list, tuple)):
            each = count // len(ref)
            part, here = ref[l // each], l % each
        high, low = pair_at(part, vector.shape[1], *at, here)
        first = jnp.dot(both, high, preferred_element_type=F32)
        second = jnp.dot(both, low, preferred_element_type=F32)
        total = jnp.where(rows == l, first[:count] + first[count:] + second[:count], total)
    return total


def apply_rows(vector, ref, *at):
    count = vector.shape[0]
    rows = lax.broadcasted_iota(jnp.int32, vector.shape, 0)
    both = jnp.concatenate(split2(vector), axis=0)
    total = jnp.zeros(vector.shape, F32)
    for l in range(count):
        first = lax.dot_general(
            both, ref[(*at, l)], (((1,), (1,)), ((), ())), preferred_element_type=F32
        )
        total = jnp.where(rows == l, first[:count] + first[count:], total)
    return total


def core_of():
    return lax.rem(lax.axis_index("wall"), 2)


def chip_of():
    return lax.div(lax.axis_index("wall"), 2)


def between(chips, core):
    inside = jnp.logical_and(chip_of() >= chips[0], chip_of() < chips[1])
    return jnp.logical_and(inside, core_of() == core)


def pair_kernel(raw_ref, *refs, first_chip, fetch, turn, **options):
    if fetch:
        next_ref, landed_ref, *outs, landed, turned_ref, arrived = refs
        copies = [
            pltpu.make_async_copy(next_ref.at[e], landed.at[0, e], arrived.at[e]) for e in range(next_ref.shape[0])
        ]
        for copy in copies:
            copy.start()
        turn_blocks(landed_ref, 0, 0, turned_ref)
    elif turn:
        landed_ref, *outs, turned_ref = refs
        for e in range(raw_ref.shape[1]):
            turn_blocks(landed_ref, 0, e, turned_ref)
    else:
        outs = refs

    def other(e, l):
        if turn or (fetch and e == 0):
            return turned_ref[0, e, l]
        return raw_ref[options["kind"], e, l]

    @pl.when(chip_of() >= first_chip)
    def _():
        make_pairs(raw_ref, other, *outs, lines=options["lines"], ascending=options["ascending"])

    if fetch:
        for copy in copies:
            copy.wait()


def make_pairs(raw_ref, other, step_ref, whole_ref, sent_ref, *, lines, ascending):
    count, width = raw_ref.shape[1], raw_ref.shape[3]
    for l in range(*lines):
        for e in range(count):
            block = lax.dot_general(
                other(e, l), raw_ref[0, e, l], (((0,), (1,)), ((), ())), preferred_element_type=F32
            )
            store_pair(step_ref, split2(block), e, l)
    order = list(range(count)) if ascending else list(range(count))[::-1]
    for l in range(*lines):
        whole = pair_at(step_ref, width, order[0], l)
        for e in order[1:]:
            whole = split2(product(whole, pair_at(step_ref, width, e, l)))
        if count % 2:
            whole = [-x for x in whole]
        store_pair(whole_ref, whole, l - lines[0])
        store_pair(sent_ref, whole, l - lines[0])


def chip_kernel(*refs, parts, width, own_first, chips):
    got_refs, own_refs, chip_ref = refs[:parts], refs[parts:-1], refs[-1]

    @pl.when(between(chips, 1))
    def _():
        each = chip_ref.shape[0] // parts
        for l in range(chip_ref.shape[0]):
            pairs = [pair_at(x[l // each], width, l % each) for x in (got_refs, own_refs)]
            store_pair(chip_ref, split2(product(*(pairs[::-1] if own_first else pairs))), l)


def turn_blocks(landed_ref, a, e, raw_ref):
    turned = jnp.swapaxes(landed_ref[a, e], 0, 1)
    for l in range(raw_ref.shape[2]):
        raw_ref[a, e, l] = turned[l]


def prepare_kernel(*refs, taken):
    blocks = refs[7 : 7 + taken]
    places, (weight_ref, rhs_ref, act_ref, state_ref, lift_ref) = refs[:7], refs[7 + taken : 12 + taken]
    slot_ref, len_ref, coef_ref, nb_ref, source_ref, arrived = refs[12 + taken + (taken > 0) :][:6]
    targets = (slot_ref, len_ref, coef_ref, nb_ref, source_ref, state_ref, lift_ref)
    copies = [
        pltpu.make_async_copy(there, here, arrived.at[i]) for i, (there, here) in enumerate(zip(places, targets))
    ]
    block_copies = []
    if taken:
        raw_ref, landed, landed_at = refs[12 + taken], refs[-2], refs[-1]
        places_in = [(a, e) for a in range(taken) for e in range(landed.shape[1]) if (a, e) != (1, 0)]
        block_copies = [
            pltpu.make_async_copy(blocks[a].at[e], landed.at[a, e], landed_at.at[a, e]) for a, e in places_in
        ]
    for copy in copies + block_copies:
        copy.start()
    for copy in copies:
        copy.wait()
    faces, slots = coef_ref.shape
    depth, lines = slot_ref.shape
    cells = 3 * slots
    k = lax.broadcasted_iota(jnp.int32, (cells, slots), 0)
    e = lax.broadcasted_iota(jnp.int32, (cells, slots), 1)
    weight = jnp.zeros((cells, slots), F32)
    own = jnp.zeros((1, slots), F32)
    for f in range(faces):
        coef = coef_ref[f : f + 1, :]
        own = own + coef
        weight = weight - jnp.where(k == nb_ref[f : f + 1, :], coef, 0.0)
    weight = weight + jnp.where(k == e + slots, own, 0.0)
    count = depth * lines
    rows = lax.broadcasted_iota(jnp.int32, (count, slots), 0)
    slot = jnp.zeros((count, slots), jnp.int32)
    for g in range(depth):
        for l in range(lines):
            slot = jnp.where(rows == g * lines + l, slot_ref[g, l], slot)
    chosen = (slot == lax.broadcasted_iota(jnp.int32, (count, slots), 1)).astype(F32).astype(BF16)
    high = weight.astype(BF16)
    mid, low = split2(weight - high.astype(F32))
    for i, part in enumerate((high, mid, low)):
        weight_ref[i * count : (i + 1) * count, :] = lax.dot_general(
            chosen, part, (((1,), (1,)), ((), ())), preferred_element_type=F32
        ).astype(BF16)
    rhs_ref[...] = jnp.dot(chosen, source_ref[...], preferred_element_type=F32)
    rows = lax.broadcasted_iota(jnp.int32, act_ref.shape[1:], 0)
    length = jnp.zeros(act_ref.shape[1:], jnp.int32)
    for l in range(lines):
        length = jnp.where(rows == l, len_ref[l], length)
    place = lax.axis_index("wall") * depth
    for g in range(depth):
        act_ref[g] = (place + g < length).astype(F32)
    for i, copy in enumerate(block_copies):
        copy.wait()
        turn_blocks(landed, *places_in[i], raw_ref)


def residual(before, state, after, weight, source, lift, depth):
    cells = jnp.concatenate([before[...], state[...], after[...]], axis=0)
    parts = jnp.dot(weight[...], cells, preferred_element_type=F32)
    count = source.shape[0]
    face_sum = parts[:count] + (parts[count : 2 * count] + parts[2 * count :])
    flux = jnp.dot(face_sum.astype(BF16), lift[...], preferred_element_type=F32)
    rhs = source[...] - flux
    lines = count // depth
    return [rhs[g * lines : (g + 1) * lines] for g in range(depth)]


def residual_kernel(before, state, after, weight, source, lift, rhs_ref):
    for g, rhs in enumerate(residual(before, state, after, weight, source, lift, rhs_ref.shape[0])):
        rhs_ref[g] = rhs


def forward_local(scaled, q_ref, act_ref, carried):
    values = []
    for g, value in enumerate(scaled):
        if carried is not None:
            value = value - apply_pairs(carried, q_ref, g)
        carried = act_ref[g] * value
        values.append(carried)
    return values


def backward_local(values, s_ref, act_ref, carried):
    solved = [None] * len(values)
    for g in range(len(values) - 1, -1, -1):
        value = values[g]
        if carried is not None:
            value = value - apply_pairs(carried, s_ref, g)
        carried = act_ref[g] * value
        solved[g] = carried
    return solved


def local_kernel(*refs, merged):
    if merged:
        *cells, raw_ref, act_ref, lower_in, scaled_ref, y_ref, leave_ref, landed_ref, arrived = refs
        copy = pltpu.make_async_copy(lower_in.at[0], landed_ref.at[0, 0], arrived)
        copy.start()
        rhs = residual(*cells, scaled_ref.shape[0])
    else:
        rhs_ref, raw_ref, act_ref, scaled_ref, y_ref, leave_ref = refs
        rhs = [rhs_ref[g] for g in range(rhs_ref.shape[0])]
    depth = len(rhs)
    scaled = [apply_rows(rhs[g], raw_ref, 0, g) for g in range(depth)]
    values = raw_steps(scaled, raw_ref, None, act_ref, None)
    for g in range(depth):
        scaled_ref[g] = scaled[g]
        y_ref[g] = values[g]
    leave_ref[...] = values[-1]
    if merged:
        copy.wait()


def raw_steps(scaled, raw_ref, first_ref, act_ref, carried):
    values = []
    for g, value in enumerate(scaled):
        if carried is not None:
            at = (first_ref, 0, 0) if first_ref is not None and g == 0 else (raw_ref, 1, g)
            value = value - apply_rows(apply_rows(carried, *at), raw_ref, 0, g)
        carried = act_ref[g] * value
        values.append(carried)
    return values


def wall_kernel(came_ref, scaled_ref, raw_ref, act_ref, y_ref, *refs):
    out_ref, leave_ref = refs[-2:]
    first_ref = refs[0] if len(refs) > 2 else None
    depth = y_ref.shape[0]
    out_ref[...] = y_ref[...]
    leave_ref[...] = y_ref[depth - 1]

    @pl.when(lax.axis_index("wall") == 1)
    def _():
        values = raw_steps([scaled_ref[g] for g in range(depth)], raw_ref, first_ref, act_ref, came_ref[...])
        for g in range(depth):
            out_ref[g] = values[g]
        leave_ref[...] = values[-1]


def chip_local_kernel(came_ref, act_ref, y_ref, *refs, chips):
    own_refs, out_ref = refs[:-1], refs[-1]
    depth = y_ref.shape[0]
    out_ref[...] = y_ref[depth - 1]

    @pl.when(between(chips, 1))
    def _():
        out_ref[...] = act_ref[depth - 1] * apply_pairs(came_ref[...], own_refs) + y_ref[depth - 1]


def three_terms(x):
    high = x.astype(BF16)
    return high, *split2(x - high.astype(F32))


def through_kernel(act_ref, q_ref, s_ref, y_ref, *refs, parts):
    whole_refs, (out_ref, sent_ref, echo_ref) = refs[:parts], refs[parts:]
    depth, lines, _, _, width = q_ref.shape
    main, below = width // LANES * LANES, lines * room_of(width)[0]
    echo = backward_local([y_ref[g] for g in range(depth)], s_ref, act_ref, None)[0]
    echo_ref[...] = echo
    for i, term in enumerate(three_terms(echo)):
        sent_ref[below + 2 * TILE * i : below + 2 * TILE * i + lines, :main] = term[:, :main]
        if width > main:
            sent_ref[below + 2 * TILE * i : below + 2 * TILE * i + lines, main:width] = term[:, main:]

    @pl.when(chip_of() > 0)
    def _():
        for l in range(lines):
            active = [act_ref[g, l : l + 1, :] for g in range(depth)]
            steps = [[-x for x in pair_at(q_ref, width, 0, l)]]
            for g in range(1, depth - 1):
                steps.append(split2(-product(steps[-1], pair_at(q_ref, width, g, l))))
            each = lines // parts
            value = [
                (active[depth - 1] * x.astype(F32)).astype(BF16)
                for x in pair_at(whole_refs[l // each], width, l % each)
            ]
            for g in range(depth - 2, -1, -1):
                reach = steps[g][0].astype(F32) + steps[g][1].astype(F32)
                total = active[g] * (reach - product(value, pair_at(s_ref, width, g, l)))
                value = split2(total)
            pair = value
            store_pair(out_ref, pair, l)
            store_pair(sent_ref, pair, l)


def hop_kernel(came_ref, act_ref, local_ref, idle_ref, *refs, chip):
    pair_refs, out_ref = refs[:-1], refs[-1]
    out_ref[...] = idle_ref[...]

    @pl.when(jnp.logical_and(chip_of() == chip, core_of() == 1))
    def _():
        gone = apply_pairs(came_ref[...], pair_refs)
        out_ref[...] = act_ref[act_ref.shape[0] - 1] * gone + local_ref[...]


def early_hop_kernel(came_ref, act_ref, mate_ref, y_ref, *refs, chip, parts):
    got_refs, own_refs, out_ref = refs[:parts], refs[parts : 2 * parts], refs[-1]
    depth = y_ref.shape[0]
    out_ref[...] = came_ref[...]

    @pl.when(jnp.logical_and(chip_of() == chip, core_of() == 1))
    def _():
        middle = apply_pairs(came_ref[...], got_refs) + mate_ref[...]
        out_ref[...] = act_ref[depth - 1] * apply_pairs(middle, own_refs) + y_ref[depth - 1]


def chosen_arrival(refs, chips, like):
    here = chip_of()
    value = jnp.zeros(like, F32)
    for ref, chip in zip(refs, chips):
        value = jnp.where(here == chip, ref[...], value)
    return value


def choose_kernel(*refs, chips):
    refs[-1][...] = chosen_arrival(refs[:-1], chips, refs[-1].shape)


def turn_kernel(enter_ref, came_ref, echo_ref, got_c, got_d, own_d, *refs, parts, chips, fill):
    got_refs, (enter_y, mid_ref, out_ref) = refs[:parts], refs[-3:]
    inside = jnp.logical_and(chip_of() >= chips[0], chip_of() < chips[1])
    if not fill:
        for held, ref in zip(refs[parts:], refs[-3:]):
            ref[...] = held[...]
    if fill:

        @pl.when(jnp.logical_not(inside))
        def _():
            enter_y[...] = enter_ref[...]
            mid_ref[...] = echo_ref[...]
            out_ref[...] = echo_ref[...]

    @pl.when(jnp.logical_and(inside, core_of() == 1))
    def _():
        enter = enter_ref[...]
        leave = apply_pairs(enter, got_refs) + came_ref[...]
        middle = apply_pairs(leave, own_d) + echo_ref[...]
        lines, width = enter.shape
        below = lines * room_of(width)[0]
        first = apply_pairs(enter, got_d)
        for i in range(3):
            first = first + got_d[below + 2 * TILE * i : below + 2 * TILE * i + lines, :width].astype(F32)
        enter_y[...] = leave
        mid_ref[...] = middle
        out_ref[...] = apply_pairs(middle, got_c) + first


def send_kernel(x_ref, enter_ref, out_ref, *, last):
    out_ref[...] = jnp.where(chip_of() == last, x_ref[...], enter_ref[...])


def steps_kernel(flow_ref, scaled_ref, q_ref, act_ref, held_ref, y_ref, *, late):
    depth = scaled_ref.shape[0]
    here, core = chip_of(), core_of()
    y_ref[...] = held_ref[...]
    if late:
        inside = jnp.logical_and(core == 0, here > 1)
    else:
        inside = jnp.logical_and(here > 0, jnp.logical_or(core == 1, here == 1))

    @pl.when(inside)
    def _():
        values = forward_local([scaled_ref[g] for g in range(depth)], q_ref, act_ref, flow_ref[...])
        for g in range(depth):
            y_ref[g] = values[g]


def entry_kernel(own_ref, came_ref, out_ref):
    out_ref[...] = jnp.where(core_of() == 1, own_ref[...], came_ref[...])


def leave_kernel(own_ref, first_ref, *refs, chips):
    came_ref, out_ref = refs[-2:]
    came_ref[...] = chosen_arrival(refs[:-2], chips, came_ref.shape)
    out_ref[...] = first_ref[...]

    @pl.when(jnp.logical_and(core_of() == 1, chip_of() > 0))
    def _():
        out_ref[...] = apply_pairs(came_ref[...], own_ref) + first_ref[...]


def wall_middle_kernel(came_ref, got_c, got_d, out_ref):
    @pl.when(lax.axis_index("wall") == 0)
    def _():
        lines, width = came_ref.shape
        below = lines * room_of(width)[0]
        value = apply_pairs(came_ref[...], got_c)
        for i in range(3):
            value = value + got_d[below + 2 * TILE * i : below + 2 * TILE * i + lines, :width].astype(F32)
        out_ref[...] = value


def last_kernel(beyond_ref, met_ref, middle_ref, wall_ref, s_ref, act_ref, y_ref, out_ref):
    depth = y_ref.shape[0]
    core, chip = core_of(), chip_of()
    first = jnp.where(chip == 0, middle_ref[...], met_ref[...])
    second = jnp.where(chip == 0, wall_ref[...], beyond_ref[...])
    solved = backward_local(
        [y_ref[g] for g in range(depth)], s_ref, act_ref, jnp.where(core == 0, first, second)
    )
    for g in range(depth):
        out_ref[g] = solved[g]


def padded_bytes(shape, dtype):
    size = jnp.dtype(dtype).itemsize
    shape = (1,) * (2 - len(shape)) + tuple(shape)
    total = -(-shape[-2] // 16) * 16 * -(-shape[-1] // 128) * 128 * size
    for extent in shape[:-2]:
        total *= extent
    return total


def run(kernel, operands, outs, blocks=1, scratch=(), aliases=None):
    held = [(x.shape, x.dtype) for x, _ in operands] + [(s, t) for s, t, _ in outs]
    limit = sum(padded_bytes(s, t) for s, t in held)
    if blocks == 1:
        in_specs = [at if isinstance(at, pl.BlockSpec) else VMEM for _, at in operands]
        out_specs = [VMEM for _ in outs]
        grid = ()
    else:

        def spec(shape, at):
            if isinstance(at, pl.BlockSpec):
                return at
            if at is None:
                return pl.BlockSpec(shape, lambda i: (0,) * len(shape))
            size = tuple(n // blocks if axis == at else n for axis, n in enumerate(shape))
            return pl.BlockSpec(size, lambda i: tuple(i if axis == at else 0 for axis in range(len(shape))))

        in_specs = [spec(x.shape, at) for x, at in operands]
        out_specs = [spec(s, at) for s, _, at in outs]
        grid = (blocks,)
        limit = 2 * limit // blocks
    limit += sum(padded_bytes(s.shape, s.dtype) for s in scratch if s.memory_space == pltpu.VMEM)
    limit = min(limit + (2 << 20), 60 << 20)
    return pl.pallas_call(
        kernel,
        grid=grid,
        in_specs=in_specs,
        out_specs=out_specs,
        out_shape=[jax.ShapeDtypeStruct(s, t) for s, t, _ in outs],
        scratch_shapes=list(scratch),
        input_output_aliases=aliases or {},
        compiler_params=pltpu.CompilerParams(vmem_limit_bytes=limit),
        cost_estimate=pl.CostEstimate(flops=1, bytes_accessed=1, transcendentals=0),
    )(*[x for x, _ in operands])


def hop_pairs(count, start, end, core=1, relay=None):
    start, end = 2 * start + 1, 2 * end + core
    target = {i: i ^ 1 for i in range(count)}
    cycle = [start, end, end ^ 1, start ^ 1]
    if relay is not None:
        cycle[3:3] = [2 * relay, 2 * relay + 1]
    target.update(zip(cycle, cycle[1:] + cycle[:1]))
    return sorted(target.items())


def in_hbm(value):
    return pltpu.with_memory_space_constraint(value, pltpu.HBM)


def after(value, *others):
    return lax.optimization_barrier((value, *others))[0]


def per_device(state, source, face_coef, neighbour, lift, elem_slot, line_len, dinv, lower, upper):
    wall_count = lax.axis_size("wall")
    surf_count = lax.axis_size("surf")
    last = wall_count // 2 - 1
    depth, lines, width, _ = dinv.shape
    slots = state.shape[0]
    block = TILE if lines % TILE == 0 else lines
    blocks = lines // block
    parts = 1
    room, columns, _ = room_of(width)
    line_vector = ((lines, width), F32, 0)
    element_vectors = ((depth, lines, width), F32, 1)
    line_sent = ((lines * room, columns), BF16, 0)
    vector_sent = ((lines * room + 6 * TILE * blocks, columns), BF16, 0)
    line_pairs = ((lines, 2, width, width), BF16, 0)
    part_sent = ((lines // parts * room, columns), BF16, 0)
    part_pairs = ((lines // parts, 2, width, width), BF16, 0)
    element_pairs = ((depth, lines, 2, width, width), BF16, 1)

    def mates(value):
        return lax.ppermute(value, "wall", [(i, i ^ 1) for i in range(wall_count)])

    def relaid(arrays, *others):
        if lines != TILE:
            return jnp.stack(arrays)
        shape = (len(arrays), depth, lines, width, width)
        return run(
            functools.partial(relayout_kernel, kinds=len(arrays)),
            [(in_hbm(jnp.transpose(x, (0, 2, 1, 3))), ANY) for x in arrays] + [(x, None) for x in others],
            [(shape, BF16, None)],
            scratch=[
                pltpu.VMEM((len(arrays), depth, width, lines, width), BF16),
                pltpu.SemaphoreType.DMA((len(arrays), depth)),
            ],
        )[0]

    count = depth * lines
    small = (elem_slot, line_len, face_coef.T, neighbour.T, source)
    in_place = lines == TILE
    blocks_in = [in_hbm(jnp.transpose(x, (0, 2, 1, 3))) for x in (dinv, lower, upper)] if in_place else []
    weight, line_source, act, near_state, near_lift, *landed = run(
        functools.partial(prepare_kernel, taken=2 if in_place else 0),
        [(in_hbm(x), ANY) for x in (*small, state, lift)] + [(x, ANY) for x in blocks_in[:2]],
        [
            ((3 * count, 3 * slots), BF16, None),
            ((count, width), F32, None),
            element_vectors,
            (state.shape, BF16, None),
            (lift.shape, BF16, None),
        ]
        + ([((2, depth, lines, width, width), BF16, None)] if in_place else []),
        scratch=[(pltpu.SMEM if i < 2 else pltpu.VMEM)(x.shape, x.dtype) for i, x in enumerate(small)]
        + [pltpu.SemaphoreType.DMA((len(small) + 2,))]
        + (
            [pltpu.VMEM((2, depth, width, lines, width), BF16), pltpu.SemaphoreType.DMA((2, depth))]
            if in_place
            else []
        ),
    )
    before = lax.ppermute(state, "surf", [(i, (i + 1) % surf_count) for i in range(surf_count)])
    beyond = lax.ppermute(state, "surf", [((i + 1) % surf_count, i) for i in range(surf_count)])
    cells = [(x, None) for x in (before, near_state, beyond, weight, line_source, near_lift)]
    raw = landed[0] if in_place else jnp.stack([dinv, lower, upper])
    vectors = [element_vectors, element_vectors, line_vector]
    if in_place:
        scaled, y_local, y_leave, first_lower = run(
            functools.partial(local_kernel, merged=True),
            cells + [(raw, None), (act, None), (blocks_in[1], ANY)],
            vectors + [((1, 1, width, lines, width), BF16, None)],
            scratch=[pltpu.SemaphoreType.DMA(())],
        )
    else:
        (rhs,) = run(residual_kernel, cells, [element_vectors])
        scaled, y_local, y_leave = run(
            functools.partial(local_kernel, merged=False), [(rhs, 1), (raw, 2), (act, 1)], vectors, blocks
        )
    came_y = mates(y_leave)
    q, *rest = run(
        functools.partial(
            pair_kernel, first_chip=1, fetch=in_place, turn=False, kind=1, lines=(0, block), ascending=True
        ),
        [(after(raw, y_leave), 2)]
        + ([(blocks_in[2], ANY), (first_lower, None)] if in_place else []),
        [element_pairs, line_pairs, line_sent]
        + (
            [((1, depth, width, lines, width), BF16, None), ((1, 1, lines, width, width), BF16, None)]
            if in_place
            else []
        ),
        blocks,
        [pltpu.SemaphoreType.DMA((depth,))] if in_place else [],
    )
    wall_y, wall_leave = run(
        wall_kernel,
        [(came_y, 0), (scaled, 1), (raw, 2), (act, 1), (y_local, 1)] + [(x, 2) for x in rest[3:]],
        [element_vectors, line_vector],
        blocks,
    )
    arrivals = [lax.ppermute(wall_leave, "wall", hop_pairs(wall_count, 0, 1))]
    a, got_a = [rest[0]], [mates(after(rest[1], came_y))]
    s, c, sent_c = run(
        functools.partial(
            pair_kernel, first_chip=0, fetch=False, turn=in_place, kind=2, lines=(0, block), ascending=False
        ),
        [(after(raw, a[-1], wall_leave), 2)] + ([(rest[2], None)] if in_place else []),
        [element_pairs, line_pairs, line_sent],
        blocks,
        [pltpu.VMEM((1, depth, lines, width, width), BF16)] if in_place else [],
    )
    got_c = mates(after(sent_c, arrivals[0],got_a[-1]))

    def hop(came, pairs, local, idle, at):
        (out,) = run(
            functools.partial(hop_kernel, chip=at),
            [(came, 0), (act, 1), (local, 0), (idle, 0)] + [(x, 0) for x in pairs],
            [line_vector],
            blocks,
        )
        return out

    out = wall_leave
    for at in range(1, last):
        if at == 1:
            (out,) = run(
                functools.partial(early_hop_kernel, chip=at, parts=parts),
                [(arrivals[-1], 0), (act, 1), (came_y, 0), (y_local, 1)] + [(x, 0) for x in got_a + a],
                [line_vector],
                blocks,
            )
            (chip_a,) = run(
                functools.partial(chip_kernel, parts=parts, width=width, own_first=False, chips=(2, last)),
                [(after(x, out) if i == 0 else x, 0) for i, x in enumerate(got_a + a)],
                [line_pairs],
                blocks,
            )
            (y_chip,) = run(
                functools.partial(chip_local_kernel, chips=(2, last)),
                [(after(came_y, out), 0), (act, 1), (y_local, 1)] + [(x, 0) for x in a],
                [line_vector],
                blocks,
            )
            through, sent_d, echo = run(
                functools.partial(through_kernel, parts=parts),
                [(act, 1), (after(q, out, chip_a, y_chip), 1), (s, 1), (wall_y, 1)] + [(x, 0) for x in a],
                [line_pairs, vector_sent, line_vector],
                blocks,
            )
        else:
            out = hop(arrivals[-1], [chip_a], y_chip, y_chip, at)
        pairs = hop_pairs(wall_count, at, at + 1, relay={1: 0}.get(at))
        arrivals.append(lax.ppermute(out, "wall", pairs))
        if at == 1:
            got_d = mates(after(sent_d, got_c, arrivals[-1]))

    def chosen(arrived, chips):
        return run(
            functools.partial(choose_kernel, chips=chips), [(x, 0) for x in arrived], [line_vector], blocks
        )[0]

    def turn(first_chip, end_chip, entered, held=()):
        return run(
            functools.partial(turn_kernel, parts=parts, chips=(first_chip, end_chip), fill=not held),
            [(x, 0) for x in (entered, came_y, echo, got_c, got_d, through, *got_a)]
            + [(x, 0) for x in held],
            [line_vector] * 3,
            blocks,
        )

    def steps(late, flow, held):
        return run(
            functools.partial(steps_kernel, late=late),
            [(flow, 0)] + [(x, 1) for x in (scaled, q, act, held)],
            [element_vectors],
            blocks,
        )

    (chip_c,) = run(
        functools.partial(chip_kernel, parts=1, width=width, own_first=True, chips=(1, last)),
        [(after(got_c, out), 0), (c, 0)],
        [line_pairs],
        blocks,
    )
    arrivals[-1] = after(arrivals[-1], chip_c)
    held = turn(last, last + 1, arrivals[-1])
    entered = chosen(arrivals, list(range(1, last + 1)))
    x_chip = held[-1]
    (out,) = run(functools.partial(send_kernel, last=last), [(x_chip, 0), (entered, 0)], [line_vector], blocks)
    arrived = [lax.ppermute(out, "wall", hop_pairs(wall_count, last, last - 1))]
    held = turn(last - 1, last, after(entered, out), held)
    x_chip = held[-1]
    enter_y, middle, _ = held
    y = wall_y
    for at in range(last - 1, 0, -1):
        came = arrived[-1]
        if at == last - 2:
            enter_y, middle, x_chip = turn(1, last - 1, after(entered, out), held)
        if at == 1:
            (flow,) = run(entry_kernel, [(enter_y, 0), (after(arrived[0], out), 0)], [line_vector], blocks)
            (y,) = steps(False, flow, wall_y)
            came = after(came, y)
        out = hop(came, [chip_c], x_chip, entered, at)
        arrived.append(lax.ppermute(out, "wall", hop_pairs(wall_count, at, at - 1, int(at > 1))))
    wall = lax.ppermute(out, "wall", hop_pairs(wall_count, 1, 0))
    beyond, left = run(
        functools.partial(leave_kernel, chips=list(range(last - 1, 0, -1))),
        [(x, 0) for x in (c, middle, *arrived[:-1])],
        [line_vector, line_vector],
        blocks,
    )
    met_left = mates(after(left, out))
    (y,) = steps(True, arrived[-1], y)
    (wall_middle,) = run(
        wall_middle_kernel, [(after(arrived[-1], wall), 0), (got_c, 0), (got_d, 0)], [line_vector], blocks
    )
    (solution,) = run(
        last_kernel,
        [(beyond, 0), (met_left, 0), (wall_middle, 0), (wall, 0)] + [(x, 1) for x in (s, act, y)],
        [element_vectors],
        blocks,
    )
    return solution


def solution(mesh):
    in_specs = (
        P(("wall", "surf"), None),
        P(("wall", "surf"), None),
        P(("wall", "surf"), None),
        P(("wall", "surf"), None),
        P(),
        P("wall", "surf"),
        P("surf"),
        P("wall", "surf", None, None),
        P("wall", "surf", None, None),
        P("wall", "surf", None, None),
    )
    out_specs = P("wall", "surf", None)
    return jax.shard_map(
        per_device, mesh=mesh, in_specs=in_specs, out_specs=out_specs, check_vma=False
    )
```

```python
import functools

import jax
import jax.numpy as jnp
from jax import lax
from jax.experimental import pallas as pl
from jax.experimental.pallas import tpu as pltpu
from jax.sharding import PartitionSpec as P

F32 = jnp.float32
BF16 = jnp.bfloat16
TILE = 8
LANES = 128
VMEM = pl.BlockSpec(memory_space=pltpu.VMEM)
ANY = pl.BlockSpec(memory_space=pl.ANY)
SMEM = pl.BlockSpec(memory_space=pltpu.SMEM)


def split2(x):
    high = x.astype(BF16)
    return high, (x - high.astype(F32)).astype(BF16)


def product(x, y):
    dot = functools.partial(jnp.dot, preferred_element_type=F32)
    return dot(x[0], y[0]) + (dot(x[0], y[1]) + dot(x[1], y[0]))


def room_of(width):
    rows = -(-width // (2 * TILE)) * 2 * TILE
    main = width // LANES * LANES
    return rows, 2 * main + (LANES if width - main <= LANES // 2 else 2 * LANES), main


def pair_at(ref, width, *at):
    if len(ref.shape) > 2:
        return [ref[(*at, i)] for i in range(2)]
    rows, columns, main = room_of(width)
    here = pl.ds(at[0] * rows, width)
    step = (columns - 2 * main) // 2
    if width == main:
        return [ref[here, i * main : (i + 1) * main] for i in range(2)]
    return [
        jnp.concatenate(
            [
                ref[here, i * main : (i + 1) * main],
                ref[here, 2 * main + i * step : 2 * main + i * step + width - main],
            ],
            axis=1,
        )
        for i in range(2)
    ]


def store_pair(ref, pair, *at):
    if len(ref.shape) > 2:
        for i in range(2):
            ref[(*at, i)] = pair[i]
        return
    width = pair[0].shape[0]
    rows, columns, main = room_of(width)
    here = pl.ds(at[0] * rows, width)
    step = (columns - 2 * main) // 2
    for i in range(2):
        ref[here, i * main : (i + 1) * main] = pair[i][:, :main]
        if width > main:
            ref[here, 2 * main + i * step : 2 * main + i * step + width - main] = pair[i][:, main:]


def apply_pairs(vector, ref, *at):
    count = vector.shape[0]
    rows = lax.broadcasted_iota(jnp.int32, vector.shape, 0)
    both = jnp.concatenate(split2(vector), axis=0)
    total = jnp.zeros(vector.shape, F32)
    for l in range(count):
        part, here = ref, l
        if isinstance(ref, (list, tuple)):
            each = count // len(ref)
            part, here = ref[l // each], l % each
        high, low = pair_at(part, vector.shape[1], *at, here)
        first = jnp.dot(both, high, preferred_element_type=F32)
        second = jnp.dot(both, low, preferred_element_type=F32)
        total = jnp.where(rows == l, first[:count] + first[count:] + second[:count], total)
    return total


def apply_rows(vector, ref, *at):
    count = vector.shape[0]
    rows = lax.broadcasted_iota(jnp.int32, vector.shape, 0)
    both = jnp.concatenate(split2(vector), axis=0)
    total = jnp.zeros(vector.shape, F32)
    for l in range(count):
        first = lax.dot_general(
            both, ref[(*at, l)], (((1,), (1,)), ((), ())), preferred_element_type=F32
        )
        total = jnp.where(rows == l, first[:count] + first[count:], total)
    return total


def core_of():
    return lax.rem(lax.axis_index("wall"), 2)


def chip_of():
    return lax.div(lax.axis_index("wall"), 2)


def between(chips, core):
    inside = jnp.logical_and(chip_of() >= chips[0], chip_of() < chips[1])
    return jnp.logical_and(inside, core_of() == core)


def pair_kernel(raw_ref, *refs, first_chip, fetch, turn, **options):
    if fetch:
        next_ref, landed_ref, *outs, landed, turned_ref, arrived = refs
        copies = [
            pltpu.make_async_copy(next_ref.at[e], landed.at[0, e], arrived.at[e]) for e in range(next_ref.shape[0])
        ]
        for copy in copies:
            copy.start()
        turn_blocks(landed_ref, 0, 0, turned_ref)
    elif turn:
        landed_ref, *outs, turned_ref = refs
        for e in range(raw_ref.shape[1]):
            turn_blocks(landed_ref, 0, e, turned_ref)
    else:
        outs = refs

    def other(e, l):
        if turn or (fetch and e == 0):
            return turned_ref[0, e, l]
        return raw_ref[options["kind"], e, l]

    @pl.when(chip_of() >= first_chip)
    def _():
        make_pairs(raw_ref, other, *outs, lines=options["lines"], ascending=options["ascending"])

    if fetch:
        for copy in copies:
            copy.wait()


def make_pairs(raw_ref, other, step_ref, whole_ref, sent_ref, *, lines, ascending):
    count, width = raw_ref.shape[1], raw_ref.shape[3]
    for l in range(*lines):
        for e in range(count):
            block = lax.dot_general(
                other(e, l), raw_ref[0, e, l], (((0,), (1,)), ((), ())), preferred_element_type=F32
            )
            store_pair(step_ref, split2(block), e, l)
    order = list(range(count)) if ascending else list(range(count))[::-1]
    for l in range(*lines):
        whole = pair_at(step_ref, width, order[0], l)
        for e in order[1:]:
            whole = split2(product(whole, pair_at(step_ref, width, e, l)))
        if count % 2:
            whole = [-x for x in whole]
        store_pair(whole_ref, whole, l - lines[0])
        store_pair(sent_ref, whole, l - lines[0])


def chip_kernel(*refs, parts, width, own_first, chips):
    got_refs, own_refs, chip_ref = refs[:parts], refs[parts:-1], refs[-1]

    @pl.when(between(chips, 1))
    def _():
        each = chip_ref.shape[0] // parts
        for l in range(chip_ref.shape[0]):
            pairs = [pair_at(x[l // each], width, l % each) for x in (got_refs, own_refs)]
            store_pair(chip_ref, split2(product(*(pairs[::-1] if own_first else pairs))), l)


def turn_blocks(landed_ref, a, e, raw_ref):
    turned = jnp.swapaxes(landed_ref[a, e], 0, 1)
    for l in range(raw_ref.shape[2]):
        raw_ref[a, e, l] = turned[l]


def prepare_kernel(*refs, taken):
    blocks = refs[7 : 7 + taken]
    places, (weight_ref, rhs_ref, act_ref, state_ref, lift_ref) = refs[:7], refs[7 + taken : 12 + taken]
    slot_ref, len_ref, coef_ref, nb_ref, source_ref, arrived = refs[12 + taken + (taken > 0) :][:6]
    targets = (slot_ref, len_ref, coef_ref, nb_ref, source_ref, state_ref, lift_ref)
    copies = [
        pltpu.make_async_copy(there, here, arrived.at[i]) for i, (there, here) in enumerate(zip(places, targets))
    ]
    block_copies = []
    if taken:
        raw_ref, landed, landed_at = refs[12 + taken], refs[-2], refs[-1]
        places_in = [(a, e) for a in range(taken) for e in range(landed.shape[1]) if (a, e) != (1, 0)]
        block_copies = [
            pltpu.make_async_copy(blocks[a].at[e], landed.at[a, e], landed_at.at[a, e]) for a, e in places_in
        ]
    for copy in copies + block_copies:
        copy.start()
    for copy in copies:
        copy.wait()
    faces, slots = coef_ref.shape
    depth, lines = slot_ref.shape
    cells = 3 * slots
    k = lax.broadcasted_iota(jnp.int32, (cells, slots), 0)
    e = lax.broadcasted_iota(jnp.int32, (cells, slots), 1)
    weight = jnp.zeros((cells, slots), F32)
    own = jnp.zeros((1, slots), F32)
    for f in range(faces):
        coef = coef_ref[f : f + 1, :]
        own = own + coef
        weight = weight - jnp.where(k == nb_ref[f : f + 1, :], coef, 0.0)
    weight = weight + jnp.where(k == e + slots, own, 0.0)
    count = depth * lines
    rows = lax.broadcasted_iota(jnp.int32, (count, slots), 0)
    slot = jnp.zeros((count, slots), jnp.int32)
    for g in range(depth):
        for l in range(lines):
            slot = jnp.where(rows == g * lines + l, slot_ref[g, l], slot)
    chosen = (slot == lax.broadcasted_iota(jnp.int32, (count, slots), 1)).astype(F32).astype(BF16)
    high = weight.astype(BF16)
    mid, low = split2(weight - high.astype(F32))
    for i, part in enumerate((high, mid, low)):
        weight_ref[i * count : (i + 1) * count, :] = lax.dot_general(
            chosen, part, (((1,), (1,)), ((), ())), preferred_element_type=F32
        ).astype(BF16)
    rhs_ref[...] = jnp.dot(chosen, source_ref[...], preferred_element_type=F32)
    rows = lax.broadcasted_iota(jnp.int32, act_ref.shape[1:], 0)
    length = jnp.zeros(act_ref.shape[1:], jnp.int32)
    for l in range(lines):
        length = jnp.where(rows == l, len_ref[l], length)
    place = lax.axis_index("wall") * depth
    for g in range(depth):
        act_ref[g] = (place + g < length).astype(F32)
    for i, copy in enumerate(block_copies):
        copy.wait()
        turn_blocks(landed, *places_in[i], raw_ref)


def copy_kernel(here, _, there):
    there[...] = here[...]


def residual(before, state, after, weight, source, lift, depth):
    cells = jnp.concatenate([before[...], state[...], after[...]], axis=0)
    parts = jnp.dot(weight[...], cells, preferred_element_type=F32)
    count = source.shape[0]
    face_sum = parts[:count] + (parts[count : 2 * count] + parts[2 * count :])
    flux = jnp.dot(face_sum.astype(BF16), lift[...], preferred_element_type=F32)
    rhs = source[...] - flux
    lines = count // depth
    return [rhs[g * lines : (g + 1) * lines] for g in range(depth)]


def residual_kernel(before, state, after, weight, source, lift, rhs_ref):
    for g, rhs in enumerate(residual(before, state, after, weight, source, lift, rhs_ref.shape[0])):
        rhs_ref[g] = rhs


def forward_local(scaled, q_ref, act_ref, carried):
    values = []
    for g, value in enumerate(scaled):
        if carried is not None:
            value = value - apply_pairs(carried, q_ref, g)
        carried = act_ref[g] * value
        values.append(carried)
    return values


def backward_local(values, s_ref, act_ref, carried):
    solved = [None] * len(values)
    for g in range(len(values) - 1, -1, -1):
        value = values[g]
        if carried is not None:
            value = value - apply_pairs(carried, s_ref, g)
        carried = act_ref[g] * value
        solved[g] = carried
    return solved


def local_kernel(*refs, merged):
    if merged:
        *cells, raw_ref, act_ref, lower_in, scaled_ref, y_ref, leave_ref, landed_ref, arrived = refs
        copy = pltpu.make_async_copy(lower_in.at[0], landed_ref.at[0, 0], arrived)
        copy.start()
        rhs = residual(*cells, scaled_ref.shape[0])
    else:
        rhs_ref, raw_ref, act_ref, scaled_ref, y_ref, leave_ref = refs
        rhs = [rhs_ref[g] for g in range(rhs_ref.shape[0])]
    depth = len(rhs)
    scaled = [apply_rows(rhs[g], raw_ref, 0, g) for g in range(depth)]
    values = raw_steps(scaled, raw_ref, None, act_ref, None)
    for g in range(depth):
        scaled_ref[g] = scaled[g]
        y_ref[g] = values[g]
    leave_ref[...] = values[-1]
    if merged:
        copy.wait()


def raw_steps(scaled, raw_ref, first_ref, act_ref, carried):
    values = []
    for g, value in enumerate(scaled):
        if carried is not None:
            at = (first_ref, 0, 0) if first_ref is not None and g == 0 else (raw_ref, 1, g)
            value = value - apply_rows(apply_rows(carried, *at), raw_ref, 0, g)
        carried = act_ref[g] * value
        values.append(carried)
    return values


def wall_kernel(came_ref, scaled_ref, raw_ref, act_ref, y_ref, *refs):
    out_ref, leave_ref = refs[-2:]
    first_ref = refs[0] if len(refs) > 2 else None
    depth = y_ref.shape[0]
    out_ref[...] = y_ref[...]
    leave_ref[...] = y_ref[depth - 1]

    @pl.when(lax.axis_index("wall") == 1)
    def _():
        values = raw_steps([scaled_ref[g] for g in range(depth)], raw_ref, first_ref, act_ref, came_ref[...])
        for g in range(depth):
            out_ref[g] = values[g]
        leave_ref[...] = values[-1]


def chip_local_kernel(came_ref, act_ref, y_ref, *refs, chips):
    own_refs, out_ref = refs[:-1], refs[-1]
    depth = y_ref.shape[0]
    out_ref[...] = y_ref[depth - 1]

    @pl.when(between(chips, 1))
    def _():
        out_ref[...] = act_ref[depth - 1] * apply_pairs(came_ref[...], own_refs) + y_ref[depth - 1]


def three_terms(x):
    high = x.astype(BF16)
    return high, *split2(x - high.astype(F32))


def through_kernel(act_ref, q_ref, s_ref, y_ref, *refs, parts):
    whole_refs, (out_ref, sent_ref, echo_ref) = refs[:parts], refs[parts:]
    depth, lines, _, _, width = q_ref.shape
    main, below = width // LANES * LANES, lines * room_of(width)[0]
    echo = backward_local([y_ref[g] for g in range(depth)], s_ref, act_ref, None)[0]
    echo_ref[...] = echo
    for i, term in enumerate(three_terms(echo)):
        sent_ref[below + 2 * TILE * i : below + 2 * TILE * i + lines, :main] = term[:, :main]
        if width > main:
            sent_ref[below + 2 * TILE * i : below + 2 * TILE * i + lines, main:width] = term[:, main:]

    @pl.when(chip_of() > 0)
    def _():
        for l in range(lines):
            active = [act_ref[g, l : l + 1, :] for g in range(depth)]
            steps = [[-x for x in pair_at(q_ref, width, 0, l)]]
            for g in range(1, depth - 1):
                steps.append(split2(-product(steps[-1], pair_at(q_ref, width, g, l))))
            each = lines // parts
            value = [
                (active[depth - 1] * x.astype(F32)).astype(BF16)
                for x in pair_at(whole_refs[l // each], width, l % each)
            ]
            for g in range(depth - 2, -1, -1):
                reach = steps[g][0].astype(F32) + steps[g][1].astype(F32)
                total = active[g] * (reach - product(value, pair_at(s_ref, width, g, l)))
                value = split2(total)
            pair = value
            store_pair(out_ref, pair, l)
            store_pair(sent_ref, pair, l)


def hop_kernel(came_ref, act_ref, local_ref, idle_ref, *refs, chip):
    pair_refs, out_ref = refs[:-1], refs[-1]
    out_ref[...] = idle_ref[...]

    @pl.when(jnp.logical_and(chip_of() == chip, core_of() == 1))
    def _():
        gone = apply_pairs(came_ref[...], pair_refs)
        out_ref[...] = act_ref[act_ref.shape[0] - 1] * gone + local_ref[...]


def early_hop_kernel(came_ref, act_ref, mate_ref, y_ref, *refs, chip, parts):
    got_refs, own_refs, out_ref = refs[:parts], refs[parts : 2 * parts], refs[-1]
    depth = y_ref.shape[0]
    out_ref[...] = came_ref[...]

    @pl.when(jnp.logical_and(chip_of() == chip, core_of() == 1))
    def _():
        middle = apply_pairs(came_ref[...], got_refs) + mate_ref[...]
        out_ref[...] = act_ref[depth - 1] * apply_pairs(middle, own_refs) + y_ref[depth - 1]


def chosen_arrival(refs, chips, like):
    here = chip_of()
    value = jnp.zeros(like, F32)
    for ref, chip in zip(refs, chips):
        value = jnp.where(here == chip, ref[...], value)
    return value


def choose_kernel(*refs, chips):
    refs[-1][...] = chosen_arrival(refs[:-1], chips, refs[-1].shape)


def turn_kernel(enter_ref, came_ref, echo_ref, got_c, got_d, own_d, *refs, parts, chips, fill):
    got_refs, (enter_y, mid_ref, out_ref) = refs[:parts], refs[-3:]
    inside = jnp.logical_and(chip_of() >= chips[0], chip_of() < chips[1])
    if not fill:
        for held, ref in zip(refs[parts:], refs[-3:]):
            ref[...] = held[...]
    if fill:

        @pl.when(jnp.logical_not(inside))
        def _():
            enter_y[...] = enter_ref[...]
            mid_ref[...] = echo_ref[...]
            out_ref[...] = echo_ref[...]

    @pl.when(jnp.logical_and(inside, core_of() == 1))
    def _():
        enter = enter_ref[...]
        leave = apply_pairs(enter, got_refs) + came_ref[...]
        middle = apply_pairs(leave, own_d) + echo_ref[...]
        lines, width = enter.shape
        below = lines * room_of(width)[0]
        first = apply_pairs(enter, got_d)
        for i in range(3):
            first = first + got_d[below + 2 * TILE * i : below + 2 * TILE * i + lines, :width].astype(F32)
        enter_y[...] = leave
        mid_ref[...] = middle
        out_ref[...] = apply_pairs(middle, got_c) + first


def send_kernel(x_ref, enter_ref, out_ref, *, last):
    out_ref[...] = jnp.where(chip_of() == last, x_ref[...], enter_ref[...])


def steps_kernel(flow_ref, scaled_ref, q_ref, act_ref, held_ref, y_ref, *, late):
    depth = scaled_ref.shape[0]
    here, core = chip_of(), core_of()
    y_ref[...] = held_ref[...]
    if late:
        inside = jnp.logical_and(core == 0, here > 1)
    else:
        inside = jnp.logical_and(here > 0, jnp.logical_or(core == 1, here == 1))

    @pl.when(inside)
    def _():
        values = forward_local([scaled_ref[g] for g in range(depth)], q_ref, act_ref, flow_ref[...])
        for g in range(depth):
            y_ref[g] = values[g]


def entry_kernel(own_ref, came_ref, out_ref):
    out_ref[...] = jnp.where(core_of() == 1, own_ref[...], came_ref[...])


def leave_kernel(own_ref, first_ref, *refs, chips):
    came_ref, out_ref = refs[-2:]
    came_ref[...] = chosen_arrival(refs[:-2], chips, came_ref.shape)
    out_ref[...] = first_ref[...]

    @pl.when(jnp.logical_and(core_of() == 1, chip_of() > 0))
    def _():
        out_ref[...] = apply_pairs(came_ref[...], own_ref) + first_ref[...]


def wall_middle_kernel(came_ref, got_c, got_d, out_ref):
    @pl.when(lax.axis_index("wall") == 0)
    def _():
        lines, width = came_ref.shape
        below = lines * room_of(width)[0]
        value = apply_pairs(came_ref[...], got_c)
        for i in range(3):
            value = value + got_d[below + 2 * TILE * i : below + 2 * TILE * i + lines, :width].astype(F32)
        out_ref[...] = value


def last_kernel(beyond_ref, met_ref, middle_ref, wall_ref, s_ref, act_ref, y_ref, out_ref):
    depth = y_ref.shape[0]
    core, chip = core_of(), chip_of()
    first = jnp.where(chip == 0, middle_ref[...], met_ref[...])
    second = jnp.where(chip == 0, wall_ref[...], beyond_ref[...])
    solved = backward_local(
        [y_ref[g] for g in range(depth)], s_ref, act_ref, jnp.where(core == 0, first, second)
    )
    for g in range(depth):
        out_ref[g] = solved[g]


def padded_bytes(shape, dtype):
    size = jnp.dtype(dtype).itemsize
    shape = (1,) * (2 - len(shape)) + tuple(shape)
    total = -(-shape[-2] // 16) * 16 * -(-shape[-1] // 128) * 128 * size
    for extent in shape[:-2]:
        total *= extent
    return total


def run(kernel, operands, outs, blocks=1, scratch=()):
    held = [(x.shape, x.dtype) for x, _ in operands] + [(s, t) for s, t, _ in outs]
    limit = sum(padded_bytes(s, t) for s, t in held)
    if blocks == 1:
        in_specs = [at if isinstance(at, pl.BlockSpec) else VMEM for _, at in operands]
        out_specs = [VMEM for _ in outs]
        grid = ()
    else:

        def spec(shape, at):
            if isinstance(at, pl.BlockSpec):
                return at
            if at is None:
                return pl.BlockSpec(shape, lambda i: (0,) * len(shape))
            size = tuple(n // blocks if axis == at else n for axis, n in enumerate(shape))
            return pl.BlockSpec(size, lambda i: tuple(i if axis == at else 0 for axis in range(len(shape))))

        in_specs = [spec(x.shape, at) for x, at in operands]
        out_specs = [spec(s, at) for s, _, at in outs]
        grid = (blocks,)
        limit = 2 * limit // blocks
    limit += sum(padded_bytes(s.shape, s.dtype) for s in scratch if s.memory_space == pltpu.VMEM)
    limit = min(limit + (2 << 20), 60 << 20)
    return pl.pallas_call(
        kernel,
        grid=grid,
        in_specs=in_specs,
        out_specs=out_specs,
        out_shape=[jax.ShapeDtypeStruct(s, t) for s, t, _ in outs],
        scratch_shapes=list(scratch),
        compiler_params=pltpu.CompilerParams(vmem_limit_bytes=limit),
        cost_estimate=pl.CostEstimate(flops=1, bytes_accessed=1, transcendentals=0),
    )(*[x for x, _ in operands])


def hop_pairs(count, start, end, core=1, relay=None):
    start, end = 2 * start + 1, 2 * end + core
    target = {i: i ^ 1 for i in range(count)}
    cycle = [start, end, end ^ 1, start ^ 1]
    if relay is not None:
        cycle[3:3] = [2 * relay, 2 * relay + 1]
    target.update(zip(cycle, cycle[1:] + cycle[:1]))
    return sorted(target.items())


def in_hbm(value):
    return pltpu.with_memory_space_constraint(value, pltpu.HBM)


def after(value, *others):
    return lax.optimization_barrier((value, *others))[0]


def per_device(state, source, face_coef, neighbour, lift, elem_slot, line_len, dinv, lower, upper):
    wall_count = lax.axis_size("wall")
    surf_count = lax.axis_size("surf")
    last = wall_count // 2 - 1
    depth, lines, width, _ = dinv.shape
    slots = state.shape[0]
    block = TILE if lines % TILE == 0 else lines
    blocks = lines // block
    parts = 1
    room, columns, _ = room_of(width)
    line_vector = ((lines, width), F32, 0)
    element_vectors = ((depth, lines, width), F32, 1)
    line_sent = ((lines * room, columns), BF16, 0)
    vector_sent = ((lines * room + 6 * TILE * blocks, columns), BF16, 0)
    line_pairs = ((lines, 2, width, width), BF16, 0)
    part_sent = ((lines // parts * room, columns), BF16, 0)
    part_pairs = ((lines // parts, 2, width, width), BF16, 0)
    element_pairs = ((depth, lines, 2, width, width), BF16, 1)

    def mates(value):
        return lax.ppermute(value, "wall", [(i, i ^ 1) for i in range(wall_count)])

    def relaid(arrays, *others):
        if lines != TILE:
            return jnp.stack(arrays)
        shape = (len(arrays), depth, lines, width, width)
        return run(
            functools.partial(relayout_kernel, kinds=len(arrays)),
            [(in_hbm(jnp.transpose(x, (0, 2, 1, 3))), ANY) for x in arrays] + [(x, None) for x in others],
            [(shape, BF16, None)],
            scratch=[
                pltpu.VMEM((len(arrays), depth, width, lines, width), BF16),
                pltpu.SemaphoreType.DMA((len(arrays), depth)),
            ],
        )[0]

    count = depth * lines
    small = (elem_slot, line_len, face_coef.T, neighbour.T, source)
    in_place = lines == TILE
    blocks_in = [in_hbm(jnp.transpose(x, (0, 2, 1, 3))) for x in (dinv, lower, upper)] if in_place else []
    weight, line_source, act, near_state, near_lift, *landed = run(
        functools.partial(prepare_kernel, taken=2 if in_place else 0),
        [(in_hbm(x), ANY) for x in (*small, state, lift)] + [(x, ANY) for x in blocks_in[:2]],
        [
            ((3 * count, 3 * slots), BF16, None),
            ((count, width), F32, None),
            element_vectors,
            (state.shape, BF16, None),
            (lift.shape, BF16, None),
        ]
        + ([((2, depth, lines, width, width), BF16, None)] if in_place else []),
        scratch=[(pltpu.SMEM if i < 2 else pltpu.VMEM)(x.shape, x.dtype) for i, x in enumerate(small)]
        + [pltpu.SemaphoreType.DMA((len(small) + 2,))]
        + (
            [pltpu.VMEM((2, depth, width, lines, width), BF16), pltpu.SemaphoreType.DMA((2, depth))]
            if in_place
            else []
        ),
    )
    before = lax.ppermute(state, "surf", [(i, (i + 1) % surf_count) for i in range(surf_count)])
    beyond = lax.ppermute(state, "surf", [((i + 1) % surf_count, i) for i in range(surf_count)])
    (before,) = run(copy_kernel, [(before, None), (weight, None)], [(state.shape, BF16, None)])
    cells = [(x, None) for x in (before, near_state, beyond, weight, line_source, near_lift)]
    raw = landed[0] if in_place else jnp.stack([dinv, lower, upper])
    vectors = [element_vectors, element_vectors, line_vector]
    if in_place:
        scaled, y_local, y_leave, first_lower = run(
            functools.partial(local_kernel, merged=True),
            cells + [(raw, None), (act, None), (blocks_in[1], ANY)],
            vectors + [((1, 1, width, lines, width), BF16, None)],
            scratch=[pltpu.SemaphoreType.DMA(())],
        )
    else:
        (rhs,) = run(residual_kernel, cells, [element_vectors])
        scaled, y_local, y_leave = run(
            functools.partial(local_kernel, merged=False), [(rhs, 1), (raw, 2), (act, 1)], vectors, blocks
        )
    came_y = mates(y_leave)
    q, *rest = run(
        functools.partial(
            pair_kernel, first_chip=1, fetch=in_place, turn=False, kind=1, lines=(0, block), ascending=True
        ),
        [(after(raw, y_leave), 2)]
        + ([(blocks_in[2], ANY), (first_lower, None)] if in_place else []),
        [element_pairs, line_pairs, line_sent]
        + (
            [((1, depth, width, lines, width), BF16, None), ((1, 1, lines, width, width), BF16, None)]
            if in_place
            else []
        ),
        blocks,
        [pltpu.SemaphoreType.DMA((depth,))] if in_place else [],
    )
    wall_y, wall_leave = run(
        wall_kernel,
        [(came_y, 0), (scaled, 1), (raw, 2), (act, 1), (y_local, 1)] + [(x, 2) for x in rest[3:]],
        [element_vectors, line_vector],
        blocks,
    )
    arrivals = [lax.ppermute(wall_leave, "wall", hop_pairs(wall_count, 0, 1))]
    a, got_a = [rest[0]], [mates(after(rest[1], came_y))]
    s, c, sent_c = run(
        functools.partial(
            pair_kernel, first_chip=0, fetch=False, turn=in_place, kind=2, lines=(0, block), ascending=False
        ),
        [(after(raw, a[-1], wall_leave), 2)] + ([(rest[2], None)] if in_place else []),
        [element_pairs, line_pairs, line_sent],
        blocks,
        [pltpu.VMEM((1, depth, lines, width, width), BF16)] if in_place else [],
    )
    got_c = mates(after(sent_c, arrivals[0],got_a[-1]))

    def hop(came, pairs, local, idle, at):
        (out,) = run(
            functools.partial(hop_kernel, chip=at),
            [(came, 0), (act, 1), (local, 0), (idle, 0)] + [(x, 0) for x in pairs],
            [line_vector],
            blocks,
        )
        return out

    out = wall_leave
    for at in range(1, last):
        if at == 1:
            (out,) = run(
                functools.partial(early_hop_kernel, chip=at, parts=parts),
                [(arrivals[-1], 0), (act, 1), (came_y, 0), (y_local, 1)] + [(x, 0) for x in got_a + a],
                [line_vector],
                blocks,
            )
            (chip_a,) = run(
                functools.partial(chip_kernel, parts=parts, width=width, own_first=False, chips=(2, last)),
                [(after(x, out) if i == 0 else x, 0) for i, x in enumerate(got_a + a)],
                [line_pairs],
                blocks,
            )
            (y_chip,) = run(
                functools.partial(chip_local_kernel, chips=(2, last)),
                [(after(came_y, out), 0), (act, 1), (y_local, 1)] + [(x, 0) for x in a],
                [line_vector],
                blocks,
            )
            through, sent_d, echo = run(
                functools.partial(through_kernel, parts=parts),
                [(act, 1), (after(q, out, chip_a, y_chip), 1), (s, 1), (wall_y, 1)] + [(x, 0) for x in a],
                [line_pairs, vector_sent, line_vector],
                blocks,
            )
        else:
            out = hop(arrivals[-1], [chip_a], y_chip, y_chip, at)
        pairs = hop_pairs(wall_count, at, at + 1, relay=0 if at == 1 else None)
        arrivals.append(lax.ppermute(out, "wall", pairs))
        if at == 1:
            got_d = mates(after(sent_d, got_c, arrivals[-1]))

    def chosen(arrived, chips):
        return run(
            functools.partial(choose_kernel, chips=chips), [(x, 0) for x in arrived], [line_vector], blocks
        )[0]

    def turn(first_chip, end_chip, entered, held=()):
        return run(
            functools.partial(turn_kernel, parts=parts, chips=(first_chip, end_chip), fill=not held),
            [(x, 0) for x in (entered, came_y, echo, got_c, got_d, through, *got_a)]
            + [(x, 0) for x in held],
            [line_vector] * 3,
            blocks,
        )

    def steps(late, flow, held):
        return run(
            functools.partial(steps_kernel, late=late),
            [(flow, 0)] + [(x, 1) for x in (scaled, q, act, held)],
            [element_vectors],
            blocks,
        )

    (chip_c,) = run(
        functools.partial(chip_kernel, parts=1, width=width, own_first=True, chips=(1, last)),
        [(after(got_c, out), 0), (c, 0)],
        [line_pairs],
        blocks,
    )
    arrivals[-1] = after(arrivals[-1], chip_c)
    held = turn(last, last + 1, arrivals[-1])
    entered = chosen(arrivals, list(range(1, last + 1)))
    x_chip = held[-1]
    (out,) = run(functools.partial(send_kernel, last=last), [(x_chip, 0), (entered, 0)], [line_vector], blocks)
    arrived = [lax.ppermute(out, "wall", hop_pairs(wall_count, last, last - 1))]
    held = turn(last - 1, last, after(entered, out), held)
    x_chip = held[-1]
    enter_y, middle, _ = held
    y = wall_y
    for at in range(last - 1, 0, -1):
        came = arrived[-1]
        if at == last - 2:
            enter_y, middle, x_chip = turn(1, last - 1, after(entered, out), held)
        if at == 1:
            (flow,) = run(entry_kernel, [(enter_y, 0), (after(arrived[0], out), 0)], [line_vector], blocks)
            (y,) = steps(False, flow, wall_y)
            came = after(came, y)
        out = hop(came, [chip_c], x_chip, entered, at)
        arrived.append(lax.ppermute(out, "wall", hop_pairs(wall_count, at, at - 1, int(at > 1))))
    wall = lax.ppermute(out, "wall", hop_pairs(wall_count, 1, 0))
    beyond, left = run(
        functools.partial(leave_kernel, chips=list(range(last - 1, 0, -1))),
        [(x, 0) for x in (c, middle, *arrived[:-1])],
        [line_vector, line_vector],
        blocks,
    )
    met_left = mates(after(left, out))
    (y,) = steps(True, arrived[-1], y)
    (wall_middle,) = run(
        wall_middle_kernel, [(after(arrived[-1], wall, y), 0), (got_c, 0), (got_d, 0)], [line_vector], blocks
    )
    (solution,) = run(
        last_kernel,
        [(beyond, 0), (met_left, 0), (wall_middle, 0), (wall, 0)] + [(x, 1) for x in (s, act, y)],
        [element_vectors],
        blocks,
    )
    return solution


def solution(mesh):
    in_specs = (
        P(("wall", "surf"), None),
        P(("wall", "surf"), None),
        P(("wall", "surf"), None),
        P(("wall", "surf"), None),
        P(),
        P("wall", "surf"),
        P("surf"),
        P("wall", "surf", None, None),
        P("wall", "surf", None, None),
        P("wall", "surf", None, None),
    )
    out_specs = P("wall", "surf", None)
    return jax.shard_map(
        per_device, mesh=mesh, in_specs=in_specs, out_specs=out_specs, check_vma=False
    )
```

```python
import functools

import jax
import jax.numpy as jnp
from jax import lax
from jax.experimental import pallas as pl
from jax.experimental.pallas import tpu as pltpu
from jax.sharding import PartitionSpec as P

F32 = jnp.float32
BF16 = jnp.bfloat16
TILE = 8
LANES = 128
VMEM = pl.BlockSpec(memory_space=pltpu.VMEM)
ANY = pl.BlockSpec(memory_space=pl.ANY)
SMEM = pl.BlockSpec(memory_space=pltpu.SMEM)


def split2(x):
    high = x.astype(BF16)
    return high, (x - high.astype(F32)).astype(BF16)


def product(x, y):
    dot = functools.partial(jnp.dot, preferred_element_type=F32)
    return dot(x[0], y[0]) + (dot(x[0], y[1]) + dot(x[1], y[0]))


def room_of(width):
    rows = -(-width // (2 * TILE)) * 2 * TILE
    main = width // LANES * LANES
    return rows, 2 * main + (LANES if width - main <= LANES // 2 else 2 * LANES), main


def pair_at(ref, width, *at):
    if len(ref.shape) > 2:
        return [ref[(*at, i)] for i in range(2)]
    rows, columns, main = room_of(width)
    here = pl.ds(at[0] * rows, width)
    step = (columns - 2 * main) // 2
    if width == main:
        return [ref[here, i * main : (i + 1) * main] for i in range(2)]
    return [
        jnp.concatenate(
            [
                ref[here, i * main : (i + 1) * main],
                ref[here, 2 * main + i * step : 2 * main + i * step + width - main],
            ],
            axis=1,
        )
        for i in range(2)
    ]


def store_pair(ref, pair, *at):
    if len(ref.shape) > 2:
        for i in range(2):
            ref[(*at, i)] = pair[i]
        return
    width = pair[0].shape[0]
    rows, columns, main = room_of(width)
    here = pl.ds(at[0] * rows, width)
    step = (columns - 2 * main) // 2
    for i in range(2):
        ref[here, i * main : (i + 1) * main] = pair[i][:, :main]
        if width > main:
            ref[here, 2 * main + i * step : 2 * main + i * step + width - main] = pair[i][:, main:]


def apply_pairs(vector, ref, *at):
    count = vector.shape[0]
    rows = lax.broadcasted_iota(jnp.int32, vector.shape, 0)
    both = jnp.concatenate(split2(vector), axis=0)
    total = jnp.zeros(vector.shape, F32)
    for l in range(count):
        part, here = ref, l
        if isinstance(ref, (list, tuple)):
            each = count // len(ref)
            part, here = ref[l // each], l % each
        high, low = pair_at(part, vector.shape[1], *at, here)
        first = jnp.dot(both, high, preferred_element_type=F32)
        second = jnp.dot(both, low, preferred_element_type=F32)
        total = jnp.where(rows == l, first[:count] + first[count:] + second[:count], total)
    return total


def apply_rows(vector, ref, *at):
    count = vector.shape[0]
    rows = lax.broadcasted_iota(jnp.int32, vector.shape, 0)
    both = jnp.concatenate(split2(vector), axis=0)
    total = jnp.zeros(vector.shape, F32)
    for l in range(count):
        first = lax.dot_general(
            both, ref[(*at, l)], (((1,), (1,)), ((), ())), preferred_element_type=F32
        )
        total = jnp.where(rows == l, first[:count] + first[count:], total)
    return total


def core_of():
    return lax.rem(lax.axis_index("wall"), 2)


def chip_of():
    return lax.div(lax.axis_index("wall"), 2)


def between(chips, core):
    inside = jnp.logical_and(chip_of() >= chips[0], chip_of() < chips[1])
    return jnp.logical_and(inside, core_of() == core)


def pair_kernel(raw_ref, *refs, first_chip, fetch, turn, **options):
    if fetch:
        next_ref, landed_ref, *outs, landed, turned_ref, arrived = refs
        copies = [
            pltpu.make_async_copy(next_ref.at[e], landed.at[0, e], arrived.at[e]) for e in range(next_ref.shape[0])
        ]
        for copy in copies:
            copy.start()
        turn_blocks(landed_ref, 0, 0, turned_ref)
    elif turn:
        landed_ref, *outs, turned_ref = refs
        for e in range(raw_ref.shape[1]):
            turn_blocks(landed_ref, 0, e, turned_ref)
    else:
        outs = refs

    def other(e, l):
        if turn or (fetch and e == 0):
            return turned_ref[0, e, l]
        return raw_ref[options["kind"], e, l]

    @pl.when(chip_of() >= first_chip)
    def _():
        make_pairs(raw_ref, other, *outs, lines=options["lines"], ascending=options["ascending"])

    if fetch:
        for copy in copies:
            copy.wait()


def make_pairs(raw_ref, other, step_ref, whole_ref, sent_ref, *, lines, ascending):
    count, width = raw_ref.shape[1], raw_ref.shape[3]
    for l in range(*lines):
        for e in range(count):
            block = lax.dot_general(
                other(e, l), raw_ref[0, e, l], (((0,), (1,)), ((), ())), preferred_element_type=F32
            )
            store_pair(step_ref, split2(block), e, l)
    order = list(range(count)) if ascending else list(range(count))[::-1]
    for l in range(*lines):
        whole = pair_at(step_ref, width, order[0], l)
        for e in order[1:]:
            whole = split2(product(whole, pair_at(step_ref, width, e, l)))
        if count % 2:
            whole = [-x for x in whole]
        store_pair(whole_ref, whole, l - lines[0])
        store_pair(sent_ref, whole, l - lines[0])


def chip_kernel(*refs, parts, width, own_first, chips):
    got_refs, own_refs, chip_ref = refs[:parts], refs[parts:-1], refs[-1]

    @pl.when(between(chips, 1))
    def _():
        each = chip_ref.shape[0] // parts
        for l in range(chip_ref.shape[0]):
            pairs = [pair_at(x[l // each], width, l % each) for x in (got_refs, own_refs)]
            store_pair(chip_ref, split2(product(*(pairs[::-1] if own_first else pairs))), l)


def turn_blocks(landed_ref, a, e, raw_ref):
    turned = jnp.swapaxes(landed_ref[a, e], 0, 1)
    for l in range(raw_ref.shape[2]):
        raw_ref[a, e, l] = turned[l]


def prepare_kernel(*refs, taken):
    blocks = refs[7 : 7 + taken]
    places, (weight_ref, rhs_ref, act_ref, state_ref, lift_ref) = refs[:7], refs[7 + taken : 12 + taken]
    slot_ref, len_ref, coef_ref, nb_ref, source_ref, arrived = refs[12 + taken + (taken > 0) :][:6]
    targets = (slot_ref, len_ref, coef_ref, nb_ref, source_ref, state_ref, lift_ref)
    copies = [
        pltpu.make_async_copy(there, here, arrived.at[i]) for i, (there, here) in enumerate(zip(places, targets))
    ]
    block_copies = []
    if taken:
        raw_ref, landed, landed_at = refs[12 + taken], refs[-2], refs[-1]
        places_in = [(a, e) for a in range(taken) for e in range(landed.shape[1]) if (a, e) != (1, 0)]
        block_copies = [
            pltpu.make_async_copy(blocks[a].at[e], landed.at[a, e], landed_at.at[a, e]) for a, e in places_in
        ]
    for copy in copies + block_copies:
        copy.start()
    for copy in copies:
        copy.wait()
    faces, slots = coef_ref.shape
    depth, lines = slot_ref.shape
    cells = 3 * slots
    k = lax.broadcasted_iota(jnp.int32, (cells, slots), 0)
    e = lax.broadcasted_iota(jnp.int32, (cells, slots), 1)
    weight = jnp.zeros((cells, slots), F32)
    own = jnp.zeros((1, slots), F32)
    for f in range(faces):
        coef = coef_ref[f : f + 1, :]
        own = own + coef
        weight = weight - jnp.where(k == nb_ref[f : f + 1, :], coef, 0.0)
    weight = weight + jnp.where(k == e + slots, own, 0.0)
    count = depth * lines
    rows = lax.broadcasted_iota(jnp.int32, (count, slots), 0)
    slot = jnp.zeros((count, slots), jnp.int32)
    for g in range(depth):
        for l in range(lines):
            slot = jnp.where(rows == g * lines + l, slot_ref[g, l], slot)
    chosen = (slot == lax.broadcasted_iota(jnp.int32, (count, slots), 1)).astype(F32).astype(BF16)
    high = weight.astype(BF16)
    mid, low = split2(weight - high.astype(F32))
    for i, part in enumerate((high, mid, low)):
        weight_ref[i * count : (i + 1) * count, :] = lax.dot_general(
            chosen, part, (((1,), (1,)), ((), ())), preferred_element_type=F32
        ).astype(BF16)
    rhs_ref[...] = jnp.dot(chosen, source_ref[...], preferred_element_type=F32)
    rows = lax.broadcasted_iota(jnp.int32, act_ref.shape[1:], 0)
    length = jnp.zeros(act_ref.shape[1:], jnp.int32)
    for l in range(lines):
        length = jnp.where(rows == l, len_ref[l], length)
    place = lax.axis_index("wall") * depth
    for g in range(depth):
        act_ref[g] = (place + g < length).astype(F32)
    for i, copy in enumerate(block_copies):
        copy.wait()
        turn_blocks(landed, *places_in[i], raw_ref)


def copy_kernel(here, _, there):
    there[...] = here[...]


def residual(before, state, after, weight, source, lift, depth):
    cells = jnp.concatenate([before[...], state[...], after[...]], axis=0)
    parts = jnp.dot(weight[...], cells, preferred_element_type=F32)
    count = source.shape[0]
    face_sum = parts[:count] + (parts[count : 2 * count] + parts[2 * count :])
    flux = jnp.dot(face_sum.astype(BF16), lift[...], preferred_element_type=F32)
    rhs = source[...] - flux
    lines = count // depth
    return [rhs[g * lines : (g + 1) * lines] for g in range(depth)]


def residual_kernel(before, state, after, weight, source, lift, rhs_ref):
    for g, rhs in enumerate(residual(before, state, after, weight, source, lift, rhs_ref.shape[0])):
        rhs_ref[g] = rhs


def forward_local(scaled, q_ref, act_ref, carried):
    values = []
    for g, value in enumerate(scaled):
        if carried is not None:
            value = value - apply_pairs(carried, q_ref, g)
        carried = act_ref[g] * value
        values.append(carried)
    return values


def backward_local(values, s_ref, act_ref, carried):
    solved = [None] * len(values)
    for g in range(len(values) - 1, -1, -1):
        value = values[g]
        if carried is not None:
            value = value - apply_pairs(carried, s_ref, g)
        carried = act_ref[g] * value
        solved[g] = carried
    return solved


def local_kernel(*refs, merged):
    if merged:
        *cells, raw_ref, act_ref, lower_in, scaled_ref, y_ref, leave_ref, landed_ref, arrived = refs
        copy = pltpu.make_async_copy(lower_in.at[0], landed_ref.at[0, 0], arrived)
        copy.start()
        rhs = residual(*cells, scaled_ref.shape[0])
    else:
        rhs_ref, raw_ref, act_ref, scaled_ref, y_ref, leave_ref = refs
        rhs = [rhs_ref[g] for g in range(rhs_ref.shape[0])]
    depth = len(rhs)
    scaled = [apply_rows(rhs[g], raw_ref, 0, g) for g in range(depth)]
    values = raw_steps(scaled, raw_ref, None, act_ref, None)
    for g in range(depth):
        scaled_ref[g] = scaled[g]
        y_ref[g] = values[g]
    leave_ref[...] = values[-1]
    if merged:
        copy.wait()


def raw_steps(scaled, raw_ref, first_ref, act_ref, carried):
    values = []
    for g, value in enumerate(scaled):
        if carried is not None:
            at = (first_ref, 0, 0) if first_ref is not None and g == 0 else (raw_ref, 1, g)
            value = value - apply_rows(apply_rows(carried, *at), raw_ref, 0, g)
        carried = act_ref[g] * value
        values.append(carried)
    return values


def wall_kernel(came_ref, scaled_ref, raw_ref, act_ref, y_ref, *refs):
    out_ref, leave_ref = refs[-2:]
    first_ref = refs[0] if len(refs) > 2 else None
    depth = y_ref.shape[0]
    out_ref[...] = y_ref[...]
    leave_ref[...] = y_ref[depth - 1]

    @pl.when(lax.axis_index("wall") == 1)
    def _():
        values = raw_steps([scaled_ref[g] for g in range(depth)], raw_ref, first_ref, act_ref, came_ref[...])
        for g in range(depth):
            out_ref[g] = values[g]
        leave_ref[...] = values[-1]


def chip_local_kernel(came_ref, act_ref, y_ref, *refs, chips):
    own_refs, out_ref = refs[:-1], refs[-1]
    depth = y_ref.shape[0]
    out_ref[...] = y_ref[depth - 1]

    @pl.when(between(chips, 1))
    def _():
        out_ref[...] = act_ref[depth - 1] * apply_pairs(came_ref[...], own_refs) + y_ref[depth - 1]


def three_terms(x):
    high = x.astype(BF16)
    return high, *split2(x - high.astype(F32))


def through_kernel(act_ref, q_ref, s_ref, y_ref, *refs, parts):
    whole_refs, (out_ref, sent_ref, echo_ref) = refs[:parts], refs[parts:]
    depth, lines, _, _, width = q_ref.shape
    main, below = width // LANES * LANES, lines * room_of(width)[0]
    echo = backward_local([y_ref[g] for g in range(depth)], s_ref, act_ref, None)[0]
    echo_ref[...] = echo
    for i, term in enumerate(three_terms(echo)):
        sent_ref[below + 2 * TILE * i : below + 2 * TILE * i + lines, :main] = term[:, :main]
        if width > main:
            sent_ref[below + 2 * TILE * i : below + 2 * TILE * i + lines, main:width] = term[:, main:]

    @pl.when(chip_of() > 0)
    def _():
        for l in range(lines):
            active = [act_ref[g, l : l + 1, :] for g in range(depth)]
            steps = [[-x for x in pair_at(q_ref, width, 0, l)]]
            for g in range(1, depth - 1):
                steps.append(split2(-product(steps[-1], pair_at(q_ref, width, g, l))))
            each = lines // parts
            value = [
                (active[depth - 1] * x.astype(F32)).astype(BF16)
                for x in pair_at(whole_refs[l // each], width, l % each)
            ]
            for g in range(depth - 2, -1, -1):
                reach = steps[g][0].astype(F32) + steps[g][1].astype(F32)
                total = active[g] * (reach - product(value, pair_at(s_ref, width, g, l)))
                value = split2(total)
            pair = value
            store_pair(out_ref, pair, l)
            store_pair(sent_ref, pair, l)


def hop_kernel(came_ref, act_ref, local_ref, idle_ref, *refs, chip):
    pair_refs, out_ref = refs[:-1], refs[-1]
    out_ref[...] = idle_ref[...]

    @pl.when(jnp.logical_and(chip_of() == chip, core_of() == 1))
    def _():
        gone = apply_pairs(came_ref[...], pair_refs)
        out_ref[...] = act_ref[act_ref.shape[0] - 1] * gone + local_ref[...]


def early_hop_kernel(came_ref, act_ref, mate_ref, y_ref, *refs, chip, parts):
    got_refs, own_refs, out_ref = refs[:parts], refs[parts : 2 * parts], refs[-1]
    depth = y_ref.shape[0]
    out_ref[...] = came_ref[...]

    @pl.when(jnp.logical_and(chip_of() == chip, core_of() == 1))
    def _():
        middle = apply_pairs(came_ref[...], got_refs) + mate_ref[...]
        out_ref[...] = act_ref[depth - 1] * apply_pairs(middle, own_refs) + y_ref[depth - 1]


def chosen_arrival(refs, chips, like):
    here = chip_of()
    value = jnp.zeros(like, F32)
    for ref, chip in zip(refs, chips):
        value = jnp.where(here == chip, ref[...], value)
    return value


def choose_kernel(*refs, chips):
    refs[-1][...] = chosen_arrival(refs[:-1], chips, refs[-1].shape)


def turn_kernel(enter_ref, came_ref, echo_ref, got_c, got_d, own_d, *refs, parts, chips, fill):
    got_refs, (enter_y, mid_ref, out_ref) = refs[:parts], refs[-3:]
    inside = jnp.logical_and(chip_of() >= chips[0], chip_of() < chips[1])
    if not fill:
        for held, ref in zip(refs[parts:], refs[-3:]):
            ref[...] = held[...]
    if fill:

        @pl.when(jnp.logical_not(inside))
        def _():
            enter_y[...] = enter_ref[...]
            mid_ref[...] = echo_ref[...]
            out_ref[...] = echo_ref[...]

    @pl.when(jnp.logical_and(inside, core_of() == 1))
    def _():
        enter = enter_ref[...]
        leave = apply_pairs(enter, got_refs) + came_ref[...]
        middle = apply_pairs(leave, own_d) + echo_ref[...]
        lines, width = enter.shape
        below = lines * room_of(width)[0]
        first = apply_pairs(enter, got_d)
        for i in range(3):
            first = first + got_d[below + 2 * TILE * i : below + 2 * TILE * i + lines, :width].astype(F32)
        enter_y[...] = leave
        mid_ref[...] = middle
        out_ref[...] = apply_pairs(middle, got_c) + first


def send_kernel(x_ref, enter_ref, out_ref, *, last):
    out_ref[...] = jnp.where(chip_of() == last, x_ref[...], enter_ref[...])


def steps_kernel(flow_ref, scaled_ref, q_ref, act_ref, held_ref, y_ref, *, late):
    depth = scaled_ref.shape[0]
    here, core = chip_of(), core_of()
    y_ref[...] = held_ref[...]
    if late:
        inside = jnp.logical_and(core == 0, here > 1)
    else:
        inside = jnp.logical_and(here > 0, jnp.logical_or(core == 1, here == 1))

    @pl.when(inside)
    def _():
        values = forward_local([scaled_ref[g] for g in range(depth)], q_ref, act_ref, flow_ref[...])
        for g in range(depth):
            y_ref[g] = values[g]


def entry_kernel(own_ref, came_ref, out_ref):
    out_ref[...] = jnp.where(core_of() == 1, own_ref[...], came_ref[...])


def leave_kernel(own_ref, first_ref, *refs, chips):
    came_ref, out_ref = refs[-2:]
    came_ref[...] = chosen_arrival(refs[:-2], chips, came_ref.shape)
    out_ref[...] = first_ref[...]

    @pl.when(jnp.logical_and(core_of() == 1, chip_of() > 0))
    def _():
        out_ref[...] = apply_pairs(came_ref[...], own_ref) + first_ref[...]


def wall_middle_kernel(came_ref, got_c, got_d, out_ref):
    @pl.when(lax.axis_index("wall") == 0)
    def _():
        lines, width = came_ref.shape
        below = lines * room_of(width)[0]
        value = apply_pairs(came_ref[...], got_c)
        for i in range(3):
            value = value + got_d[below + 2 * TILE * i : below + 2 * TILE * i + lines, :width].astype(F32)
        out_ref[...] = value


def last_kernel(beyond_ref, met_ref, middle_ref, wall_ref, whole_ref, echo_ref, s_ref, act_ref, y_ref, out_ref):
    depth = y_ref.shape[0]
    core, chip = core_of(), chip_of()
    first = jnp.where(chip == 0, middle_ref[...], met_ref[...])
    second = jnp.where(chip == 0, wall_ref[...], beyond_ref[...])
    carried = jnp.where(core == 0, first, second)

    @pl.when(chip == 0)
    def _():
        out_ref[0] = apply_pairs(carried, whole_ref) + echo_ref[...]
        value = carried
        for g in range(depth - 1, 0, -1):
            value = act_ref[g] * (y_ref[g] - apply_pairs(value, s_ref, g))
            out_ref[g] = value

    @pl.when(chip > 0)
    def _():
        solved = backward_local([y_ref[g] for g in range(depth)], s_ref, act_ref, carried)
        for g in range(depth):
            out_ref[g] = solved[g]


def padded_bytes(shape, dtype):
    size = jnp.dtype(dtype).itemsize
    shape = (1,) * (2 - len(shape)) + tuple(shape)
    total = -(-shape[-2] // 16) * 16 * -(-shape[-1] // 128) * 128 * size
    for extent in shape[:-2]:
        total *= extent
    return total


def run(kernel, operands, outs, blocks=1, scratch=()):
    held = [(x.shape, x.dtype) for x, _ in operands] + [(s, t) for s, t, _ in outs]
    limit = sum(padded_bytes(s, t) for s, t in held)
    if blocks == 1:
        in_specs = [at if isinstance(at, pl.BlockSpec) else VMEM for _, at in operands]
        out_specs = [VMEM for _ in outs]
        grid = ()
    else:

        def spec(shape, at):
            if isinstance(at, pl.BlockSpec):
                return at
            if at is None:
                return pl.BlockSpec(shape, lambda i: (0,) * len(shape))
            size = tuple(n // blocks if axis == at else n for axis, n in enumerate(shape))
            return pl.BlockSpec(size, lambda i: tuple(i if axis == at else 0 for axis in range(len(shape))))

        in_specs = [spec(x.shape, at) for x, at in operands]
        out_specs = [spec(s, at) for s, _, at in outs]
        grid = (blocks,)
        limit = 2 * limit // blocks
    limit += sum(padded_bytes(s.shape, s.dtype) for s in scratch if s.memory_space == pltpu.VMEM)
    limit = min(limit + (2 << 20), 60 << 20)
    return pl.pallas_call(
        kernel,
        grid=grid,
        in_specs=in_specs,
        out_specs=out_specs,
        out_shape=[jax.ShapeDtypeStruct(s, t) for s, t, _ in outs],
        scratch_shapes=list(scratch),
        compiler_params=pltpu.CompilerParams(vmem_limit_bytes=limit),
        cost_estimate=pl.CostEstimate(flops=1, bytes_accessed=1, transcendentals=0),
    )(*[x for x, _ in operands])


def hop_pairs(count, start, end, core=1, relay=None):
    start, end = 2 * start + 1, 2 * end + core
    target = {i: i ^ 1 for i in range(count)}
    cycle = [start, end, end ^ 1, start ^ 1]
    if relay is not None:
        cycle[3:3] = [2 * relay, 2 * relay + 1]
    target.update(zip(cycle, cycle[1:] + cycle[:1]))
    return sorted(target.items())


def in_hbm(value):
    return pltpu.with_memory_space_constraint(value, pltpu.HBM)


def after(value, *others):
    return lax.optimization_barrier((value, *others))[0]


def per_device(state, source, face_coef, neighbour, lift, elem_slot, line_len, dinv, lower, upper):
    wall_count = lax.axis_size("wall")
    surf_count = lax.axis_size("surf")
    last = wall_count // 2 - 1
    depth, lines, width, _ = dinv.shape
    slots = state.shape[0]
    block = TILE if lines % TILE == 0 else lines
    blocks = lines // block
    parts = 1
    room, columns, _ = room_of(width)
    line_vector = ((lines, width), F32, 0)
    element_vectors = ((depth, lines, width), F32, 1)
    line_sent = ((lines * room, columns), BF16, 0)
    vector_sent = ((lines * room + 6 * TILE * blocks, columns), BF16, 0)
    line_pairs = ((lines, 2, width, width), BF16, 0)
    part_sent = ((lines // parts * room, columns), BF16, 0)
    part_pairs = ((lines // parts, 2, width, width), BF16, 0)
    element_pairs = ((depth, lines, 2, width, width), BF16, 1)

    def mates(value):
        return lax.ppermute(value, "wall", [(i, i ^ 1) for i in range(wall_count)])

    def relaid(arrays, *others):
        if lines != TILE:
            return jnp.stack(arrays)
        shape = (len(arrays), depth, lines, width, width)
        return run(
            functools.partial(relayout_kernel, kinds=len(arrays)),
            [(in_hbm(jnp.transpose(x, (0, 2, 1, 3))), ANY) for x in arrays] + [(x, None) for x in others],
            [(shape, BF16, None)],
            scratch=[
                pltpu.VMEM((len(arrays), depth, width, lines, width), BF16),
                pltpu.SemaphoreType.DMA((len(arrays), depth)),
            ],
        )[0]

    count = depth * lines
    small = (elem_slot, line_len, face_coef.T, neighbour.T, source)
    in_place = lines == TILE
    blocks_in = [in_hbm(jnp.transpose(x, (0, 2, 1, 3))) for x in (dinv, lower, upper)] if in_place else []
    weight, line_source, act, near_state, near_lift, *landed = run(
        functools.partial(prepare_kernel, taken=2 if in_place else 0),
        [(in_hbm(x), ANY) for x in (*small, state, lift)] + [(x, ANY) for x in blocks_in[:2]],
        [
            ((3 * count, 3 * slots), BF16, None),
            ((count, width), F32, None),
            element_vectors,
            (state.shape, BF16, None),
            (lift.shape, BF16, None),
        ]
        + ([((2, depth, lines, width, width), BF16, None)] if in_place else []),
        scratch=[(pltpu.SMEM if i < 2 else pltpu.VMEM)(x.shape, x.dtype) for i, x in enumerate(small)]
        + [pltpu.SemaphoreType.DMA((len(small) + 2,))]
        + (
            [pltpu.VMEM((2, depth, width, lines, width), BF16), pltpu.SemaphoreType.DMA((2, depth))]
            if in_place
            else []
        ),
    )
    before = lax.ppermute(state, "surf", [(i, (i + 1) % surf_count) for i in range(surf_count)])
    beyond = lax.ppermute(state, "surf", [((i + 1) % surf_count, i) for i in range(surf_count)])
    (before,) = run(copy_kernel, [(before, None), (weight, None)], [(state.shape, BF16, None)])
    cells = [(x, None) for x in (before, near_state, beyond, weight, line_source, near_lift)]
    raw = landed[0] if in_place else jnp.stack([dinv, lower, upper])
    vectors = [element_vectors, element_vectors, line_vector]
    if in_place:
        scaled, y_local, y_leave, first_lower = run(
            functools.partial(local_kernel, merged=True),
            cells + [(raw, None), (act, None), (blocks_in[1], ANY)],
            vectors + [((1, 1, width, lines, width), BF16, None)],
            scratch=[pltpu.SemaphoreType.DMA(())],
        )
    else:
        (rhs,) = run(residual_kernel, cells, [element_vectors])
        scaled, y_local, y_leave = run(
            functools.partial(local_kernel, merged=False), [(rhs, 1), (raw, 2), (act, 1)], vectors, blocks
        )
    came_y = mates(y_leave)
    q, *rest = run(
        functools.partial(
            pair_kernel, first_chip=1, fetch=in_place, turn=False, kind=1, lines=(0, block), ascending=True
        ),
        [(after(raw, y_leave), 2)]
        + ([(blocks_in[2], ANY), (first_lower, None)] if in_place else []),
        [element_pairs, line_pairs, line_sent]
        + (
            [((1, depth, width, lines, width), BF16, None), ((1, 1, lines, width, width), BF16, None)]
            if in_place
            else []
        ),
        blocks,
        [pltpu.SemaphoreType.DMA((depth,))] if in_place else [],
    )
    wall_y, wall_leave = run(
        wall_kernel,
        [(came_y, 0), (scaled, 1), (raw, 2), (act, 1), (y_local, 1)] + [(x, 2) for x in rest[3:]],
        [element_vectors, line_vector],
        blocks,
    )
    arrivals = [lax.ppermute(wall_leave, "wall", hop_pairs(wall_count, 0, 1))]
    a, got_a = [rest[0]], [mates(after(rest[1], came_y))]
    s, c, sent_c = run(
        functools.partial(
            pair_kernel, first_chip=0, fetch=False, turn=in_place, kind=2, lines=(0, block), ascending=False
        ),
        [(after(raw, a[-1], wall_leave), 2)] + ([(rest[2], None)] if in_place else []),
        [element_pairs, line_pairs, line_sent],
        blocks,
        [pltpu.VMEM((1, depth, lines, width, width), BF16)] if in_place else [],
    )
    got_c = mates(after(sent_c, arrivals[0],got_a[-1]))

    def hop(came, pairs, local, idle, at):
        (out,) = run(
            functools.partial(hop_kernel, chip=at),
            [(came, 0), (act, 1), (local, 0), (idle, 0)] + [(x, 0) for x in pairs],
            [line_vector],
            blocks,
        )
        return out

    out = wall_leave
    for at in range(1, last):
        if at == 1:
            (out,) = run(
                functools.partial(early_hop_kernel, chip=at, parts=parts),
                [(arrivals[-1], 0), (act, 1), (came_y, 0), (y_local, 1)] + [(x, 0) for x in got_a + a],
                [line_vector],
                blocks,
            )
            (chip_a,) = run(
                functools.partial(chip_kernel, parts=parts, width=width, own_first=False, chips=(2, last)),
                [(after(x, out) if i == 0 else x, 0) for i, x in enumerate(got_a + a)],
                [line_pairs],
                blocks,
            )
            (y_chip,) = run(
                functools.partial(chip_local_kernel, chips=(2, last)),
                [(after(came_y, out), 0), (act, 1), (y_local, 1)] + [(x, 0) for x in a],
                [line_vector],
                blocks,
            )
            through, sent_d, echo = run(
                functools.partial(through_kernel, parts=parts),
                [(act, 1), (after(q, out, chip_a, y_chip), 1), (s, 1), (wall_y, 1)] + [(x, 0) for x in a],
                [line_pairs, vector_sent, line_vector],
                blocks,
            )
        else:
            out = hop(arrivals[-1], [chip_a], y_chip, y_chip, at)
        pairs = hop_pairs(wall_count, at, at + 1, relay=0 if at == 1 else None)
        arrivals.append(lax.ppermute(out, "wall", pairs))
        if at == 1:
            got_d = mates(after(sent_d, got_c, arrivals[-1]))

    def chosen(arrived, chips):
        return run(
            functools.partial(choose_kernel, chips=chips), [(x, 0) for x in arrived], [line_vector], blocks
        )[0]

    def turn(first_chip, end_chip, entered, held=()):
        return run(
            functools.partial(turn_kernel, parts=parts, chips=(first_chip, end_chip), fill=not held),
            [(x, 0) for x in (entered, came_y, echo, got_c, got_d, through, *got_a)]
            + [(x, 0) for x in held],
            [line_vector] * 3,
            blocks,
        )

    def steps(late, flow, held):
        return run(
            functools.partial(steps_kernel, late=late),
            [(flow, 0)] + [(x, 1) for x in (scaled, q, act, held)],
            [element_vectors],
            blocks,
        )

    (chip_c,) = run(
        functools.partial(chip_kernel, parts=1, width=width, own_first=True, chips=(1, last)),
        [(after(got_c, out), 0), (c, 0)],
        [line_pairs],
        blocks,
    )
    arrivals[-1] = after(arrivals[-1], chip_c)
    held = turn(last, last + 1, arrivals[-1])
    entered = chosen(arrivals, list(range(1, last + 1)))
    x_chip = held[-1]
    (out,) = run(functools.partial(send_kernel, last=last), [(x_chip, 0), (entered, 0)], [line_vector], blocks)
    arrived = [lax.ppermute(out, "wall", hop_pairs(wall_count, last, last - 1))]
    held = turn(last - 1, last, after(entered, out), held)
    x_chip = held[-1]
    enter_y, middle, _ = held
    y = wall_y
    for at in range(last - 1, 0, -1):
        came = arrived[-1]
        if at == last - 2:
            enter_y, middle, x_chip = turn(1, last - 1, after(entered, out), held)
        if at == 1:
            (flow,) = run(entry_kernel, [(enter_y, 0), (after(arrived[0], out), 0)], [line_vector], blocks)
            (y,) = steps(False, flow, wall_y)
            came = after(came, y)
        out = hop(came, [chip_c], x_chip, entered, at)
        arrived.append(lax.ppermute(out, "wall", hop_pairs(wall_count, at, at - 1, int(at > 1))))
    wall = lax.ppermute(out, "wall", hop_pairs(wall_count, 1, 0))
    beyond, left = run(
        functools.partial(leave_kernel, chips=list(range(last - 1, 0, -1))),
        [(x, 0) for x in (c, middle, *arrived[:-1])],
        [line_vector, line_vector],
        blocks,
    )
    met_left = mates(after(left, out))
    (y,) = steps(True, arrived[-1], y)
    (wall_middle,) = run(
        wall_middle_kernel, [(after(arrived[-1], wall, y), 0), (got_c, 0), (got_d, 0)], [line_vector], blocks
    )
    (solution,) = run(
        last_kernel,
        [(x, 0) for x in (beyond, met_left, wall_middle, wall, c, echo)] + [(x, 1) for x in (s, act, y)],
        [element_vectors],
        blocks,
    )
    return solution


def solution(mesh):
    in_specs = (
        P(("wall", "surf"), None),
        P(("wall", "surf"), None),
        P(("wall", "surf"), None),
        P(("wall", "surf"), None),
        P(),
        P("wall", "surf"),
        P("surf"),
        P("wall", "surf", None, None),
        P("wall", "surf", None, None),
        P("wall", "surf", None, None),
    )
    out_specs = P("wall", "surf", None)
    return jax.shard_map(
        per_device, mesh=mesh, in_specs=in_specs, out_specs=out_specs, check_vma=False
    )
```

```python
import functools

import jax
import jax.numpy as jnp
from jax import lax
from jax.experimental import pallas as pl
from jax.experimental.pallas import tpu as pltpu
from jax.sharding import PartitionSpec as P

F32 = jnp.float32
BF16 = jnp.bfloat16
TILE = 8
LANES = 128
VMEM = pl.BlockSpec(memory_space=pltpu.VMEM)
ANY = pl.BlockSpec(memory_space=pl.ANY)
SMEM = pl.BlockSpec(memory_space=pltpu.SMEM)


def split2(x):
    high = x.astype(BF16)
    return high, (x - high.astype(F32)).astype(BF16)


def product(x, y):
    left = jnp.concatenate([x[0], x[0], x[1]], axis=1)
    right = jnp.concatenate([y[0], y[1], y[0]], axis=0)
    return jnp.dot(left, right, preferred_element_type=F32)


def room_of(width):
    rows = -(-width // (2 * TILE)) * 2 * TILE
    main = width // LANES * LANES
    return rows, 2 * main + (LANES if width - main <= LANES // 2 else 2 * LANES), main


def pair_at(ref, width, *at):
    if len(ref.shape) > 2:
        return [ref[(*at, i)] for i in range(2)]
    rows, columns, main = room_of(width)
    here = pl.ds(at[0] * rows, width)
    step = (columns - 2 * main) // 2
    if width == main:
        return [ref[here, i * main : (i + 1) * main] for i in range(2)]
    return [
        jnp.concatenate(
            [
                ref[here, i * main : (i + 1) * main],
                ref[here, 2 * main + i * step : 2 * main + i * step + width - main],
            ],
            axis=1,
        )
        for i in range(2)
    ]


def store_pair(ref, pair, *at):
    if len(ref.shape) > 2:
        for i in range(2):
            ref[(*at, i)] = pair[i]
        return
    width = pair[0].shape[0]
    rows, columns, main = room_of(width)
    here = pl.ds(at[0] * rows, width)
    step = (columns - 2 * main) // 2
    for i in range(2):
        ref[here, i * main : (i + 1) * main] = pair[i][:, :main]
        if width > main:
            ref[here, 2 * main + i * step : 2 * main + i * step + width - main] = pair[i][:, main:]


def apply_pairs(vector, ref, *at):
    count = vector.shape[0]
    rows = lax.broadcasted_iota(jnp.int32, vector.shape, 0)
    both = jnp.concatenate(split2(vector), axis=0)
    total = jnp.zeros(vector.shape, F32)
    for l in range(count):
        part, here = ref, l
        if isinstance(ref, (list, tuple)):
            each = count // len(ref)
            part, here = ref[l // each], l % each
        high, low = pair_at(part, vector.shape[1], *at, here)
        first = jnp.dot(both, high, preferred_element_type=F32)
        second = jnp.dot(both, low, preferred_element_type=F32)
        total = jnp.where(rows == l, first[:count] + first[count:] + second[:count], total)
    return total


def apply_rows(vector, ref, *at):
    count = vector.shape[0]
    rows = lax.broadcasted_iota(jnp.int32, vector.shape, 0)
    both = jnp.concatenate(split2(vector), axis=0)
    total = jnp.zeros(vector.shape, F32)
    for l in range(count):
        first = lax.dot_general(
            both, ref[(*at, l)], (((1,), (1,)), ((), ())), preferred_element_type=F32
        )
        total = jnp.where(rows == l, first[:count] + first[count:], total)
    return total


def core_of():
    return lax.rem(lax.axis_index("wall"), 2)


def chip_of():
    return lax.div(lax.axis_index("wall"), 2)


def between(chips, core):
    inside = jnp.logical_and(chip_of() >= chips[0], chip_of() < chips[1])
    return jnp.logical_and(inside, core_of() == core)


def pair_kernel(raw_ref, *refs, first_chip, fetch, turn, **options):
    if fetch:
        next_ref, landed_ref, *outs, landed, turned_ref, arrived = refs
        copies = [
            pltpu.make_async_copy(next_ref.at[e], landed.at[0, e], arrived.at[e]) for e in range(next_ref.shape[0])
        ]
        for copy in copies:
            copy.start()
        turn_blocks(landed_ref, 0, 0, turned_ref)
    elif turn:
        landed_ref, *outs, turned_ref = refs
        for e in range(raw_ref.shape[1]):
            turn_blocks(landed_ref, 0, e, turned_ref)
    else:
        outs = refs

    def other(e, l):
        if turn or (fetch and e == 0):
            return turned_ref[0, e, l]
        return raw_ref[options["kind"], e, l]

    @pl.when(chip_of() >= first_chip)
    def _():
        make_pairs(raw_ref, other, *outs, lines=options["lines"], ascending=options["ascending"])

    if fetch:
        for copy in copies:
            copy.wait()


def make_pairs(raw_ref, other, step_ref, whole_ref, sent_ref, *, lines, ascending):
    count, width = raw_ref.shape[1], raw_ref.shape[3]
    for l in range(*lines):
        for e in range(count):
            block = lax.dot_general(
                other(e, l), raw_ref[0, e, l], (((0,), (1,)), ((), ())), preferred_element_type=F32
            )
            store_pair(step_ref, split2(block), e, l)
    order = list(range(count)) if ascending else list(range(count))[::-1]
    for l in range(*lines):
        whole = pair_at(step_ref, width, order[0], l)
        for e in order[1:]:
            whole = split2(product(whole, pair_at(step_ref, width, e, l)))
        if count % 2:
            whole = [-x for x in whole]
        store_pair(whole_ref, whole, l - lines[0])
        store_pair(sent_ref, whole, l - lines[0])


def chip_kernel(*refs, parts, width, own_first, chips):
    got_refs, own_refs, chip_ref = refs[:parts], refs[parts:-1], refs[-1]

    @pl.when(between(chips, 1))
    def _():
        each = chip_ref.shape[0] // parts
        for l in range(chip_ref.shape[0]):
            pairs = [pair_at(x[l // each], width, l % each) for x in (got_refs, own_refs)]
            store_pair(chip_ref, split2(product(*(pairs[::-1] if own_first else pairs))), l)


def turn_blocks(landed_ref, a, e, raw_ref):
    turned = jnp.swapaxes(landed_ref[a, e], 0, 1)
    for l in range(raw_ref.shape[2]):
        raw_ref[a, e, l] = turned[l]


def prepare_kernel(*refs, taken):
    blocks = refs[7 : 7 + taken]
    places, (weight_ref, rhs_ref, act_ref, state_ref, lift_ref) = refs[:7], refs[7 + taken : 12 + taken]
    slot_ref, len_ref, coef_ref, nb_ref, source_ref, arrived = refs[12 + taken + (taken > 0) :][:6]
    targets = (slot_ref, len_ref, coef_ref, nb_ref, source_ref, state_ref, lift_ref)
    copies = [
        pltpu.make_async_copy(there, here, arrived.at[i]) for i, (there, here) in enumerate(zip(places, targets))
    ]
    block_copies = []
    if taken:
        raw_ref, landed, landed_at = refs[12 + taken], refs[-2], refs[-1]
        places_in = [(a, e) for a in range(taken) for e in range(landed.shape[1]) if (a, e) != (1, 0)]
        block_copies = [
            pltpu.make_async_copy(blocks[a].at[e], landed.at[a, e], landed_at.at[a, e]) for a, e in places_in
        ]
    for copy in copies + block_copies:
        copy.start()
    for copy in copies:
        copy.wait()
    faces, slots = coef_ref.shape
    depth, lines = slot_ref.shape
    cells = 3 * slots
    k = lax.broadcasted_iota(jnp.int32, (cells, slots), 0)
    e = lax.broadcasted_iota(jnp.int32, (cells, slots), 1)
    weight = jnp.zeros((cells, slots), F32)
    own = jnp.zeros((1, slots), F32)
    for f in range(faces):
        coef = coef_ref[f : f + 1, :]
        own = own + coef
        weight = weight - jnp.where(k == nb_ref[f : f + 1, :], coef, 0.0)
    weight = weight + jnp.where(k == e + slots, own, 0.0)
    count = depth * lines
    rows = lax.broadcasted_iota(jnp.int32, (count, slots), 0)
    slot = jnp.zeros((count, slots), jnp.int32)
    for g in range(depth):
        for l in range(lines):
            slot = jnp.where(rows == g * lines + l, slot_ref[g, l], slot)
    chosen = (slot == lax.broadcasted_iota(jnp.int32, (count, slots), 1)).astype(F32).astype(BF16)
    high = weight.astype(BF16)
    mid, low = split2(weight - high.astype(F32))
    for i, part in enumerate((high, mid, low)):
        weight_ref[i * count : (i + 1) * count, :] = lax.dot_general(
            chosen, part, (((1,), (1,)), ((), ())), preferred_element_type=F32
        ).astype(BF16)
    rhs_ref[...] = jnp.dot(chosen, source_ref[...], preferred_element_type=F32)
    rows = lax.broadcasted_iota(jnp.int32, act_ref.shape[1:], 0)
    length = jnp.zeros(act_ref.shape[1:], jnp.int32)
    for l in range(lines):
        length = jnp.where(rows == l, len_ref[l], length)
    place = lax.axis_index("wall") * depth
    for g in range(depth):
        act_ref[g] = (place + g < length).astype(F32)
    for i, copy in enumerate(block_copies):
        copy.wait()
        turn_blocks(landed, *places_in[i], raw_ref)


def copy_kernel(here, _, there):
    there[...] = here[...]


def residual(before, state, after, weight, source, lift, depth):
    cells = jnp.concatenate([before[...], state[...], after[...]], axis=0)
    parts = jnp.dot(weight[...], cells, preferred_element_type=F32)
    count = source.shape[0]
    face_sum = parts[:count] + (parts[count : 2 * count] + parts[2 * count :])
    flux = jnp.dot(face_sum.astype(BF16), lift[...], preferred_element_type=F32)
    rhs = source[...] - flux
    lines = count // depth
    return [rhs[g * lines : (g + 1) * lines] for g in range(depth)]


def residual_kernel(before, state, after, weight, source, lift, rhs_ref):
    for g, rhs in enumerate(residual(before, state, after, weight, source, lift, rhs_ref.shape[0])):
        rhs_ref[g] = rhs


def forward_local(scaled, q_ref, act_ref, carried):
    values = []
    for g, value in enumerate(scaled):
        if carried is not None:
            value = value - apply_pairs(carried, q_ref, g)
        carried = act_ref[g] * value
        values.append(carried)
    return values


def backward_local(values, s_ref, act_ref, carried):
    solved = [None] * len(values)
    for g in range(len(values) - 1, -1, -1):
        value = values[g]
        if carried is not None:
            value = value - apply_pairs(carried, s_ref, g)
        carried = act_ref[g] * value
        solved[g] = carried
    return solved


def local_kernel(*refs, merged):
    if merged:
        *cells, raw_ref, act_ref, lower_in, scaled_ref, y_ref, leave_ref, landed_ref, arrived = refs
        copy = pltpu.make_async_copy(lower_in.at[0], landed_ref.at[0, 0], arrived)
        copy.start()
        rhs = residual(*cells, scaled_ref.shape[0])
    else:
        rhs_ref, raw_ref, act_ref, scaled_ref, y_ref, leave_ref = refs
        rhs = [rhs_ref[g] for g in range(rhs_ref.shape[0])]
    depth = len(rhs)
    scaled = [apply_rows(rhs[g], raw_ref, 0, g) for g in range(depth)]
    values = raw_steps(scaled, raw_ref, None, act_ref, None)
    for g in range(depth):
        scaled_ref[g] = scaled[g]
        y_ref[g] = values[g]
    leave_ref[...] = values[-1]
    if merged:
        copy.wait()


def raw_steps(scaled, raw_ref, first_ref, act_ref, carried):
    values = []
    for g, value in enumerate(scaled):
        if carried is not None:
            at = (first_ref, 0, 0) if first_ref is not None and g == 0 else (raw_ref, 1, g)
            value = value - apply_rows(apply_rows(carried, *at), raw_ref, 0, g)
        carried = act_ref[g] * value
        values.append(carried)
    return values


def wall_kernel(came_ref, scaled_ref, raw_ref, act_ref, y_ref, *refs):
    out_ref, leave_ref = refs[-2:]
    first_ref = refs[0] if len(refs) > 2 else None
    depth = y_ref.shape[0]
    out_ref[...] = y_ref[...]
    leave_ref[...] = y_ref[depth - 1]

    @pl.when(lax.axis_index("wall") == 1)
    def _():
        values = raw_steps([scaled_ref[g] for g in range(depth)], raw_ref, first_ref, act_ref, came_ref[...])
        for g in range(depth):
            out_ref[g] = values[g]
        leave_ref[...] = values[-1]


def chip_local_kernel(came_ref, act_ref, y_ref, *refs, chips):
    own_refs, out_ref = refs[:-1], refs[-1]
    depth = y_ref.shape[0]
    out_ref[...] = y_ref[depth - 1]

    @pl.when(between(chips, 1))
    def _():
        out_ref[...] = act_ref[depth - 1] * apply_pairs(came_ref[...], own_refs) + y_ref[depth - 1]


def three_terms(x):
    high = x.astype(BF16)
    return high, *split2(x - high.astype(F32))


def through_kernel(act_ref, q_ref, s_ref, y_ref, *refs, parts):
    whole_refs, (out_ref, sent_ref, echo_ref) = refs[:parts], refs[parts:]
    depth, lines, _, _, width = q_ref.shape
    main, below = width // LANES * LANES, lines * room_of(width)[0]
    echo = backward_local([y_ref[g] for g in range(depth)], s_ref, act_ref, None)[0]
    echo_ref[...] = echo
    for i, term in enumerate(three_terms(echo)):
        sent_ref[below + 2 * TILE * i : below + 2 * TILE * i + lines, :main] = term[:, :main]
        if width > main:
            sent_ref[below + 2 * TILE * i : below + 2 * TILE * i + lines, main:width] = term[:, main:]

    @pl.when(chip_of() > 0)
    def _():
        for l in range(lines):
            active = [act_ref[g, l : l + 1, :] for g in range(depth)]
            steps = [[-x for x in pair_at(q_ref, width, 0, l)]]
            for g in range(1, depth - 1):
                steps.append(split2(-product(steps[-1], pair_at(q_ref, width, g, l))))
            each = lines // parts
            value = [
                (active[depth - 1] * x.astype(F32)).astype(BF16)
                for x in pair_at(whole_refs[l // each], width, l % each)
            ]
            for g in range(depth - 2, -1, -1):
                reach = steps[g][0].astype(F32) + steps[g][1].astype(F32)
                total = active[g] * (reach - product(value, pair_at(s_ref, width, g, l)))
                value = split2(total)
            pair = value
            store_pair(out_ref, pair, l)
            store_pair(sent_ref, pair, l)


def hop_kernel(came_ref, act_ref, local_ref, idle_ref, *refs, chip):
    pair_refs, out_ref = refs[:-1], refs[-1]
    out_ref[...] = idle_ref[...]

    @pl.when(jnp.logical_and(chip_of() == chip, core_of() == 1))
    def _():
        gone = apply_pairs(came_ref[...], pair_refs)
        out_ref[...] = act_ref[act_ref.shape[0] - 1] * gone + local_ref[...]


def early_hop_kernel(came_ref, act_ref, mate_ref, y_ref, *refs, chip, parts):
    got_refs, own_refs, out_ref = refs[:parts], refs[parts : 2 * parts], refs[-1]
    depth = y_ref.shape[0]
    out_ref[...] = came_ref[...]

    @pl.when(jnp.logical_and(chip_of() == chip, core_of() == 1))
    def _():
        middle = apply_pairs(came_ref[...], got_refs) + mate_ref[...]
        out_ref[...] = act_ref[depth - 1] * apply_pairs(middle, own_refs) + y_ref[depth - 1]


def chosen_arrival(refs, chips, like):
    here = chip_of()
    value = jnp.zeros(like, F32)
    for ref, chip in zip(refs, chips):
        value = jnp.where(here == chip, ref[...], value)
    return value


def choose_kernel(*refs, chips):
    refs[-1][...] = chosen_arrival(refs[:-1], chips, refs[-1].shape)


def turn_kernel(enter_ref, came_ref, echo_ref, got_c, got_d, own_d, *refs, parts, chips, fill):
    got_refs, (enter_y, mid_ref, out_ref) = refs[:parts], refs[-3:]
    inside = jnp.logical_and(chip_of() >= chips[0], chip_of() < chips[1])
    if not fill:
        for held, ref in zip(refs[parts:], refs[-3:]):
            ref[...] = held[...]
    if fill:

        @pl.when(jnp.logical_not(inside))
        def _():
            enter_y[...] = enter_ref[...]
            mid_ref[...] = echo_ref[...]
            out_ref[...] = echo_ref[...]

    @pl.when(jnp.logical_and(inside, core_of() == 1))
    def _():
        enter = enter_ref[...]
        leave = apply_pairs(enter, got_refs) + came_ref[...]
        middle = apply_pairs(leave, own_d) + echo_ref[...]
        lines, width = enter.shape
        below = lines * room_of(width)[0]
        first = apply_pairs(enter, got_d)
        for i in range(3):
            first = first + got_d[below + 2 * TILE * i : below + 2 * TILE * i + lines, :width].astype(F32)
        enter_y[...] = leave
        mid_ref[...] = middle
        out_ref[...] = apply_pairs(middle, got_c) + first


def send_kernel(x_ref, enter_ref, out_ref, *, last):
    out_ref[...] = jnp.where(chip_of() == last, x_ref[...], enter_ref[...])


def steps_kernel(flow_ref, scaled_ref, q_ref, act_ref, held_ref, y_ref, *, late):
    depth = scaled_ref.shape[0]
    here, core = chip_of(), core_of()
    y_ref[...] = held_ref[...]
    if late:
        inside = jnp.logical_and(core == 0, here > 1)
    else:
        inside = jnp.logical_and(here > 0, jnp.logical_or(core == 1, here == 1))

    @pl.when(inside)
    def _():
        values = forward_local([scaled_ref[g] for g in range(depth)], q_ref, act_ref, flow_ref[...])
        for g in range(depth):
            y_ref[g] = values[g]


def entry_kernel(own_ref, came_ref, out_ref):
    out_ref[...] = jnp.where(core_of() == 1, own_ref[...], came_ref[...])


def leave_kernel(own_ref, first_ref, *refs, chips):
    came_ref, out_ref = refs[-2:]
    came_ref[...] = chosen_arrival(refs[:-2], chips, came_ref.shape)
    out_ref[...] = first_ref[...]

    @pl.when(jnp.logical_and(core_of() == 1, chip_of() > 0))
    def _():
        out_ref[...] = apply_pairs(came_ref[...], own_ref) + first_ref[...]


def wall_middle_kernel(came_ref, got_c, got_d, out_ref):
    @pl.when(lax.axis_index("wall") == 0)
    def _():
        lines, width = came_ref.shape
        below = lines * room_of(width)[0]
        value = apply_pairs(came_ref[...], got_c)
        for i in range(3):
            value = value + got_d[below + 2 * TILE * i : below + 2 * TILE * i + lines, :width].astype(F32)
        out_ref[...] = value


def last_kernel(beyond_ref, met_ref, middle_ref, wall_ref, whole_ref, echo_ref, s_ref, act_ref, y_ref, out_ref):
    depth = y_ref.shape[0]
    core, chip = core_of(), chip_of()
    first = jnp.where(chip == 0, middle_ref[...], met_ref[...])
    second = jnp.where(chip == 0, wall_ref[...], beyond_ref[...])
    carried = jnp.where(core == 0, first, second)

    @pl.when(chip == 0)
    def _():
        out_ref[0] = apply_pairs(carried, whole_ref) + echo_ref[...]
        value = carried
        for g in range(depth - 1, 0, -1):
            value = act_ref[g] * (y_ref[g] - apply_pairs(value, s_ref, g))
            out_ref[g] = value

    @pl.when(chip > 0)
    def _():
        solved = backward_local([y_ref[g] for g in range(depth)], s_ref, act_ref, carried)
        for g in range(depth):
            out_ref[g] = solved[g]


def padded_bytes(shape, dtype):
    size = jnp.dtype(dtype).itemsize
    shape = (1,) * (2 - len(shape)) + tuple(shape)
    total = -(-shape[-2] // 16) * 16 * -(-shape[-1] // 128) * 128 * size
    for extent in shape[:-2]:
        total *= extent
    return total


def run(kernel, operands, outs, blocks=1, scratch=()):
    held = [(x.shape, x.dtype) for x, _ in operands] + [(s, t) for s, t, _ in outs]
    limit = sum(padded_bytes(s, t) for s, t in held)
    if blocks == 1:
        in_specs = [at if isinstance(at, pl.BlockSpec) else VMEM for _, at in operands]
        out_specs = [VMEM for _ in outs]
        grid = ()
    else:

        def spec(shape, at):
            if isinstance(at, pl.BlockSpec):
                return at
            if at is None:
                return pl.BlockSpec(shape, lambda i: (0,) * len(shape))
            size = tuple(n // blocks if axis == at else n for axis, n in enumerate(shape))
            return pl.BlockSpec(size, lambda i: tuple(i if axis == at else 0 for axis in range(len(shape))))

        in_specs = [spec(x.shape, at) for x, at in operands]
        out_specs = [spec(s, at) for s, _, at in outs]
        grid = (blocks,)
        limit = 2 * limit // blocks
    limit += sum(padded_bytes(s.shape, s.dtype) for s in scratch if s.memory_space == pltpu.VMEM)
    limit = min(limit + (2 << 20), 60 << 20)
    return pl.pallas_call(
        kernel,
        grid=grid,
        in_specs=in_specs,
        out_specs=out_specs,
        out_shape=[jax.ShapeDtypeStruct(s, t) for s, t, _ in outs],
        scratch_shapes=list(scratch),
        compiler_params=pltpu.CompilerParams(vmem_limit_bytes=limit),
        cost_estimate=pl.CostEstimate(flops=1, bytes_accessed=1, transcendentals=0),
    )(*[x for x, _ in operands])


def hop_pairs(count, start, end, core=1, relay=None):
    start, end = 2 * start + 1, 2 * end + core
    target = {i: i ^ 1 for i in range(count)}
    cycle = [start, end, end ^ 1, start ^ 1]
    if relay is not None:
        cycle[3:3] = [2 * relay, 2 * relay + 1]
    target.update(zip(cycle, cycle[1:] + cycle[:1]))
    return sorted(target.items())


def in_hbm(value):
    return pltpu.with_memory_space_constraint(value, pltpu.HBM)


def after(value, *others):
    return lax.optimization_barrier((value, *others))[0]


def per_device(state, source, face_coef, neighbour, lift, elem_slot, line_len, dinv, lower, upper):
    wall_count = lax.axis_size("wall")
    surf_count = lax.axis_size("surf")
    last = wall_count // 2 - 1
    depth, lines, width, _ = dinv.shape
    slots = state.shape[0]
    block = TILE if lines % TILE == 0 else lines
    blocks = lines // block
    parts = 1
    room, columns, _ = room_of(width)
    line_vector = ((lines, width), F32, 0)
    element_vectors = ((depth, lines, width), F32, 1)
    line_sent = ((lines * room, columns), BF16, 0)
    vector_sent = ((lines * room + 6 * TILE * blocks, columns), BF16, 0)
    line_pairs = ((lines, 2, width, width), BF16, 0)
    part_sent = ((lines // parts * room, columns), BF16, 0)
    part_pairs = ((lines // parts, 2, width, width), BF16, 0)
    element_pairs = ((depth, lines, 2, width, width), BF16, 1)

    def mates(value):
        return lax.ppermute(value, "wall", [(i, i ^ 1) for i in range(wall_count)])

    def relaid(arrays, *others):
        if lines != TILE:
            return jnp.stack(arrays)
        shape = (len(arrays), depth, lines, width, width)
        return run(
            functools.partial(relayout_kernel, kinds=len(arrays)),
            [(in_hbm(jnp.transpose(x, (0, 2, 1, 3))), ANY) for x in arrays] + [(x, None) for x in others],
            [(shape, BF16, None)],
            scratch=[
                pltpu.VMEM((len(arrays), depth, width, lines, width), BF16),
                pltpu.SemaphoreType.DMA((len(arrays), depth)),
            ],
        )[0]

    count = depth * lines
    small = (elem_slot, line_len, face_coef.T, neighbour.T, source)
    in_place = lines == TILE
    blocks_in = [in_hbm(jnp.transpose(x, (0, 2, 1, 3))) for x in (dinv, lower, upper)] if in_place else []
    weight, line_source, act, near_state, near_lift, *landed = run(
        functools.partial(prepare_kernel, taken=2 if in_place else 0),
        [(in_hbm(x), ANY) for x in (*small, state, lift)] + [(x, ANY) for x in blocks_in[:2]],
        [
            ((3 * count, 3 * slots), BF16, None),
            ((count, width), F32, None),
            element_vectors,
            (state.shape, BF16, None),
            (lift.shape, BF16, None),
        ]
        + ([((2, depth, lines, width, width), BF16, None)] if in_place else []),
        scratch=[(pltpu.SMEM if i < 2 else pltpu.VMEM)(x.shape, x.dtype) for i, x in enumerate(small)]
        + [pltpu.SemaphoreType.DMA((len(small) + 2,))]
        + (
            [pltpu.VMEM((2, depth, width, lines, width), BF16), pltpu.SemaphoreType.DMA((2, depth))]
            if in_place
            else []
        ),
    )
    before = lax.ppermute(state, "surf", [(i, (i + 1) % surf_count) for i in range(surf_count)])
    beyond = lax.ppermute(state, "surf", [((i + 1) % surf_count, i) for i in range(surf_count)])
    (before,) = run(copy_kernel, [(before, None), (weight, None)], [(state.shape, BF16, None)])
    cells = [(x, None) for x in (before, near_state, beyond, weight, line_source, near_lift)]
    raw = landed[0] if in_place else jnp.stack([dinv, lower, upper])
    vectors = [element_vectors, element_vectors, line_vector]
    if in_place:
        scaled, y_local, y_leave, first_lower = run(
            functools.partial(local_kernel, merged=True),
            cells + [(raw, None), (act, None), (blocks_in[1], ANY)],
            vectors + [((1, 1, width, lines, width), BF16, None)],
            scratch=[pltpu.SemaphoreType.DMA(())],
        )
    else:
        (rhs,) = run(residual_kernel, cells, [element_vectors])
        scaled, y_local, y_leave = run(
            functools.partial(local_kernel, merged=False), [(rhs, 1), (raw, 2), (act, 1)], vectors, blocks
        )
    came_y = mates(y_leave)
    q, *rest = run(
        functools.partial(
            pair_kernel, first_chip=1, fetch=in_place, turn=False, kind=1, lines=(0, block), ascending=True
        ),
        [(after(raw, y_leave), 2)]
        + ([(blocks_in[2], ANY), (first_lower, None)] if in_place else []),
        [element_pairs, line_pairs, line_sent]
        + (
            [((1, depth, width, lines, width), BF16, None), ((1, 1, lines, width, width), BF16, None)]
            if in_place
            else []
        ),
        blocks,
        [pltpu.SemaphoreType.DMA((depth,))] if in_place else [],
    )
    wall_y, wall_leave = run(
        wall_kernel,
        [(came_y, 0), (scaled, 1), (raw, 2), (act, 1), (y_local, 1)] + [(x, 2) for x in rest[3:]],
        [element_vectors, line_vector],
        blocks,
    )
    arrivals = [lax.ppermute(wall_leave, "wall", hop_pairs(wall_count, 0, 1))]
    a, got_a = [rest[0]], [mates(after(rest[1], came_y))]
    s, c, sent_c = run(
        functools.partial(
            pair_kernel, first_chip=0, fetch=False, turn=in_place, kind=2, lines=(0, block), ascending=False
        ),
        [(after(raw, a[-1], wall_leave), 2)] + ([(rest[2], None)] if in_place else []),
        [element_pairs, line_pairs, line_sent],
        blocks,
        [pltpu.VMEM((1, depth, lines, width, width), BF16)] if in_place else [],
    )
    got_c = mates(after(sent_c, arrivals[0],got_a[-1]))

    def hop(came, pairs, local, idle, at):
        (out,) = run(
            functools.partial(hop_kernel, chip=at),
            [(came, 0), (act, 1), (local, 0), (idle, 0)] + [(x, 0) for x in pairs],
            [line_vector],
            blocks,
        )
        return out

    out = wall_leave
    for at in range(1, last):
        if at == 1:
            (out,) = run(
                functools.partial(early_hop_kernel, chip=at, parts=parts),
                [(arrivals[-1], 0), (act, 1), (came_y, 0), (y_local, 1)] + [(x, 0) for x in got_a + a],
                [line_vector],
                blocks,
            )
            (chip_a,) = run(
                functools.partial(chip_kernel, parts=parts, width=width, own_first=False, chips=(2, last)),
                [(after(x, out) if i == 0 else x, 0) for i, x in enumerate(got_a + a)],
                [line_pairs],
                blocks,
            )
            (y_chip,) = run(
                functools.partial(chip_local_kernel, chips=(2, last)),
                [(after(came_y, out), 0), (act, 1), (y_local, 1)] + [(x, 0) for x in a],
                [line_vector],
                blocks,
            )
            through, sent_d, echo = run(
                functools.partial(through_kernel, parts=parts),
                [(act, 1), (after(q, out, chip_a, y_chip), 1), (s, 1), (wall_y, 1)] + [(x, 0) for x in a],
                [line_pairs, vector_sent, line_vector],
                blocks,
            )
        else:
            out = hop(arrivals[-1], [chip_a], y_chip, y_chip, at)
        pairs = hop_pairs(wall_count, at, at + 1, relay=0 if at == 1 else None)
        arrivals.append(lax.ppermute(out, "wall", pairs))
        if at == 1:
            got_d = mates(after(sent_d, got_c, arrivals[-1]))

    def chosen(arrived, chips):
        return run(
            functools.partial(choose_kernel, chips=chips), [(x, 0) for x in arrived], [line_vector], blocks
        )[0]

    def turn(first_chip, end_chip, entered, held=()):
        return run(
            functools.partial(turn_kernel, parts=parts, chips=(first_chip, end_chip), fill=not held),
            [(x, 0) for x in (entered, came_y, echo, got_c, got_d, through, *got_a)]
            + [(x, 0) for x in held],
            [line_vector] * 3,
            blocks,
        )

    def steps(late, flow, held):
        return run(
            functools.partial(steps_kernel, late=late),
            [(flow, 0)] + [(x, 1) for x in (scaled, q, act, held)],
            [element_vectors],
            blocks,
        )

    (chip_c,) = run(
        functools.partial(chip_kernel, parts=1, width=width, own_first=True, chips=(1, last)),
        [(after(got_c, out), 0), (c, 0)],
        [line_pairs],
        blocks,
    )
    arrivals[-1] = after(arrivals[-1], chip_c)
    held = turn(last, last + 1, arrivals[-1])
    entered = chosen(arrivals, list(range(1, last + 1)))
    x_chip = held[-1]
    (out,) = run(functools.partial(send_kernel, last=last), [(x_chip, 0), (entered, 0)], [line_vector], blocks)
    arrived = [lax.ppermute(out, "wall", hop_pairs(wall_count, last, last - 1))]
    held = turn(last - 1, last, after(entered, out), held)
    x_chip = held[-1]
    enter_y, middle, _ = held
    y = wall_y
    for at in range(last - 1, 0, -1):
        came = arrived[-1]
        if at == last - 2:
            enter_y, middle, x_chip = turn(1, last - 1, after(entered, out), held)
        if at == 1:
            (flow,) = run(entry_kernel, [(enter_y, 0), (after(arrived[0], out), 0)], [line_vector], blocks)
            (y,) = steps(False, flow, wall_y)
            came = after(came, y)
        out = hop(came, [chip_c], x_chip, entered, at)
        arrived.append(lax.ppermute(out, "wall", hop_pairs(wall_count, at, at - 1, int(at > 1))))
    wall = lax.ppermute(out, "wall", hop_pairs(wall_count, 1, 0))
    beyond, left = run(
        functools.partial(leave_kernel, chips=list(range(last - 1, 0, -1))),
        [(x, 0) for x in (c, middle, *arrived[:-1])],
        [line_vector, line_vector],
        blocks,
    )
    met_left = mates(after(left, out))
    (y,) = steps(True, arrived[-1], y)
    (wall_middle,) = run(
        wall_middle_kernel, [(after(arrived[-1], wall, y), 0), (got_c, 0), (got_d, 0)], [line_vector], blocks
    )
    (solution,) = run(
        last_kernel,
        [(x, 0) for x in (beyond, met_left, wall_middle, wall, c, echo)] + [(x, 1) for x in (s, act, y)],
        [element_vectors],
        blocks,
    )
    return solution


def solution(mesh):
    in_specs = (
        P(("wall", "surf"), None),
        P(("wall", "surf"), None),
        P(("wall", "surf"), None),
        P(("wall", "surf"), None),
        P(),
        P("wall", "surf"),
        P("surf"),
        P("wall", "surf", None, None),
        P("wall", "surf", None, None),
        P("wall", "surf", None, None),
    )
    out_specs = P("wall", "surf", None)
    return jax.shard_map(
        per_device, mesh=mesh, in_specs=in_specs, out_specs=out_specs, check_vma=False
    )
```
